32 devices in a mesh: dp: 16 (over z, y, x), ffn: 2 (over core).
Axes of the slice: x: 2, y: 2, z: 4, core: 2. Of those that a mesh axis runs over, the one named last changes fastest.
Arguments:
- item_table: float32 [25088, 256], P(('dp', 'ffn')), may hold values from -0.75 to 0.75
- attn_in: float32 [3, 256, 512], P(None, None, 'ffn'), may hold values from -0.375 to 0.375
- attn_out: float32 [512, 256], P('ffn'), may hold values from -0.75 to 0.75
- ffn_up: float32 [256, 1024], P(None, 'ffn'), may hold values from -0.375 to 0.375
- ffn_down: float32 [1024, 256], P('ffn'), may hold values from -0.1875 to 0.1875
- position_table: float32 [512, 256], replicated, may hold values from -3 to 3
- norm_gains: float32 [3, 256], replicated, may hold values from 0.5 to 1.5
- item_first: float32 [25088, 256], P(('dp', 'ffn')), may hold values from -0.00015957387 to 0.00015957387
- item_second: float32 [25088, 256], P(('dp', 'ffn')), may hold values from 1.31528e-10 to 5.26112e-10
- attn_in_first: float32 [3, 256, 512], P(None, None, 'ffn'), may hold values from -0.00015957387 to 0.00015957387
- attn_in_second: float32 [3, 256, 512], P(None, None, 'ffn'), may hold values from 1.31528e-10 to 5.26112e-10
- attn_out_first: float32 [512, 256], P('ffn'), may hold values from -0.00015957387 to 0.00015957387
- attn_out_second: float32 [512, 256], P('ffn'), may hold values from 1.31528e-10 to 5.26112e-10
- ffn_up_first: float32 [256, 1024], P(None, 'ffn'), may hold values from -0.00015957387 to 0.00015957387
- ffn_up_second: float32 [256, 1024], P(None, 'ffn'), may hold values from 1.31528e-10 to 5.26112e-10
- ffn_down_first: float32 [1024, 256], P('ffn'), may hold values from -0.00015957387 to 0.00015957387
- ffn_down_second: float32 [1024, 256], P('ffn'), may hold values from 1.31528e-10 to 5.26112e-10
- position_first: float32 [512, 256], replicated, may hold values from -0.00015957387 to 0.00015957387
- position_second: float32 [512, 256], replicated, may hold values from 1.31528e-10 to 5.26112e-10
- gains_first: float32 [3, 256], replicated, may hold values from -0.00079786935 to 0.00079786935
- gains_second: float32 [3, 256], replicated, may hold values from 3.2882e-09 to 1.31528e-08
- owner_group: int32 [16, 2048, 1], P('dp'), may hold values from 0 to 15; in each aligned block of 2048 rows (0 to 2047, 2048 to 4095, ..., all dimensions but the last counted through in order) at most 256 rows name the same one
- row_offset: int32 [16, 2048], P('dp'), may hold values from 0 to 1567
- segment_ids: int32 [16, 1024], P('dp'), may hold values from 0 to 17, never falling along the last dimension, each value on 1 to 512 neighbouring positions
- live_slots: int32 [16], P('dp'), may hold values from 1 to 1024, as said below
- log_freq: float32 [16, 1024], P('dp'), may hold values from -2 to 0
Outputs:
- item_new: float32 [25088, 256], P(('dp', 'ffn'))
- item_first_new: float32 [25088, 256], P(('dp', 'ffn'))
- item_second_new: float32 [25088, 256], P(('dp', 'ffn'))
- attn_in_new: float32 [3, 256, 512], P(None, None, 'ffn')
- attn_in_first_new: float32 [3, 256, 512], P(None, None, 'ffn')
- attn_in_second_new: float32 [3, 256, 512], P(None, None, 'ffn')
- attn_out_new: float32 [512, 256], P('ffn')
- attn_out_first_new: float32 [512, 256], P('ffn')
- attn_out_second_new: float32 [512, 256], P('ffn')
- ffn_up_new: float32 [256, 1024], P(None, 'ffn')
- ffn_up_first_new: float32 [256, 1024], P(None, 'ffn')
- ffn_up_second_new: float32 [256, 1024], P(None, 'ffn')
- ffn_down_new: float32 [1024, 256], P('ffn')
- ffn_down_first_new: float32 [1024, 256], P('ffn')
- ffn_down_second_new: float32 [1024, 256], P('ffn')
- position_new: float32 [512, 256], replicated
- position_first_new: float32 [512, 256], replicated
- position_second_new: float32 [512, 256], replicated
- gains_new: float32 [3, 256], replicated
- gains_first_new: float32 [3, 256], replicated
- gains_second_new: float32 [3, 256], replicated
- loss_sum: float32 [], replicated
- live_count: float32 [], replicated
- grad_norm: float32 [], replicated
The draws below stay inside these ranges and needn't reach their ends.
Inputs may be any that keep to these rules, and one draw needn't show every extreme that they name: `owner_group`: among the 2048 entries of one device, no group is named more than 256 times. `live_slots`: slots at or past a row's live count are padding. `segment_ids`: A segment is a run of at most 512 slots.
All inputs are finite; a program needn't handle non-finite values.
Results may differ from the reference program's by a relative error of at most 0.012.
The reference program's roundings to bfloat16 on the way count: a program that leaves them out, or rounds other values in their place, can miss the bound.
Values may be sent and summed in bfloat16 or wider, within the bound.
A program may use at most 192 MiB of HBM per device.

```python
import math
import jax
import jax.numpy as jnp
import numpy as np
from jax import lax

D = 256
HEADS = 8
HEAD = 64
FF = 1024
MAXLEN = 512
SLOTS = 1024
QBLOCK = 512
TAB_DEV = 784
STEP = 10
ROW_DEV = 1
ROWS = 16
ITEMS = 25088
CAP = 256
PARAMS = 7602944
N_DP = 16


def draw_live_slots(key, part):
    key = jax.random.fold_in(key, 7)
    jitter = jax.random.randint(key, (ROWS,), 0, SLOTS // 8 + 1)
    order = jnp.arange(ROWS, dtype=jnp.int32)
    reach = (ROWS - 1 - order) * (2 * SLOTS // 3) // max(ROWS - 1, 1)
    return (SLOTS - reach - jitter * (order < ROWS - 1).astype(jnp.int32)).astype(jnp.int32)


def set_ends(array, own_key, low, largest):
    spot = [jax.random.randint(jax.random.fold_in(own_key, axis), (), 0, length) for axis, length in enumerate(array.shape)]
    widest = array.shape.index(max(array.shape))
    next_to = spot[:widest] + [(spot[widest] + 1) % array.shape[widest]] + spot[widest + 1:]
    return array.at[tuple(spot)].set(low).at[tuple(next_to)].set(largest)


def level_of(rng, dims, shards, low, high):
    loudness, own = 1.0, jax.random.fold_in(rng, 6)
    for axis_at, parts in shards:
        heights = jnp.exp(jax.random.uniform(jax.random.fold_in(own, axis_at), (parts,), jnp.float32, low / len(shards), high / len(shards)))
        loudness = loudness * jnp.repeat(heights, dims[axis_at] // parts).reshape([-1 if axis == axis_at else 1 for axis in range(len(dims))])
    return loudness


def split_up(count, total, most, lean):
    portions = [(1 << 20) // math.isqrt(grade ** lean) + 1 for grade in range(2, count + 1)]
    rest, counts = total - most - (count - 1), [1] * (count - 1)
    while rest > 0:
        movable = [i for i in range(count - 1) if counts[i] < most]
        whole, budget = sum([portions[i] for i in movable]), rest
        for i in movable:
            more = min(most - counts[i], max(1, budget * portions[i] // whole), rest)
            counts[i] = counts[i] + more
            rest = rest - more
    return np.array([most] + counts)


def ragged_sizes(rng, number_of, total, bound, lean):
    if number_of == 2:
        one = jax.random.randint(rng, (), max(1, total - bound), min(bound, total - 1) + 1)
        return jnp.stack([one, total - one])
    sizes = jnp.asarray(split_up(number_of, total, bound, lean), jnp.int32)
    pairs = (number_of - 1) // 2
    giver, sink = sizes[1:1 + 2 * pairs:2], sizes[2:2 + 2 * pairs:2]
    room = jnp.minimum(giver - 1, bound - sink)
    moved = jax.random.randint(jax.random.fold_in(rng, 1), (pairs,), 0, 1 << 20) % (room + 1)
    sizes = sizes.at[1:1 + 2 * pairs:2].set(giver - moved).at[2:2 + 2 * pairs:2].set(sink + moved)
    return sizes[jax.random.permutation(jax.random.fold_in(rng, 2), number_of)]


def shared_out(own_key, own, number, rows, number_of, top, most, lean):
    order = jax.random.permutation(own_key, number_of)
    heavy_load, ordinary = portions_of(number_of, rows * top, most, lean, True), portions_of(number_of, rows * top, most, lean, False)
    places = jnp.arange(number_of)

    def named(tallies, rotation):
        used = int((tallies > 0).sum())
        fixed = max(1, used // 4)
        moved = fixed + (places - fixed + rotation * (used - fixed)) % max(1, number_of - fixed)
        return jnp.zeros((number_of,), jnp.int32).at[order[jnp.where(places < fixed, places, moved)]].set(jnp.asarray(tallies, jnp.int32))

    tallies = jnp.where(number % 4 == 0, named(heavy_load, number // 4), named(ordinary, number - number // 4 - 1))
    mixed = jax.random.permutation(jax.random.fold_in(own, 3), number_of)
    giver, sink = mixed[0:number_of // 2 * 2:2], mixed[1:number_of // 2 * 2:2]
    slack = jnp.minimum(tallies[giver] - 1, most - tallies[sink]) // 2
    slack = jnp.where((giver == order[0]) | (sink == order[0]) | (tallies[sink] == 0), 0, jnp.maximum(slack, 0))
    moved = jax.random.randint(jax.random.fold_in(own, 4), (number_of // 2,), 0, 1 << 20) % (slack + 1)
    tallies = tallies.at[giver].add(-moved).at[sink].add(moved)
    labels = jnp.searchsorted(jnp.cumsum(tallies), jnp.arange(rows * top), side="right").astype(jnp.int32)
    table = labels.reshape(top, rows).T
    table = table[jax.random.permutation(jax.random.fold_in(own, 1), rows)]
    rotation = jax.random.randint(jax.random.fold_in(own, 2), (rows, 1), 0, top)
    return jnp.take_along_axis(table, (jnp.arange(top)[None, :] + rotation) % top, axis=1)


def portions_of(amount, total, most, slope, full):
    weights = [(1 << 20) // math.isqrt(rank ** slope) + 1 for rank in range(1, amount + 1)]
    largest = most if full else min(most, max(-(-total // amount), total * weights[0] // sum(weights)))
    least = 1 if total - largest >= amount - 1 else 0
    counts, rest = [largest] + [least] * (amount - 1), total - largest - least * (amount - 1)
    while rest > 0:
        free = [i for i in range(1, amount) if counts[i] < largest] or [i for i in range(1, amount) if counts[i] < most]
        pool, left = sum([weights[i] for i in free]), rest
        for i in free:
            more = min(most - counts[i], max(1, left * weights[i] // pool), rest)
            counts[i] = counts[i] + more
            rest = rest - more
    return np.array(counts)


def gaussian(stream_key, extent, width, most, cuts=(), kind=jnp.bfloat16):
    array = width * jax.random.normal(stream_key, extent, jnp.float32)
    if cuts:
        array = array * level_of(stream_key, extent, cuts, -0.22, 0.18)
    return jnp.clip(array, -most, most).astype(kind)


def setup_inputs(seed: int = 0) -> dict:
    arg_keys = jax.random.split(jax.random.key(seed), 27)
    item_table = gaussian(arg_keys[0], (ITEMS, D), 0.125, 0.75, ((0, 32),), jnp.float32)
    attn_in = gaussian(arg_keys[1], (3, D, HEADS * HEAD), D ** -0.5, 0.375, ((2, 2),), jnp.float32)
    attn_out = gaussian(arg_keys[2], (HEADS * HEAD, D), (HEADS * HEAD // 8) ** -0.5, 0.75, ((0, 2),), jnp.float32)
    ffn_up = gaussian(arg_keys[3], (D, FF), D ** -0.5, 0.375, ((1, 2),), jnp.float32)
    ffn_down = gaussian(arg_keys[4], (FF, D), FF ** -0.5, 0.1875, ((0, 2),), jnp.float32)
    position_table = gaussian(arg_keys[5], (MAXLEN, D), 0.5, 3.0, (), jnp.float32)
    norm_gains = jnp.clip(1.0 + 0.1 * jax.random.normal(arg_keys[6], (3, D), jnp.float32), 0.5, 1.5)
    item_first = gaussian(arg_keys[7], (ITEMS, D), (0.11 / PARAMS ** 0.5), 0.00015957387, ((0, 32),), jnp.float32)
    item_second = jnp.clip(jnp.exp(math.log(5.261119873090081e-10) - 1.3862944 * jax.random.uniform(arg_keys[8], (ITEMS, D), jnp.float32) ** level_of(arg_keys[8], (ITEMS, D), ((0, 32),), -0.2, 0.2)), 1.3152799682725203e-10, 5.261119873090081e-10)
    attn_in_first = gaussian(arg_keys[9], (3, D, HEADS * HEAD), (0.11 / PARAMS ** 0.5), 0.00015957387, ((2, 2),), jnp.float32)
    attn_in_second = jnp.clip(jnp.exp(math.log(5.261119873090081e-10) - 1.3862944 * jax.random.uniform(arg_keys[10], (3, D, HEADS * HEAD), jnp.float32) ** level_of(arg_keys[10], (3, D, HEADS * HEAD), ((2, 2),), -0.2, 0.2)), 1.3152799682725203e-10, 5.261119873090081e-10)
    attn_out_first = gaussian(arg_keys[11], (HEADS * HEAD, D), (0.11 / PARAMS ** 0.5), 0.00015957387, ((0, 2),), jnp.float32)
    attn_out_second = jnp.clip(jnp.exp(math.log(5.261119873090081e-10) - 1.3862944 * jax.random.uniform(arg_keys[12], (HEADS * HEAD, D), jnp.float32) ** level_of(arg_keys[12], (HEADS * HEAD, D), ((0, 2),), -0.2, 0.2)), 1.3152799682725203e-10, 5.261119873090081e-10)
    ffn_up_first = gaussian(arg_keys[13], (D, FF), (0.11 / PARAMS ** 0.5), 0.00015957387, ((1, 2),), jnp.float32)
    ffn_up_second = jnp.clip(jnp.exp(math.log(5.261119873090081e-10) - 1.3862944 * jax.random.uniform(arg_keys[14], (D, FF), jnp.float32) ** level_of(arg_keys[14], (D, FF), ((1, 2),), -0.2, 0.2)), 1.3152799682725203e-10, 5.261119873090081e-10)
    ffn_down_first = gaussian(arg_keys[15], (FF, D), (0.11 / PARAMS ** 0.5), 0.00015957387, ((0, 2),), jnp.float32)
    ffn_down_second = jnp.clip(jnp.exp(math.log(5.261119873090081e-10) - 1.3862944 * jax.random.uniform(arg_keys[16], (FF, D), jnp.float32) ** level_of(arg_keys[16], (FF, D), ((0, 2),), -0.2, 0.2)), 1.3152799682725203e-10, 5.261119873090081e-10)
    position_first = gaussian(arg_keys[17], (MAXLEN, D), (0.11 / PARAMS ** 0.5), 0.00015957387, (), jnp.float32)
    position_second = jnp.clip(jnp.exp(jax.random.uniform(arg_keys[18], (MAXLEN, D), jnp.float32, math.log(1.3152799682725203e-10), math.log(5.261119873090081e-10))), 1.3152799682725203e-10, 5.261119873090081e-10)
    gains_first = gaussian(arg_keys[19], (3, D), (0.55 / PARAMS ** 0.5), 0.00079786935, (), jnp.float32)
    gains_second = jnp.clip(jnp.exp(jax.random.uniform(arg_keys[20], (3, D), jnp.float32, math.log(3.2881999345590884e-09), math.log(1.3152799738236354e-08))), 3.2881999345590884e-09, 1.3152799738236354e-08)
    owner_group_keys = jax.random.split(jax.random.fold_in(arg_keys[21], 1), ROWS * (2 * SLOTS) // (2 * SLOTS * ROW_DEV))
    owner_group_turns = jax.random.permutation(jax.random.fold_in(arg_keys[21], 3), ROWS * (2 * SLOTS) // (2 * SLOTS * ROW_DEV))
    owner_group = jax.vmap(lambda own, number: shared_out(jax.random.fold_in(arg_keys[21], 2), own, number, 2 * SLOTS * ROW_DEV, N_DP, 1, CAP, 1))(owner_group_keys, owner_group_turns).reshape((ROWS, 2 * SLOTS, 1))
    row_offset = set_ends(jax.random.randint(arg_keys[22], (ROWS, 2 * SLOTS), 0, 2 * TAB_DEV), jax.random.fold_in(arg_keys[22], 1), 0, (2 * TAB_DEV) - 1).astype(jnp.int32)
    segment_ids = jax.vmap(lambda own: jnp.searchsorted(jnp.cumsum(ragged_sizes(own, SLOTS // MAXLEN + SLOTS // 64, SLOTS, MAXLEN, 1)), jnp.arange(SLOTS), side="right"))(jax.random.split(arg_keys[23], ROWS)).reshape((ROWS, SLOTS)).astype(jnp.int32)
    live_slots = draw_live_slots(jax.random.fold_in(arg_keys[26], 71), 0)
    log_freq = jnp.clip(-2.0 + 2.0 * jax.random.uniform(arg_keys[25], (ROWS, SLOTS), jnp.float32) ** level_of(arg_keys[25], (ROWS, SLOTS), ((0, 16),), -0.2, 0.2), -2.0, 0.0)
    return {"item_table": item_table, "attn_in": attn_in, "attn_out": attn_out, "ffn_up": ffn_up, "ffn_down": ffn_down, "position_table": position_table, "norm_gains": norm_gains, "item_first": item_first, "item_second": item_second, "attn_in_first": attn_in_first, "attn_in_second": attn_in_second, "attn_out_first": attn_out_first, "attn_out_second": attn_out_second, "ffn_up_first": ffn_up_first, "ffn_up_second": ffn_up_second, "ffn_down_first": ffn_down_first, "ffn_down_second": ffn_down_second, "position_first": position_first, "position_second": position_second, "gains_first": gains_first, "gains_second": gains_second, "owner_group": owner_group, "row_offset": row_offset, "segment_ids": segment_ids, "live_slots": live_slots, "log_freq": log_freq}


EPSILON = 1e-05
SCALE = 0.125
CLIP = 1.0
RATE = 0.05
RATE_POSITION = 0.3
RATE_GAINS = 0.5
DECAY = 0.01
BETA_ONE = 0.9
BETA_TWO = 0.999
ADAM_EPS = 1e-08
HIGH = lax.Precision.HIGHEST

@jax.custom_vjp
def low(v):
    return lax.optimization_barrier(v.astype(jnp.bfloat16)).astype(jnp.float32)

@jax.custom_vjp
def low_back(v):
    return v

def low_keep(v):
    return (low(v), None)

def low_pass(kept, grad):
    return (grad,)

def back_keep(v):
    return (v, None)

def back_low(kept, grad):
    return (low(grad),)
low.defvjp(low_keep, low_pass)
low_back.defvjp(back_keep, back_low)

def norm_rows(value, gain):
    centred = value - lax.optimization_barrier(jnp.mean(value, -1, keepdims=True))
    spread = lax.optimization_barrier(jnp.mean(centred * centred, -1, keepdims=True))
    return centred * lax.rsqrt(spread + EPSILON) * gain

def layout(segment, live):
    slots = jnp.arange(segment.shape[0], dtype=jnp.int32)
    before = jnp.concatenate([jnp.full((1,), -1, jnp.int32), segment[:-1]])
    starts = lax.cummax(jnp.where(segment != before, slots, 0), axis=0)
    return (slots - starts, slots < live)

def row_loss(dense, rows, segment, live, logq):
    attn_in, attn_out, ffn_up, ffn_down, position_table, norm_gains = dense
    place, alive = layout(segment, live)
    embedded = low(rows[:SLOTS])
    candidates = low(rows[SLOTS:])
    first = embedded + position_table[place]
    normed = low(norm_rows(first, norm_gains[0]))
    triple = low(low_back(jnp.einsum('td,cdf->ctf', normed, low(attn_in), precision=HIGH)))
    query = triple[0].reshape(SLOTS, HEADS, HEAD)
    keys = triple[1].reshape(SLOTS, HEADS, HEAD)
    values = triple[2].reshape(SLOTS, HEADS, HEAD)
    slots = jnp.arange(SLOTS, dtype=jnp.int32)

    def block(start):
        rows_q = start + jnp.arange(QBLOCK, dtype=jnp.int32)
        part = lax.dynamic_slice_in_dim(query, start, QBLOCK, 0)
        seg_q = lax.dynamic_slice_in_dim(segment, start, QBLOCK, 0)
        scores = low_back(jnp.einsum('qhe,khe->hqk', part, keys, precision=HIGH) * SCALE)
        allowed = (slots[None, :] <= rows_q[:, None]) & (segment[None, :] == seg_q[:, None])
        scores = jnp.where(allowed[None], scores, -1e+30)
        top = lax.optimization_barrier(jnp.max(scores, -1, keepdims=True))
        expo = jnp.exp(scores - top)
        prob = low(expo / lax.optimization_barrier(jnp.sum(expo, -1, keepdims=True)))
        return low(low_back(jnp.einsum('hqk,khe->qhe', prob, values, precision=HIGH)))
    starts = jnp.arange(0, SLOTS, QBLOCK, dtype=jnp.int32)
    attended = lax.map(jax.checkpoint(block), starts).reshape(SLOTS, HEADS * HEAD)
    second = first + low_back(jnp.dot(attended, low(attn_out), precision=HIGH))
    lifted = low(norm_rows(second, norm_gains[1]))
    inner = low_back(jnp.dot(lifted, low(ffn_up), precision=HIGH))
    hidden = low(jax.nn.gelu(inner))
    third = second + low_back(jnp.dot(hidden, low(ffn_down), precision=HIGH))
    final = low(norm_rows(third, norm_gains[2]))
    logits = low_back(jnp.dot(final, candidates.T, precision=HIGH)) - logq[None, :]
    logits = jnp.where(alive[None, :], logits, -1e+30)
    top = lax.optimization_barrier(jnp.max(logits, -1, keepdims=True))
    total = top[:, 0] + jnp.log(lax.optimization_barrier(jnp.sum(jnp.exp(logits - top), -1)))
    return jnp.sum(jnp.where(alive, total - jnp.diagonal(logits), 0.0))

def adamw(weight, grad, first, second, decay, rate):
    first = BETA_ONE * first + (1.0 - BETA_ONE) * grad
    second = BETA_TWO * second + (1.0 - BETA_TWO) * grad * grad
    moved = first / (1.0 - BETA_ONE ** STEP) / (jnp.sqrt(second / (1.0 - BETA_TWO ** STEP)) + ADAM_EPS)
    return (weight - rate * (moved + decay * weight), first, second)

def reference(item_table, attn_in, attn_out, ffn_up, ffn_down, position_table, norm_gains, item_first, item_second, attn_in_first, attn_in_second, attn_out_first, attn_out_second, ffn_up_first, ffn_up_second, ffn_down_first, ffn_down_second, position_first, position_second, gains_first, gains_second, owner_group, row_offset, segment_ids, live_slots, log_freq):
    items = owner_group[:, :, 0] * (2 * TAB_DEV) + row_offset
    dense = (attn_in, attn_out, ffn_up, ffn_down, position_table, norm_gains)

    def total_loss(dense, table):
        rows = table[items]

        def step(carry, inputs):
            row, segment, live, logq = inputs
            return (carry + jax.checkpoint(row_loss)(dense, row, segment, live, logq), None)
        loss, _ = lax.scan(step, jnp.zeros((), jnp.float32), (rows, segment_ids, live_slots, log_freq))
        return loss
    loss, pullback = jax.vjp(total_loss, dense, item_table)
    grads_dense, grad_table = pullback(jnp.ones((), jnp.float32))
    grads = (grad_table,) + tuple(grads_dense)
    weights = (item_table,) + dense
    firsts = (item_first, attn_in_first, attn_out_first, ffn_up_first, ffn_down_first, position_first, gains_first)
    seconds = (item_second, attn_in_second, attn_out_second, ffn_up_second, ffn_down_second, position_second, gains_second)
    rates = (RATE, RATE, RATE, RATE, RATE, RATE_POSITION, RATE_GAINS)
    squares = jnp.zeros((), jnp.float32)
    for grad in grads:
        squares = squares + jnp.sum(grad * grad)
    norm = jnp.sqrt(squares)
    factor = CLIP / jnp.maximum(norm, CLIP)
    results = []
    for index_w in range(7):
        decay = 0.0 if index_w == 6 else DECAY
        results.extend(adamw(weights[index_w], grads[index_w] * factor, firsts[index_w], seconds[index_w], decay, rates[index_w]))
    count = jnp.sum(live_slots).astype(jnp.float32)
    return (results[0], results[1], results[2], results[3], results[4], results[5], results[6], results[7], results[8], results[9], results[10], results[11], results[12], results[13], results[14], results[15], results[16], results[17], results[18], results[19], results[20], loss, count, norm)
```

```python
import functools

import jax
import jax.numpy as jnp
from jax import lax
from jax.experimental import pallas as pl
from jax.experimental.pallas import tpu as pltpu
from jax.sharding import PartitionSpec as P

HEAD = 64
QBLOCK = 512
STEP = 10


EPSILON = 1e-05
SCALE = 0.125
CLIP = 1.0
RATE = 0.05
RATE_POSITION = 0.3
RATE_GAINS = 0.5
DECAY = 0.01
BETA_ONE = 0.9
BETA_TWO = 0.999
ADAM_EPS = 1e-08
LOWF = jnp.bfloat16
WIDE = jnp.float32


def norm_rows(value, gain):
    centred = value - jnp.mean(value, -1, keepdims=True)
    spread = jnp.mean(centred * centred, -1, keepdims=True)
    return centred * lax.rsqrt(spread + EPSILON) * gain


def norm_back(value, gain, grad):
    centred = value - jnp.mean(value, -1, keepdims=True)
    inverse = lax.rsqrt(jnp.mean(centred * centred, -1, keepdims=True) + EPSILON)
    unit = centred * inverse
    d_unit = grad * gain
    d_value = inverse * (
        d_unit
        - jnp.mean(d_unit, -1, keepdims=True)
        - unit * jnp.mean(d_unit * unit, -1, keepdims=True)
    )
    return (d_value, jnp.sum(grad * unit, 0))


def block_mask(segment, start, width):
    rows_q = start + jnp.arange(width, dtype=jnp.int32)
    cols = jnp.arange(segment.shape[0], dtype=jnp.int32)
    return (cols[None, :] <= rows_q[:, None]) & (
        segment[None, :] == segment[start : start + width][:, None]
    )


def split_heads(triple):
    heads = triple.shape[2] // HEAD
    return [triple[c].reshape(triple.shape[1], heads, HEAD) for c in range(3)]


def attend(triple, segment):
    query, keys, values = split_heads(triple)
    width = min(QBLOCK, query.shape[0])
    outputs, sums = ([], [])
    for start in range(0, query.shape[0], width):
        scores = (
            jnp.einsum(
                "qhe,khe->hqk", query[start : start + width], keys, preferred_element_type=WIDE
            )
            * SCALE
        )
        scores = jnp.where(block_mask(segment, start, width)[None], scores, -1e30)
        top = jnp.max(scores, -1, keepdims=True)
        expo = jnp.exp(scores - top)
        total = jnp.sum(expo, -1, keepdims=True)
        prob = (expo / total).astype(LOWF)
        outputs.append(
            jnp.einsum("hqk,khe->qhe", prob, values, preferred_element_type=WIDE).astype(LOWF)
        )
        sums.append(top + jnp.log(total))
    joined = jnp.concatenate(outputs, 0)
    return (joined.reshape(joined.shape[0], -1), jnp.concatenate(sums, 1))


def attend_back(triple, segment, sums, d_attended):
    query, keys, values = split_heads(triple)
    d_heads = d_attended.reshape(query.shape)
    width = min(QBLOCK, query.shape[0])
    d_query = []
    d_keys = jnp.zeros(keys.shape, WIDE)
    d_values = jnp.zeros(values.shape, WIDE)
    for start in range(0, query.shape[0], width):
        part = query[start : start + width]
        d_part = d_heads[start : start + width]
        scores = jnp.einsum("qhe,khe->hqk", part, keys, preferred_element_type=WIDE) * SCALE
        scores = jnp.where(block_mask(segment, start, width)[None], scores, -1e30)
        prob = jnp.exp(scores - sums[:, start : start + width])
        d_prob = jnp.einsum("qhe,khe->hqk", d_part, values, preferred_element_type=WIDE)
        d_scores = (prob * (d_prob - jnp.sum(prob * d_prob, -1, keepdims=True))).astype(LOWF)
        d_query.append(
            jnp.einsum("hqk,khe->qhe", d_scores, keys, preferred_element_type=WIDE) * SCALE
        )
        d_keys = (
            d_keys + jnp.einsum("hqk,qhe->khe", d_scores, part, preferred_element_type=WIDE) * SCALE
        )
        d_values = d_values + jnp.einsum(
            "hqk,qhe->khe", prob.astype(LOWF), d_part, preferred_element_type=WIDE
        )
    stacked = jnp.stack([jnp.concatenate(d_query, 0), d_keys, d_values])
    return stacked.reshape(3, query.shape[0], -1).astype(LOWF)


def layer_forward(rows, segment, live, logq, weights):
    attn_in, attn_out, ffn_up, ffn_down, position_table, norm_gains = weights
    slots = segment.shape[0]
    order = jnp.arange(slots, dtype=jnp.int32)
    before = jnp.concatenate([jnp.full((1,), -1, jnp.int32), segment[:-1]])
    place = order - lax.cummax(jnp.where(segment != before, order, 0), axis=0)
    alive = order < live
    first = rows[:slots].astype(WIDE) + jnp.take(position_table, place, axis=0)
    normed = norm_rows(first, norm_gains[0]).astype(LOWF)
    triple = jnp.einsum("td,cdf->ctf", normed, attn_in, preferred_element_type=WIDE).astype(LOWF)
    attended, sums = attend(triple, segment)
    second = first + lax.psum(jnp.dot(attended, attn_out, preferred_element_type=WIDE), "ffn")
    lifted = norm_rows(second, norm_gains[1]).astype(LOWF)
    inner = jnp.dot(lifted, ffn_up, preferred_element_type=WIDE)
    hidden = jax.nn.gelu(inner).astype(LOWF)
    third = second + lax.psum(jnp.dot(hidden, ffn_down, preferred_element_type=WIDE), "ffn")
    final = norm_rows(third, norm_gains[2]).astype(LOWF)
    logits = (
        jnp.einsum("id,jd->ij", final, rows[slots:], preferred_element_type=WIDE) - logq[None, :]
    )
    logits = jnp.where(alive[None, :], logits, -1e30)
    top = jnp.max(logits, -1, keepdims=True)
    expo = jnp.exp(logits - top)
    total = jnp.sum(expo, -1, keepdims=True)
    loss = jnp.sum(jnp.where(alive, top[:, 0] + jnp.log(total[:, 0]) - jnp.diagonal(logits), 0.0))
    identity = (order[:, None] == order[None, :]).astype(WIDE)
    grad_logits = ((expo / total - identity) * alive[:, None].astype(WIDE)).astype(LOWF)
    saved = (
        place,
        first,
        normed,
        triple,
        attended,
        sums,
        second,
        lifted,
        inner,
        hidden,
        third,
        final,
        grad_logits,
    )
    return (loss, saved)


def layer_backward(saved, candidates, segment, weights):
    attn_in, attn_out, ffn_up, ffn_down, position_table, norm_gains = weights
    (
        place,
        first,
        normed,
        triple,
        attended,
        sums,
        second,
        lifted,
        inner,
        hidden,
        third,
        final,
        grad_logits,
    ) = saved
    d_final = jnp.dot(grad_logits, candidates, preferred_element_type=WIDE)
    d_cand = jnp.einsum("ij,id->jd", grad_logits, final, preferred_element_type=WIDE)
    d_third, gain_three = norm_back(third, norm_gains[2], d_final)
    d_branch = d_third.astype(LOWF)
    grad_down = jnp.einsum("tf,td->fd", hidden, d_branch, preferred_element_type=WIDE)
    d_hidden = jnp.einsum("td,fd->tf", d_branch, ffn_down, preferred_element_type=WIDE)
    _, gelu_back = jax.vjp(jax.nn.gelu, inner)
    d_inner = gelu_back(d_hidden)[0].astype(LOWF)
    grad_up = jnp.einsum("td,tf->df", lifted, d_inner, preferred_element_type=WIDE)
    d_lifted = lax.psum(
        jnp.einsum("tf,df->td", d_inner, ffn_up, preferred_element_type=WIDE), "ffn"
    )
    d_lift_in, gain_two = norm_back(second, norm_gains[1], d_lifted)
    d_second = d_third + d_lift_in
    d_mixed = d_second.astype(LOWF)
    grad_out = jnp.einsum("tf,td->fd", attended, d_mixed, preferred_element_type=WIDE)
    d_attended = jnp.einsum("td,fd->tf", d_mixed, attn_out, preferred_element_type=WIDE).astype(
        LOWF
    )
    d_triple = attend_back(triple, segment, sums, d_attended)
    grad_in = jnp.einsum("td,ctf->cdf", normed, d_triple, preferred_element_type=WIDE)
    d_normed = lax.psum(
        jnp.einsum("ctf,cdf->td", d_triple, attn_in, preferred_element_type=WIDE), "ffn"
    )
    d_norm_in, gain_one = norm_back(first, norm_gains[0], d_normed)
    d_first = d_second + d_norm_in
    grad_position = jax.ops.segment_sum(d_first, place, position_table.shape[0])
    grads = (
        grad_in,
        grad_out,
        grad_up,
        grad_down,
        grad_position,
        jnp.stack([gain_one, gain_two, gain_three]),
    )
    return (jnp.concatenate([d_first, d_cand], 0), grads)


MESH = pl.DeviceIdType.MESH
TILE = 128
GROUP = 256
REST = 48 * 1024 * 1024


def tile_iota(shape, axis):
    return lax.broadcasted_iota(jnp.int32, shape, axis)


def diagonal_of(size):
    return (tile_iota((size, size), 0) == tile_iota((size, size), 1)).astype(WIDE)


def as_column(row, eye, ones):
    return jnp.dot((eye * row).astype(LOWF), ones, preferred_element_type=WIDE)


def one_hot(condition):
    return jnp.where(condition, 1.0, 0.0).astype(LOWF)


def wait_arrival(ref, semaphore, me, core):
    pltpu.make_async_remote_copy(
        src_ref=ref,
        dst_ref=ref,
        send_sem=semaphore,
        recv_sem=semaphore,
        device_id=(me, core),
        device_id_type=MESH,
    ).wait_recv()


def wait_sent(ref, semaphore, me, core):
    pltpu.make_async_remote_copy(
        src_ref=ref,
        dst_ref=ref,
        send_sem=semaphore,
        recv_sem=semaphore,
        device_id=(me, core),
        device_id_type=MESH,
    ).wait_send()


def send(source, target, send_sem, recv_sem, where):
    pltpu.make_async_remote_copy(
        src_ref=source,
        dst_ref=target,
        send_sem=send_sem,
        recv_sem=recv_sem,
        device_id=where,
        device_id_type=MESH,
    ).start()


def over(count, step):
    def run(index, carry):
        step(index)
        return carry

    lax.fori_loop(0, count, run, 0)


def greet(groups, me, core):
    barrier = pltpu.get_barrier_semaphore()
    over(
        groups - 1,
        lambda k: pl.semaphore_signal(
            barrier, inc=1, device_id=((me + k + 1) % groups, core), device_id_type=MESH
        ),
    )
    pl.semaphore_signal(barrier, inc=1, device_id=(me, 1 - core), device_id_type=MESH)
    return barrier


def fetch_kernel(
    groups,
    table_ref,
    own_ref,
    off_ref,
    rows_ref,
    flat_ref,
    reqs_ref,
    table,
    rank,
    column,
    want,
    asked,
    leaving,
    arrived,
    total,
    part,
    theirs,
    table_sems,
    want_sent,
    want_came,
    row_sent,
    row_came,
    pair_sent,
    pair_came,
):
    me, core = lax.axis_index("dp"), lax.axis_index("ffn")
    held = table_ref.shape[0]
    entries = own_ref.shape[1]
    half = entries // groups
    share = TILE // half
    tiles = entries // TILE
    barrier = greet(groups, me, core)
    mine = pl.ds(pl.multiple_of(core * held, 16), held)
    table[mine, :] = table_ref[...].astype(LOWF)
    table[2 * held :, :] = jnp.zeros((table.shape[0] - 2 * held, table.shape[1]), LOWF)
    upper = one_hot(tile_iota((GROUP, GROUP), 0) <= tile_iota((GROUP, GROUP), 1))
    group_of = tile_iota((groups, GROUP), 0)
    before = jnp.zeros((groups, 1), WIDE)
    filled = jnp.zeros((3 * groups, TILE), WIDE)
    place = (me % share) * half
    for chunk in range(entries // GROUP):
        at = slice(chunk * GROUP, (chunk + 1) * GROUP)
        owner, offset = own_ref[:, at], off_ref[:, at]
        marks = jnp.where(group_of == owner, 1.0, 0.0)
        running = jnp.dot(marks.astype(LOWF), upper, preferred_element_type=WIDE) + before
        before = running[:, GROUP - 1 :]
        ranks = (jnp.sum(marks * running, 0, keepdims=True) - 1.0).astype(jnp.int32) - core * half
        inside = (ranks >= 0) & (ranks < half)
        slot = jnp.where(inside, owner * half + ranks, -1)
        flat_ref[:, at] = jnp.broadcast_to(slot, (8, GROUP))
        picks = one_hot(tile_iota((TILE, GROUP), 0) == jnp.where(inside, ranks + place, -1))
        parts = jnp.concatenate(
            [
                marks * lax.shift_right_logical(offset, 6).astype(WIDE),
                marks * (offset & 63).astype(WIDE),
                marks,
            ],
            0,
        ).astype(LOWF)
        filled = filled + lax.dot_general(
            parts, picks, (((1,), (1,)), ((), ())), preferred_element_type=WIDE
        )
    asking = (
        64.0 * filled[:groups] + filled[groups : 2 * groups] + filled[2 * groups :]
    ).astype(jnp.int32)
    for owner in range(groups):
        want[owner] = jnp.broadcast_to(asking[owner : owner + 1], (8, TILE))
    asked[me] = want[me]
    pl.semaphore_wait(barrier, groups)
    send(table.at[mine], table.at[mine], table_sems.at[0], table_sems.at[1], (me, 1 - core))

    def ask(k):
        owner = (me + k + 1) % groups
        send(want.at[owner], asked.at[me], want_sent.at[owner], want_came.at[me], (owner, core))

    over(groups - 1, ask)
    eye = diagonal_of(TILE)
    ones = jnp.ones((TILE, TILE), LOWF)
    for chunk in range(tiles):
        at = slice(chunk * TILE, (chunk + 1) * TILE)
        slot = flat_ref[0:1, at] + 1
        column[at, :] = (
            64.0 * as_column(lax.shift_right_logical(slot, 6).astype(WIDE), eye, ones)
            + as_column((slot & 63).astype(WIDE), eye, ones)
            - 1.0
        )
    total[...] = jnp.zeros(total.shape, WIDE)
    theirs_at = pl.ds(pl.multiple_of((1 - core) * held, 16), held)
    wait_arrival(table.at[theirs_at], table_sems.at[1], me, core)
    lanes = tile_iota((TILE, TILE), 1).astype(WIDE)

    def serve(k):
        tile = (me // share + k) % tiles
        line = jnp.zeros((1, TILE), jnp.int32)
        for j in range(share):
            source = tile * share + j

            @pl.when(source != me)
            def _():
                wait_arrival(asked.at[source], want_came.at[source], me, core)

        for j in range(share):
            line = line + asked[tile * share + j][0:1, :]
        reqs_ref[pl.ds(tile, 1), :] = line
        number = (
            64.0 * as_column(lax.shift_right_logical(line, 6).astype(WIDE), eye, ones)
            + as_column((line & 63).astype(WIDE), eye, ones)
            - 1.0
        )
        hot = jnp.concatenate(
            [one_hot(number == lanes + float(b * TILE)) for b in range(table.shape[0] // TILE)], 1
        )
        picked = jnp.dot(hot, table[...], preferred_element_type=WIDE).astype(LOWF)
        leaving[pl.ds(pl.multiple_of(tile * TILE, TILE), TILE), :] = picked
        for j in range(share):
            source = tile * share + j
            out = leaving.at[pl.ds(pl.multiple_of(source * half, half), half)]
            into = pl.ds(pl.multiple_of(me * half, half), half)

            @pl.when(source != me)
            def _():
                send(out, arrived.at[into], row_sent.at[source], row_came.at[me], (source, core))

            @pl.when(source == me)
            def _():
                arrived[into, :] = picked[j * half : (j + 1) * half]

    over(tiles, serve)

    def place_rows(k):
        first = me * half // GROUP
        group = (first - k + entries // GROUP) % (entries // GROUP)
        for j in range(GROUP // half):
            owner = group * (GROUP // half) + j

            @pl.when(owner != me)
            def _():
                block = arrived.at[pl.ds(pl.multiple_of(owner * half, half), half)]
                wait_arrival(block, row_came.at[owner], me, core)

        came = arrived[pl.ds(pl.multiple_of(group * GROUP, GROUP), GROUP), :]
        base = (group * GROUP).astype(WIDE)

        def block(b):
            at = pl.ds(pl.multiple_of(b * GROUP, GROUP), GROUP)
            where = column[at, :] - base
            lane = tile_iota((GROUP, TILE), 1).astype(WIDE)
            hot = jnp.concatenate([one_hot(where == lane), one_hot(where == lane + float(TILE))], 1)
            total[at, :] += jnp.dot(hot, came, preferred_element_type=WIDE)

        over(entries // GROUP, block)

    over(entries // GROUP, place_rows)
    for side in range(2):
        at = pl.ds(side * entries // 2, entries // 2)
        part[at, :] = total[at, :].astype(LOWF)
        send(part.at[at], theirs.at[at], pair_sent.at[side], pair_came.at[side], (me, 1 - core))
    for side in range(2):
        at = pl.ds(side * entries // 2, entries // 2)
        wait_arrival(theirs.at[at], pair_came.at[side], me, core)
        rows_ref[at, :] = part[at, :] + theirs[at, :]
        wait_sent(part.at[at], pair_sent.at[side], me, core)
    wait_sent(table.at[mine], table_sems.at[0], me, core)

    def finish(k):
        other = (me + k + 1) % groups
        wait_sent(want.at[other], want_sent.at[other], me, core)
        block = leaving.at[pl.ds(pl.multiple_of(other * half, half), half)]
        wait_sent(block, row_sent.at[other], me, core)

    over(groups - 1, finish)


VMEM = pl.BlockSpec(memory_space=pltpu.VMEM)
DMA = pltpu.SemaphoreType.DMA


def fetch_rows(item_table, owners, offsets, groups):
    held, width = item_table.shape
    entries = owners.shape[1]
    half = entries // groups
    padded = -(-2 * held // TILE) * TILE
    return pl.pallas_call(
        functools.partial(fetch_kernel, groups),
        out_shape=(
            jax.ShapeDtypeStruct((entries, width), LOWF),
            jax.ShapeDtypeStruct((8, entries), jnp.int32),
            jax.ShapeDtypeStruct((entries // TILE, TILE), jnp.int32),
        ),
        in_specs=[VMEM] * 3,
        out_specs=(VMEM,) * 3,
        scratch_shapes=[
            pltpu.VMEM((padded, width), LOWF),
            pltpu.VMEM((8, entries), jnp.int32),
            pltpu.VMEM((entries, TILE), WIDE),
            pltpu.VMEM((groups, 8, TILE), jnp.int32),
            pltpu.VMEM((groups, 8, TILE), jnp.int32),
            pltpu.VMEM((entries, width), LOWF),
            pltpu.VMEM((entries, width), LOWF),
            pltpu.VMEM((entries, width), WIDE),
            pltpu.VMEM((entries, width), LOWF),
            pltpu.VMEM((entries, width), LOWF),
            DMA((2,)),
            DMA((groups,)),
            DMA((groups,)),
            DMA((groups,)),
            DMA((groups,)),
            DMA((2,)),
            DMA((2,)),
        ],
        compiler_params=pltpu.CompilerParams(
            collective_id=0, has_side_effects=True, vmem_limit_bytes=REST
        ),
    )(item_table, owners, offsets)


def return_kernel(
    groups,
    rows_ref,
    flat_ref,
    reqs_ref,
    in_ref,
    out_ref,
    up_ref,
    down_ref,
    pos_ref,
    small_ref,
    table_ref,
    weights_ref,
    position_ref,
    few_ref,
    stats_ref,
    grads,
    shares,
    shard,
    whole,
    leaving,
    arrived,
    total,
    theirs,
    few,
    squares,
    other_half,
    share_sent,
    share_came,
    row_sent,
    row_came,
    whole_sent,
    whole_came,
    few_sent,
    few_came,
    square_sent,
    square_came,
    pair_sems,
):
    me, core = lax.axis_index("dp"), lax.axis_index("ffn")
    held, width = table_ref.shape
    entries = flat_ref.shape[1]
    half = entries // groups
    share = TILE // half
    tiles = entries // TILE
    length = grads.shape[0] // groups
    barrier = greet(groups, me, core)

    def greet_across(k):
        where = ((me + k + 1) % groups, 1 - core)
        pl.semaphore_signal(barrier, inc=1, device_id=where, device_id_type=MESH)

    over(groups - 1, greet_across)
    at = 0
    for block in (
        *(in_ref[c] for c in range(3)),
        out_ref[...],
        up_ref[:, :width],
        up_ref[:, width:],
        down_ref[...],
    ):
        grads[at : at + block.shape[0], :] = block.astype(LOWF)
        at += block.shape[0]
    pos_half = pos_ref.shape[0] // 2
    my_half = pl.ds(pl.multiple_of(core * pos_half, pos_half), pos_half)
    pos_at = at
    grads[at : at + pos_half, :] = pos_ref[my_half, :].astype(LOWF)
    at += pos_half
    if at < grads.shape[0]:
        grads[at:, :] = jnp.zeros((grads.shape[0] - at, width), LOWF)
    few[me] = small_ref[...]
    pl.semaphore_wait(barrier, 2 * groups - 1)
    my_share = pl.ds(pl.multiple_of(me * length, 16), length)

    def give_share(k):
        other = (me + k + 1) % groups
        block = grads.at[pl.ds(pl.multiple_of(other * length, 16), length)]
        send(block, shares.at[my_share], share_sent.at[other], share_came.at[me], (other, core))
        send(few.at[me], few.at[me], few_sent.at[other], few_came.at[me], (other, core))

    over(groups - 1, give_share)

    def give_rows(k):
        tile = (me // share + k) % tiles
        number = flat_ref[0:1, :] - tile * TILE
        hot = one_hot(tile_iota((TILE, entries), 0) == number)
        picked = jnp.dot(hot, rows_ref[...], preferred_element_type=WIDE).astype(LOWF)
        leaving[pl.ds(pl.multiple_of(tile * TILE, TILE), TILE), :] = picked
        for j in range(share):
            owner = tile * share + j
            out = leaving.at[pl.ds(pl.multiple_of(owner * half, half), half)]
            into = pl.ds(pl.multiple_of(me * half, half), half)

            @pl.when(owner != me)
            def _():
                send(out, arrived.at[into], row_sent.at[owner], row_came.at[me], (owner, core))

            @pl.when(owner == me)
            def _():
                arrived[into, :] = picked[j * half : (j + 1) * half]

    over(tiles, give_rows)
    shard[...] = grads[my_share, :].astype(WIDE)

    def take_share(k):
        other = (me - k - 1 + groups) % groups
        block = pl.ds(pl.multiple_of(other * length, 16), length)
        wait_arrival(shares.at[block], share_came.at[other], me, core)
        shard[...] += shares[block, :].astype(WIDE)

    over(groups - 1, take_share)
    whole[my_share, :] = shard[...].astype(LOWF)

    def give_whole(k):
        other = (me + k + 1) % groups
        block = whole.at[my_share]
        send(block, block, whole_sent.at[other], whole_came.at[me], (other, core))

    over(groups - 1, give_whole)
    total[...] = jnp.zeros(total.shape, WIDE)
    step_rows = 2 * held // 7

    def take_rows(k):
        first = me * half // GROUP
        group = (first - k + entries // GROUP) % (entries // GROUP)
        for j in range(GROUP // half):
            source = group * (GROUP // half) + j

            @pl.when(source != me)
            def _():
                block = arrived.at[pl.ds(pl.multiple_of(source * half, half), half)]
                wait_arrival(block, row_came.at[source], me, core)

        came = arrived[pl.ds(pl.multiple_of(group * GROUP, GROUP), GROUP), :]
        lines = [reqs_ref[pl.ds(2 * group + i, 1), :] - 1 for i in range(2)]

        def block(b):
            at = pl.ds(pl.multiple_of(b * step_rows, 8), step_rows)
            rows = tile_iota((step_rows, TILE), 0) + b * step_rows
            hot = jnp.concatenate([one_hot(rows == line) for line in lines], 1)
            total[at, :] += jnp.dot(hot, came, preferred_element_type=WIDE)

        over(7, block)

    over(entries // GROUP, take_rows)
    away = total.at[pl.ds(pl.multiple_of((1 - core) * held, 8), held)]
    send(away, theirs, pair_sems.at[0], pair_sems.at[1], (me, 1 - core))
    wait_arrival(theirs, pair_sems.at[1], me, core)
    final = total[pl.ds(pl.multiple_of(core * held, 8), held), :] + theirs[...]
    table_ref[...] = final
    own_square = jnp.sum(final * final) + jnp.sum(shard[...] * shard[...])
    slot = me * 2 + core
    squares[slot] = jnp.full((8, TILE), own_square, WIDE)

    def give_square(k):
        where = me * 2 + core + k + 1
        where = where % (2 * groups)
        other = (where // 2, where % 2)
        send(squares.at[slot], squares.at[slot], square_sent.at[where], square_came.at[slot], other)

    over(2 * groups - 1, give_square)

    def take_whole(k):
        other = (me - k - 1 + groups) % groups
        block = pl.ds(pl.multiple_of(other * length, 16), length)
        wait_arrival(whole.at[block], whole_came.at[other], me, core)
        wait_arrival(few.at[other], few_came.at[other], me, core)

    over(groups - 1, take_whole)
    position_own = whole.at[pl.ds(pos_at, pos_half)]
    send(position_own, other_half, pair_sems.at[2], pair_sems.at[3], (me, 1 - core))
    weights_ref[...] = whole[...]
    few_total = few[0]
    for source in range(1, groups):
        few_total = few_total + few[source]
    few_ref[...] = few_total
    position_ref[my_half, :] = whole[pos_at : pos_at + pos_half, :]
    wait_arrival(other_half, pair_sems.at[3], me, core)
    your_half = pl.ds(pl.multiple_of((1 - core) * pos_half, pos_half), pos_half)
    position_ref[your_half, :] = other_half[...]

    def take_square(k):
        other = (slot + k + 1) % (2 * groups)
        wait_arrival(squares.at[other], square_came.at[other], me, core)

    over(2 * groups - 1, take_square)
    stats_ref[...] = jnp.sum(squares[...], 0)

    def finish(k):
        other = (me + k + 1) % groups
        block = grads.at[pl.ds(pl.multiple_of(other * length, 16), length)]
        wait_sent(block, share_sent.at[other], me, core)
        wait_sent(few.at[me], few_sent.at[other], me, core)
        block = leaving.at[pl.ds(pl.multiple_of(other * half, half), half)]
        wait_sent(block, row_sent.at[other], me, core)
        wait_sent(whole.at[my_share], whole_sent.at[other], me, core)

    over(groups - 1, finish)

    def finish_square(k):
        other = (slot + k + 1) % (2 * groups)
        wait_sent(squares.at[slot], square_sent.at[other], me, core)

    over(2 * groups - 1, finish_square)
    wait_sent(away, pair_sems.at[0], me, core)
    wait_sent(position_own, pair_sems.at[2], me, core)


def return_rows(d_rows, flat, reqs, grads, small, held, groups):
    width = d_rows.shape[1]
    entries = flat.shape[1]
    grad_in, grad_out, grad_up, grad_down, grad_position = grads
    rows = (grad_in.size + grad_out.size + grad_up.size + grad_down.size) // width
    rows = rows + grad_position.shape[0] // 2
    length = -(-rows // groups // 16) * 16
    if length * groups < rows:
        length = length + 16
    return pl.pallas_call(
        functools.partial(return_kernel, groups),
        out_shape=(
            jax.ShapeDtypeStruct((held, width), WIDE),
            jax.ShapeDtypeStruct((groups * length, width), LOWF),
            jax.ShapeDtypeStruct(grad_position.shape, LOWF),
            jax.ShapeDtypeStruct(small.shape, WIDE),
            jax.ShapeDtypeStruct((8, TILE), WIDE),
        ),
        in_specs=[VMEM] * 9,
        out_specs=(VMEM,) * 5,
        scratch_shapes=[
            pltpu.VMEM((groups * length, width), LOWF),
            pltpu.VMEM((groups * length, width), LOWF),
            pltpu.VMEM((length, width), WIDE),
            pltpu.VMEM((groups * length, width), LOWF),
            pltpu.VMEM((entries, width), LOWF),
            pltpu.VMEM((entries, width), LOWF),
            pltpu.VMEM((2 * held, width), WIDE),
            pltpu.VMEM((held, width), WIDE),
            pltpu.VMEM((groups, *small.shape), WIDE),
            pltpu.VMEM((2 * groups, 8, TILE), WIDE),
            pltpu.VMEM((grad_position.shape[0] // 2, width), LOWF),
            DMA((groups,)),
            DMA((groups,)),
            DMA((groups,)),
            DMA((groups,)),
            DMA((groups,)),
            DMA((groups,)),
            DMA((groups,)),
            DMA((groups,)),
            DMA((2 * groups,)),
            DMA((2 * groups,)),
            DMA((4,)),
        ],
        compiler_params=pltpu.CompilerParams(
            collective_id=1, has_side_effects=True, vmem_limit_bytes=REST
        ),
    )(d_rows, flat, reqs, grad_in, grad_out, grad_up, grad_down, grad_position, small)


def adamw(weight, grad, first, second, decay, rate):
    first = BETA_ONE * first + (1.0 - BETA_ONE) * grad
    second = BETA_TWO * second + (1.0 - BETA_TWO) * grad * grad
    moved = first / (1.0 - BETA_ONE**STEP) / (jnp.sqrt(second / (1.0 - BETA_TWO**STEP)) + ADAM_EPS)
    return (weight - rate * (moved + decay * weight), first, second)


def body(
    item_table,
    attn_in,
    attn_out,
    ffn_up,
    ffn_down,
    position_table,
    norm_gains,
    item_first,
    item_second,
    attn_in_first,
    attn_in_second,
    attn_out_first,
    attn_out_second,
    ffn_up_first,
    ffn_up_second,
    ffn_down_first,
    ffn_down_second,
    position_first,
    position_second,
    gains_first,
    gains_second,
    owner_group,
    row_offset,
    segment_ids,
    live_slots,
    log_freq,
):
    groups = lax.axis_size("dp")
    slots = segment_ids.shape[1]
    owners = owner_group.reshape(1, -1)
    offsets = row_offset.reshape(1, -1)
    weights = (
        attn_in.astype(LOWF),
        attn_out.astype(LOWF),
        ffn_up.astype(LOWF),
        ffn_down.astype(LOWF),
        position_table,
        norm_gains,
    )
    rows, flat, reqs = fetch_rows(item_table, owners, offsets, groups)
    loss, saved = layer_forward(rows, segment_ids[0], live_slots[0], log_freq[0], weights)
    d_rows, grads = layer_backward(saved, rows[slots:], segment_ids[0], weights)
    few = jnp.concatenate(
        [
            grads[5],
            jnp.full((1, rows.shape[1]), loss, WIDE),
            jnp.full((1, rows.shape[1]), jnp.sum(live_slots).astype(WIDE), WIDE),
            jnp.zeros((3, rows.shape[1]), WIDE),
        ],
        0,
    )
    held, width = item_table.shape
    grad_table, shared, grad_position, few, stats = return_rows(
        d_rows.astype(LOWF), flat, reqs, grads[:5], few, held, groups
    )
    shared = shared.astype(WIDE)
    grad_position = grad_position.astype(WIDE)
    last = 3 * width
    grad_in = shared[:last].reshape(attn_in.shape)
    grad_out = shared[last : last + attn_out.shape[0]]
    last = last + attn_out.shape[0]
    grad_up = jnp.concatenate([shared[last : last + width], shared[last + width : last + 2 * width]], 1)
    last = last + 2 * width
    grad_down = shared[last : last + ffn_down.shape[0]]
    grad_gains = few[:3]
    loss_sum, live_count = few[3, 0], few[4, 0]
    grad_norm = jnp.sqrt(stats[0, 0] + jnp.sum(grad_gains * grad_gains))
    factor = CLIP / jnp.maximum(grad_norm, CLIP)
    table_new = adamw(item_table, grad_table * factor, item_first, item_second, DECAY, RATE)
    in_new = adamw(attn_in, grad_in * factor, attn_in_first, attn_in_second, DECAY, RATE)
    out_new = adamw(attn_out, grad_out * factor, attn_out_first, attn_out_second, DECAY, RATE)
    up_new = adamw(ffn_up, grad_up * factor, ffn_up_first, ffn_up_second, DECAY, RATE)
    down_new = adamw(ffn_down, grad_down * factor, ffn_down_first, ffn_down_second, DECAY, RATE)
    position_new = adamw(
        position_table,
        grad_position * factor,
        position_first,
        position_second,
        DECAY,
        RATE_POSITION,
    )
    gains_new = adamw(norm_gains, grad_gains * factor, gains_first, gains_second, 0.0, RATE_GAINS)
    return (
        table_new[0],
        table_new[1],
        table_new[2],
        in_new[0],
        in_new[1],
        in_new[2],
        out_new[0],
        out_new[1],
        out_new[2],
        up_new[0],
        up_new[1],
        up_new[2],
        down_new[0],
        down_new[1],
        down_new[2],
        position_new[0],
        position_new[1],
        position_new[2],
        gains_new[0],
        gains_new[1],
        gains_new[2],
        loss_sum,
        live_count,
        grad_norm,
    )


def solution(mesh):
    return jax.shard_map(
        body,
        mesh=mesh,
        in_specs=(
            P(("dp", "ffn"), None),
            P(None, None, "ffn"),
            P("ffn", None),
            P(None, "ffn"),
            P("ffn", None),
            P(),
            P(),
            P(("dp", "ffn"), None),
            P(("dp", "ffn"), None),
            P(None, None, "ffn"),
            P(None, None, "ffn"),
            P("ffn", None),
            P("ffn", None),
            P(None, "ffn"),
            P(None, "ffn"),
            P("ffn", None),
            P("ffn", None),
            P(),
            P(),
            P(),
            P(),
            P("dp", None, None),
            P("dp", None),
            P("dp", None),
            P("dp"),
            P("dp", None),
        ),
        out_specs=(
            P(("dp", "ffn"), None),
            P(("dp", "ffn"), None),
            P(("dp", "ffn"), None),
            P(None, None, "ffn"),
            P(None, None, "ffn"),
            P(None, None, "ffn"),
            P("ffn", None),
            P("ffn", None),
            P("ffn", None),
            P(None, "ffn"),
            P(None, "ffn"),
            P(None, "ffn"),
            P("ffn", None),
            P("ffn", None),
            P("ffn", None),
            P(),
            P(),
            P(),
            P(),
            P(),
            P(),
            P(),
            P(),
            P(),
        ),
        check_vma=False,
    )
```

```python
import functools
import types

import jax
import jax.numpy as jnp
from jax import lax
from jax.experimental import pallas as pl
from jax.experimental.pallas import tpu as pltpu
from jax.sharding import PartitionSpec as P

HEAD = 64
STEP = 10


EPSILON = 1e-05
SCALE = 0.125
CLIP = 1.0
RATE = 0.05
RATE_POSITION = 0.3
RATE_GAINS = 0.5
DECAY = 0.01
BETA_ONE = 0.9
BETA_TWO = 0.999
ADAM_EPS = 1e-08
GELU_A = 0.7978845608028654
GELU_B = 0.044715
LOWF = jnp.bfloat16
WIDE = jnp.float32


MESH = pl.DeviceIdType.MESH
TILE = 128
GROUP = 256
REST = 48 * 1024 * 1024


def tile_iota(shape, axis):
    return lax.broadcasted_iota(jnp.int32, shape, axis)


def diagonal_of(size):
    return (tile_iota((size, size), 0) == tile_iota((size, size), 1)).astype(WIDE)


def as_column(row, eye, ones):
    return jnp.dot((eye * row).astype(LOWF), ones, preferred_element_type=WIDE)


def one_hot(condition):
    return jnp.where(condition, 1.0, 0.0).astype(LOWF)


def wait_arrival(ref, semaphore, me, core):
    pltpu.make_async_remote_copy(
        src_ref=ref,
        dst_ref=ref,
        send_sem=semaphore,
        recv_sem=semaphore,
        device_id=(me, core),
        device_id_type=MESH,
    ).wait_recv()


def wait_sent(ref, semaphore, me, core):
    pltpu.make_async_remote_copy(
        src_ref=ref,
        dst_ref=ref,
        send_sem=semaphore,
        recv_sem=semaphore,
        device_id=(me, core),
        device_id_type=MESH,
    ).wait_send()


def send(source, target, send_sem, recv_sem, where):
    pltpu.make_async_remote_copy(
        src_ref=source,
        dst_ref=target,
        send_sem=send_sem,
        recv_sem=recv_sem,
        device_id=where,
        device_id_type=MESH,
    ).start()


def over(count, step):
    def run(index, carry):
        step(index)
        return carry

    lax.fori_loop(0, count, run, 0)


def greet(groups, me, core):
    barrier = pltpu.get_barrier_semaphore()
    over(
        groups - 1,
        lambda k: pl.semaphore_signal(
            barrier, inc=1, device_id=((me + k + 1) % groups, core), device_id_type=MESH
        ),
    )
    pl.semaphore_signal(barrier, inc=1, device_id=(me, 1 - core), device_id_type=MESH)
    return barrier


def fetch_kernel(
    groups,
    table_ref,
    own_ref,
    off_ref,
    rows_ref,
    flat_ref,
    reqs_ref,
    table,
    rank,
    column,
    want,
    asked,
    leaving,
    arrived,
    total,
    part,
    theirs,
    table_sems,
    want_sent,
    want_came,
    row_sent,
    row_came,
    pair_sent,
    pair_came,
):
    me, core = lax.axis_index("dp"), lax.axis_index("ffn")
    held = table_ref.shape[0]
    entries = own_ref.shape[1]
    half = entries // groups
    share = TILE // half
    tiles = entries // TILE
    barrier = greet(groups, me, core)
    mine = pl.ds(pl.multiple_of(core * held, 16), held)
    table[mine, :] = table_ref[...].astype(LOWF)
    table[2 * held :, :] = jnp.zeros((table.shape[0] - 2 * held, table.shape[1]), LOWF)
    upper = one_hot(tile_iota((GROUP, GROUP), 0) <= tile_iota((GROUP, GROUP), 1))
    group_of = tile_iota((groups, GROUP), 0)
    before = jnp.zeros((groups, 1), WIDE)
    filled = jnp.zeros((3 * groups, TILE), WIDE)
    place = (me % share) * half
    for chunk in range(entries // GROUP):
        at = slice(chunk * GROUP, (chunk + 1) * GROUP)
        owner, offset = own_ref[:, at], off_ref[:, at]
        marks = jnp.where(group_of == owner, 1.0, 0.0)
        running = jnp.dot(marks.astype(LOWF), upper, preferred_element_type=WIDE) + before
        before = running[:, GROUP - 1 :]
        ranks = (jnp.sum(marks * running, 0, keepdims=True) - 1.0).astype(jnp.int32) - core * half
        inside = (ranks >= 0) & (ranks < half)
        slot = jnp.where(inside, owner * half + ranks, -1)
        flat_ref[:, at] = jnp.broadcast_to(slot, (8, GROUP))
        picks = one_hot(tile_iota((TILE, GROUP), 0) == jnp.where(inside, ranks + place, -1))
        parts = jnp.concatenate(
            [
                marks * lax.shift_right_logical(offset, 6).astype(WIDE),
                marks * (offset & 63).astype(WIDE),
                marks,
            ],
            0,
        ).astype(LOWF)
        filled = filled + lax.dot_general(
            parts, picks, (((1,), (1,)), ((), ())), preferred_element_type=WIDE
        )
    asking = (
        64.0 * filled[:groups] + filled[groups : 2 * groups] + filled[2 * groups :]
    ).astype(jnp.int32)
    for owner in range(groups):
        want[owner] = jnp.broadcast_to(asking[owner : owner + 1], (8, TILE))
    asked[me] = want[me]
    pl.semaphore_wait(barrier, groups)
    send(table.at[mine], table.at[mine], table_sems.at[0], table_sems.at[1], (me, 1 - core))

    def ask(k):
        owner = (me + k + 1) % groups
        send(want.at[owner], asked.at[me], want_sent.at[owner], want_came.at[me], (owner, core))

    over(groups - 1, ask)
    eye = diagonal_of(TILE)
    ones = jnp.ones((TILE, TILE), LOWF)
    for chunk in range(tiles):
        at = slice(chunk * TILE, (chunk + 1) * TILE)
        slot = flat_ref[0:1, at] + 1
        column[at, :] = (
            64.0 * as_column(lax.shift_right_logical(slot, 6).astype(WIDE), eye, ones)
            + as_column((slot & 63).astype(WIDE), eye, ones)
            - 1.0
        )
    total[...] = jnp.zeros(total.shape, WIDE)
    theirs_at = pl.ds(pl.multiple_of((1 - core) * held, 16), held)
    wait_arrival(table.at[theirs_at], table_sems.at[1], me, core)
    lanes = tile_iota((TILE, TILE), 1).astype(WIDE)

    def serve(k):
        tile = (me // share + k) % tiles
        line = jnp.zeros((1, TILE), jnp.int32)
        for j in range(share):
            source = tile * share + j

            @pl.when(source != me)
            def _():
                wait_arrival(asked.at[source], want_came.at[source], me, core)

        for j in range(share):
            line = line + asked[tile * share + j][0:1, :]
        reqs_ref[pl.ds(tile, 1), :] = line
        number = (
            64.0 * as_column(lax.shift_right_logical(line, 6).astype(WIDE), eye, ones)
            + as_column((line & 63).astype(WIDE), eye, ones)
            - 1.0
        )
        hot = jnp.concatenate(
            [one_hot(number == lanes + float(b * TILE)) for b in range(table.shape[0] // TILE)], 1
        )
        picked = jnp.dot(hot, table[...], preferred_element_type=WIDE).astype(LOWF)
        leaving[pl.ds(pl.multiple_of(tile * TILE, TILE), TILE), :] = picked
        for j in range(share):
            source = tile * share + j
            out = leaving.at[pl.ds(pl.multiple_of(source * half, half), half)]
            into = pl.ds(pl.multiple_of(me * half, half), half)

            @pl.when(source != me)
            def _():
                send(out, arrived.at[into], row_sent.at[source], row_came.at[me], (source, core))

            @pl.when(source == me)
            def _():
                arrived[into, :] = picked[j * half : (j + 1) * half]

    over(tiles, serve)

    def place_rows(k):
        first = me * half // GROUP
        group = (first - k + entries // GROUP) % (entries // GROUP)
        for j in range(GROUP // half):
            owner = group * (GROUP // half) + j

            @pl.when(owner != me)
            def _():
                block = arrived.at[pl.ds(pl.multiple_of(owner * half, half), half)]
                wait_arrival(block, row_came.at[owner], me, core)

        came = arrived[pl.ds(pl.multiple_of(group * GROUP, GROUP), GROUP), :]
        base = (group * GROUP).astype(WIDE)

        def block(b):
            at = pl.ds(pl.multiple_of(b * GROUP, GROUP), GROUP)
            where = column[at, :] - base
            lane = tile_iota((GROUP, TILE), 1).astype(WIDE)
            hot = jnp.concatenate([one_hot(where == lane), one_hot(where == lane + float(TILE))], 1)
            total[at, :] += jnp.dot(hot, came, preferred_element_type=WIDE)

        over(entries // GROUP, block)

    over(entries // GROUP, place_rows)
    for side in range(2):
        at = pl.ds(side * entries // 2, entries // 2)
        part[at, :] = total[at, :].astype(LOWF)
        send(part.at[at], theirs.at[at], pair_sent.at[side], pair_came.at[side], (me, 1 - core))
    for side in range(2):
        at = pl.ds(side * entries // 2, entries // 2)
        wait_arrival(theirs.at[at], pair_came.at[side], me, core)
        rows_ref[at, :] = part[at, :] + theirs[at, :]
        wait_sent(part.at[at], pair_sent.at[side], me, core)
    wait_sent(table.at[mine], table_sems.at[0], me, core)

    def finish(k):
        other = (me + k + 1) % groups
        wait_sent(want.at[other], want_sent.at[other], me, core)
        block = leaving.at[pl.ds(pl.multiple_of(other * half, half), half)]
        wait_sent(block, row_sent.at[other], me, core)

    over(groups - 1, finish)


VMEM = pl.BlockSpec(memory_space=pltpu.VMEM)
DMA = pltpu.SemaphoreType.DMA


def fetch_rows(item_table, owners, offsets, groups):
    held, width = item_table.shape
    entries = owners.shape[1]
    half = entries // groups
    padded = -(-2 * held // TILE) * TILE
    return pl.pallas_call(
        functools.partial(fetch_kernel, groups),
        out_shape=(
            jax.ShapeDtypeStruct((entries, width), LOWF),
            jax.ShapeDtypeStruct((8, entries), jnp.int32),
            jax.ShapeDtypeStruct((entries // TILE, TILE), jnp.int32),
        ),
        in_specs=[VMEM] * 3,
        out_specs=(VMEM,) * 3,
        scratch_shapes=[
            pltpu.VMEM((padded, width), LOWF),
            pltpu.VMEM((8, entries), jnp.int32),
            pltpu.VMEM((entries, TILE), WIDE),
            pltpu.VMEM((groups, 8, TILE), jnp.int32),
            pltpu.VMEM((groups, 8, TILE), jnp.int32),
            pltpu.VMEM((entries, width), LOWF),
            pltpu.VMEM((entries, width), LOWF),
            pltpu.VMEM((entries, width), WIDE),
            pltpu.VMEM((entries, width), LOWF),
            pltpu.VMEM((entries, width), LOWF),
            DMA((2,)),
            DMA((groups,)),
            DMA((groups,)),
            DMA((groups,)),
            DMA((groups,)),
            DMA((2,)),
            DMA((2,)),
        ],
        compiler_params=pltpu.CompilerParams(
            collective_id=0, has_side_effects=True, vmem_limit_bytes=REST
        ),
    )(item_table, owners, offsets)


def return_kernel(
    groups,
    rows_ref,
    flat_ref,
    reqs_ref,
    in_ref,
    out_ref,
    up_ref,
    down_ref,
    pos_ref,
    small_ref,
    table_ref,
    weights_ref,
    position_ref,
    few_ref,
    stats_ref,
    grads,
    shares,
    shard,
    whole,
    leaving,
    arrived,
    total,
    theirs,
    few,
    squares,
    other_half,
    share_sent,
    share_came,
    row_sent,
    row_came,
    whole_sent,
    whole_came,
    few_sent,
    few_came,
    square_sent,
    square_came,
    pair_sems,
):
    me, core = lax.axis_index("dp"), lax.axis_index("ffn")
    held, width = table_ref.shape
    entries = flat_ref.shape[1]
    half = entries // groups
    share = TILE // half
    tiles = entries // TILE
    length = grads.shape[0] // groups
    barrier = greet(groups, me, core)

    def greet_across(k):
        where = ((me + k + 1) % groups, 1 - core)
        pl.semaphore_signal(barrier, inc=1, device_id=where, device_id_type=MESH)

    over(groups - 1, greet_across)
    at = 0
    for block in (
        *(in_ref[c] for c in range(3)),
        out_ref[...],
        up_ref[:, :width],
        up_ref[:, width:],
        down_ref[...],
    ):
        grads[at : at + block.shape[0], :] = block.astype(LOWF)
        at += block.shape[0]
    pos_half = pos_ref.shape[0]
    my_half = pl.ds(pl.multiple_of(core * pos_half, pos_half), pos_half)
    pos_at = at
    grads[at : at + pos_half, :] = pos_ref[...].astype(LOWF)
    at += pos_half
    if at < grads.shape[0]:
        grads[at:, :] = jnp.zeros((grads.shape[0] - at, width), LOWF)
    few[me] = small_ref[...]
    pl.semaphore_wait(barrier, 2 * groups - 1)
    my_share = pl.ds(pl.multiple_of(me * length, 16), length)

    def give_share(k):
        other = (me + k + 1) % groups
        block = grads.at[pl.ds(pl.multiple_of(other * length, 16), length)]
        send(block, shares.at[my_share], share_sent.at[other], share_came.at[me], (other, core))
        send(few.at[me], few.at[me], few_sent.at[other], few_came.at[me], (other, core))

    over(groups - 1, give_share)

    def give_rows(k):
        tile = (me // share + k) % tiles
        number = flat_ref[0:1, :] - tile * TILE
        hot = one_hot(tile_iota((TILE, entries), 0) == number)
        picked = jnp.dot(hot, rows_ref[...], preferred_element_type=WIDE).astype(LOWF)
        leaving[pl.ds(pl.multiple_of(tile * TILE, TILE), TILE), :] = picked
        for j in range(share):
            owner = tile * share + j
            out = leaving.at[pl.ds(pl.multiple_of(owner * half, half), half)]
            into = pl.ds(pl.multiple_of(me * half, half), half)

            @pl.when(owner != me)
            def _():
                send(out, arrived.at[into], row_sent.at[owner], row_came.at[me], (owner, core))

            @pl.when(owner == me)
            def _():
                arrived[into, :] = picked[j * half : (j + 1) * half]

    over(tiles, give_rows)
    shard[...] = grads[my_share, :].astype(WIDE)

    def take_share(k):
        other = (me - k - 1 + groups) % groups
        block = pl.ds(pl.multiple_of(other * length, 16), length)
        wait_arrival(shares.at[block], share_came.at[other], me, core)
        shard[...] += shares[block, :].astype(WIDE)

    over(groups - 1, take_share)
    whole[my_share, :] = shard[...].astype(LOWF)

    def give_whole(k):
        other = (me + k + 1) % groups
        block = whole.at[my_share]
        send(block, block, whole_sent.at[other], whole_came.at[me], (other, core))

    over(groups - 1, give_whole)
    total[...] = jnp.zeros(total.shape, WIDE)
    step_rows = 2 * held // 7

    def take_rows(k):
        first = me * half // GROUP
        group = (first - k + entries // GROUP) % (entries // GROUP)
        for j in range(GROUP // half):
            source = group * (GROUP // half) + j

            @pl.when(source != me)
            def _():
                block = arrived.at[pl.ds(pl.multiple_of(source * half, half), half)]
                wait_arrival(block, row_came.at[source], me, core)

        came = arrived[pl.ds(pl.multiple_of(group * GROUP, GROUP), GROUP), :]
        lines = [reqs_ref[pl.ds(2 * group + i, 1), :] - 1 for i in range(2)]

        def block(b):
            at = pl.ds(pl.multiple_of(b * step_rows, 8), step_rows)
            rows = tile_iota((step_rows, TILE), 0) + b * step_rows
            hot = jnp.concatenate([one_hot(rows == line) for line in lines], 1)
            total[at, :] += jnp.dot(hot, came, preferred_element_type=WIDE)

        over(7, block)

    over(entries // GROUP, take_rows)
    away = total.at[pl.ds(pl.multiple_of((1 - core) * held, 8), held)]
    send(away, theirs, pair_sems.at[0], pair_sems.at[1], (me, 1 - core))
    wait_arrival(theirs, pair_sems.at[1], me, core)
    final = total[pl.ds(pl.multiple_of(core * held, 8), held), :] + theirs[...]
    table_ref[...] = final
    own_square = jnp.sum(final * final) + jnp.sum(shard[...] * shard[...])
    slot = me * 2 + core
    squares[slot] = jnp.full((8, TILE), own_square, WIDE)

    def give_square(k):
        where = me * 2 + core + k + 1
        where = where % (2 * groups)
        other = (where // 2, where % 2)
        send(squares.at[slot], squares.at[slot], square_sent.at[where], square_came.at[slot], other)

    over(2 * groups - 1, give_square)

    def take_whole(k):
        other = (me - k - 1 + groups) % groups
        block = pl.ds(pl.multiple_of(other * length, 16), length)
        wait_arrival(whole.at[block], whole_came.at[other], me, core)
        wait_arrival(few.at[other], few_came.at[other], me, core)

    over(groups - 1, take_whole)
    position_own = whole.at[pl.ds(pos_at, pos_half)]
    send(position_own, other_half, pair_sems.at[2], pair_sems.at[3], (me, 1 - core))
    weights_ref[...] = whole[...]
    few_total = few[0]
    for source in range(1, groups):
        few_total = few_total + few[source]
    few_ref[...] = few_total
    position_ref[my_half, :] = whole[pos_at : pos_at + pos_half, :]
    wait_arrival(other_half, pair_sems.at[3], me, core)
    your_half = pl.ds(pl.multiple_of((1 - core) * pos_half, pos_half), pos_half)
    position_ref[your_half, :] = other_half[...]

    def take_square(k):
        other = (slot + k + 1) % (2 * groups)
        wait_arrival(squares.at[other], square_came.at[other], me, core)

    over(2 * groups - 1, take_square)
    stats_ref[...] = jnp.sum(squares[...], 0)

    def finish(k):
        other = (me + k + 1) % groups
        block = grads.at[pl.ds(pl.multiple_of(other * length, 16), length)]
        wait_sent(block, share_sent.at[other], me, core)
        wait_sent(few.at[me], few_sent.at[other], me, core)
        block = leaving.at[pl.ds(pl.multiple_of(other * half, half), half)]
        wait_sent(block, row_sent.at[other], me, core)
        wait_sent(whole.at[my_share], whole_sent.at[other], me, core)

    over(groups - 1, finish)

    def finish_square(k):
        other = (slot + k + 1) % (2 * groups)
        wait_sent(squares.at[slot], square_sent.at[other], me, core)

    over(2 * groups - 1, finish_square)
    wait_sent(away, pair_sems.at[0], me, core)
    wait_sent(position_own, pair_sems.at[2], me, core)


def return_rows(d_rows, flat, reqs, grads, small, held, groups):
    width = d_rows.shape[1]
    entries = flat.shape[1]
    grad_in, grad_out, grad_up, grad_down, grad_position = grads
    rows = (grad_in.size + grad_out.size + grad_up.size + grad_down.size) // width
    rows = rows + grad_position.shape[0]
    length = -(-rows // groups // 16) * 16
    if length * groups < rows:
        length = length + 16
    return pl.pallas_call(
        functools.partial(return_kernel, groups),
        out_shape=(
            jax.ShapeDtypeStruct((held, width), WIDE),
            jax.ShapeDtypeStruct((groups * length, width), LOWF),
            jax.ShapeDtypeStruct((2 * grad_position.shape[0], width), LOWF),
            jax.ShapeDtypeStruct(small.shape, WIDE),
            jax.ShapeDtypeStruct((8, TILE), WIDE),
        ),
        in_specs=[VMEM] * 9,
        out_specs=(VMEM,) * 5,
        scratch_shapes=[
            pltpu.VMEM((groups * length, width), LOWF),
            pltpu.VMEM((groups * length, width), LOWF),
            pltpu.VMEM((length, width), WIDE),
            pltpu.VMEM((groups * length, width), LOWF),
            pltpu.VMEM((entries, width), LOWF),
            pltpu.VMEM((entries, width), LOWF),
            pltpu.VMEM((2 * held, width), WIDE),
            pltpu.VMEM((held, width), WIDE),
            pltpu.VMEM((groups, *small.shape), WIDE),
            pltpu.VMEM((2 * groups, 8, TILE), WIDE),
            pltpu.VMEM(grad_position.shape, LOWF),
            DMA((groups,)),
            DMA((groups,)),
            DMA((groups,)),
            DMA((groups,)),
            DMA((groups,)),
            DMA((groups,)),
            DMA((groups,)),
            DMA((groups,)),
            DMA((2 * groups,)),
            DMA((2 * groups,)),
            DMA((4,)),
        ],
        compiler_params=pltpu.CompilerParams(
            collective_id=1, has_side_effects=True, vmem_limit_bytes=REST
        ),
    )(d_rows, flat, reqs, grad_in, grad_out, grad_up, grad_down, grad_position, small)


NN = (((1,), (0,)), ((), ()))
NT = (((1,), (1,)), ((), ()))
TN = (((0,), (0,)), ((), ()))
LOWEST = -1e30
REACH = 4
LEVELS = 32


def matmul(left, right, dims=NN):
    return lax.dot_general(left, right, dims, preferred_element_type=WIDE)


def spread_rows(value):
    centred = value - jnp.mean(value, -1, keepdims=True)
    inverse = lax.rsqrt(jnp.mean(centred * centred, -1, keepdims=True) + EPSILON)
    return centred * inverse, inverse


def spread_back(unit, inverse, gain, grad):
    d_unit = grad * gain
    return inverse * (
        d_unit
        - jnp.mean(d_unit, -1, keepdims=True)
        - unit * jnp.mean(d_unit * unit, -1, keepdims=True)
    )


def windows(slots):
    found, at = [], 0
    for block in range(slots // TILE):
        low = max(0, block - REACH) * TILE
        width = (block + 1) * TILE - low
        found.append((block, low, width, at))
        at += width
    return found, at


def layer_scratch(slots, width, heads_width, hidden, places):
    own = slots // 2
    pairs = heads_width // TILE
    area = windows(slots)[1]
    blocks = slots // TILE
    return {
        "w_out": ((2, heads_width, width), LOWF),
        "w_up": ((2, width, hidden), LOWF),
        "w_down": ((2, hidden, width), LOWF),
        "w_in": ((3, width, heads_width), LOWF),
        "segments": ((slots, TILE), WIDE),
        "place": ((slots, TILE), WIDE),
        "bias": ((area, TILE), WIDE),
        "pos_high": ((places, width), LOWF),
        "pos_low": ((places, width), LOWF),
        "first": ((slots, width), WIDE),
        "normed": ((slots, width), LOWF),
        "normed_t": ((width, slots), LOWF),
        "queries": ((pairs, blocks, 2 * TILE, TILE), LOWF),
        "keys": ((pairs, slots, TILE), LOWF),
        "values": ((pairs, slots, TILE), LOWF),
        "keys_t": ((pairs, TILE, slots), LOWF),
        "values_t": ((pairs, TILE, slots), LOWF),
        "probs": ((pairs, area, 2 * TILE), WIDE),
        "mixed": ((pairs, slots, TILE), LOWF),
        "mixed_in": ((pairs, own, TILE), LOWF),
        "joined": ((2, own, heads_width), LOWF),
        "unit_one": ((own, width), WIDE),
        "inverse_one": ((own, TILE), WIDE),
        "lifted": ((own, width), LOWF),
        "hidden": ((2, own, hidden), LOWF),
        "slope": ((2, own, hidden), WIDE),
        "unit_two": ((own, width), WIDE),
        "inverse_two": ((own, TILE), WIDE),
        "final": ((own, width), LOWF),
        "logit_bias": ((1, slots), WIDE),
        "d_logits": ((own, slots), LOWF),
        "d_third": ((own, width), WIDE),
        "d_branch": ((own, width), LOWF),
        "d_inner": ((2, own, hidden), LOWF),
        "d_second": ((own, width), WIDE),
        "d_mixed": ((own, width), LOWF),
        "d_heads": ((pairs, slots, TILE), LOWF),
        "d_heads_out": ((pairs, own, TILE), LOWF),
        "d_cand": ((slots, width), WIDE),
        "d_cand_in": ((slots, width), WIDE),
        "g_out": ((2, heads_width, width), WIDE),
        "g_up": ((2, width, hidden), WIDE),
        "g_down": ((2, hidden, width), WIDE),
        "g_out_in": ((heads_width, width), WIDE),
        "g_up_in": ((width, hidden), WIDE),
        "g_down_in": ((hidden, width), WIDE),
        "d_keys": ((pairs, slots, TILE), WIDE),
        "d_values": ((pairs, slots, TILE), WIDE),
        "d_triple": ((3, slots, heads_width), LOWF),
        "d_normed": ((slots, width), WIDE),
        "d_normed_in": ((own, width), WIDE),
        "d_first": ((slots, width), LOWF),
        "few": ((8, width), WIDE),
        "few_in": ((8, width), WIDE),
    }


LINKS = 16


def layer_kernel(names, *refs):
    (rows_ref, seg_ref, live_ref, logq_ref, in_ref, out_ref, up_ref, down_ref, pos_ref, gain_ref) = refs[:10]
    (rows_out, gin_ref, gout_ref, gup_ref, gdown_ref, gpos_ref, few_ref) = refs[10:17]
    s = types.SimpleNamespace(**dict(zip(names, refs[17:])))
    sent, came = refs[-2:]
    me, core = lax.axis_index("dp"), lax.axis_index("ffn")
    other = 1 - core
    slots, width = s.first.shape
    own = slots // 2
    pairs = s.keys.shape[0]
    hidden = s.w_up.shape[2]
    places = pos_ref.shape[0]
    mine = pl.ds(pl.multiple_of(core * own, own), own)
    yours = pl.ds(pl.multiple_of(other * own, own), own)
    barrier = pltpu.get_barrier_semaphore()
    pl.semaphore_signal(barrier, inc=1, device_id=(me, other), device_id_type=MESH)

    def swap(index, source, target):
        send(source, target, sent.at[index], came.at[index], (me, other))

    def swapped(index, source, target):
        wait_arrival(target, came.at[index], me, core)

    s.w_out[core] = out_ref[...].astype(LOWF)
    s.w_up[core] = up_ref[...].astype(LOWF)
    s.w_down[core] = down_ref[...].astype(LOWF)
    pl.semaphore_wait(barrier, 1)
    swap(0, s.w_out.at[core], s.w_out.at[core])
    swap(1, s.w_up.at[core], s.w_up.at[core])
    swap(2, s.w_down.at[core], s.w_down.at[core])
    for c in range(3):
        s.w_in[c] = in_ref[c].astype(LOWF)
    high = pos_ref[...].astype(LOWF)
    s.pos_high[...] = high
    s.pos_low[...] = (pos_ref[...] - high.astype(WIDE)).astype(LOWF)
    seg = seg_ref[...]
    level = tile_iota((LEVELS, slots), 0)
    starts = jnp.sum(jnp.where(seg < level, 1.0, 0.0), 1, keepdims=True)
    start = jnp.sum(jnp.where(seg == level, starts, 0.0), 0, keepdims=True)
    place_row = tile_iota((1, slots), 1) - start.astype(jnp.int32)
    eye = diagonal_of(TILE)
    ones = jnp.ones((TILE, TILE), LOWF)
    seg_wide = seg.astype(WIDE)
    for b in range(slots // TILE):
        at = slice(b * TILE, (b + 1) * TILE)
        s.segments[at, :] = as_column(seg_wide[:, at], eye, ones)
        line = place_row[:, at]
        s.place[at, :] = 8.0 * as_column(
            lax.shift_right_logical(line, 3).astype(WIDE), eye, ones
        ) + as_column((line & 7).astype(WIDE), eye, ones)
    found, _ = windows(slots)
    causal = tile_iota((TILE, TILE), 0) <= tile_iota((TILE, TILE), 1)
    for b, low, span, at in found:
        line = seg_wide[:, b * TILE : (b + 1) * TILE]
        for t in range(span // TILE):
            same = s.segments[low + t * TILE : low + (t + 1) * TILE, :] == line
            if low + t * TILE == b * TILE:
                same = same & causal
            s.bias[at + t * TILE : at + (t + 1) * TILE, :] = jnp.where(same, 0.0, LOWEST)
    live = live_ref[0]
    alive_row = tile_iota((1, slots), 1) < live
    s.logit_bias[...] = jnp.where(alive_row, -logq_ref[...], LOWEST)
    first_lanes = (tile_iota((1, TILE), 1) < HEAD).astype(WIDE)
    pick = [first_lanes.astype(LOWF), (1.0 - first_lanes).astype(LOWF)]
    gain = [gain_ref[g : g + 1, :] for g in range(3)]
    step = 2 * TILE

    def enter(r):
        at = pl.ds(pl.multiple_of(r * step, step), step)
        where = s.place[at, :]
        lane = tile_iota((step, TILE), 1).astype(WIDE)
        hot = jnp.concatenate(
            [one_hot(where == lane + float(t * TILE)) for t in range(places // TILE)], 1
        )
        first = (
            rows_ref[at, :].astype(WIDE)
            + matmul(hot, s.pos_high[...])
            + matmul(hot, s.pos_low[...])
        )
        s.first[at, :] = first
        normed = (spread_rows(first)[0] * gain[0]).astype(LOWF)
        s.normed[at, :] = normed
        s.normed_t[:, at] = normed.astype(WIDE).T.astype(LOWF)
        query = (matmul(normed, s.w_in[0]) * SCALE).astype(LOWF)
        keys = matmul(normed, s.w_in[1]).astype(LOWF)
        values = matmul(normed, s.w_in[2]).astype(LOWF)
        keys_t = keys.astype(WIDE).T.astype(LOWF)
        values_t = values.astype(WIDE).T.astype(LOWF)
        for hp in range(pairs):
            lanes = slice(hp * TILE, (hp + 1) * TILE)
            s.keys[hp, at, :] = keys[:, lanes]
            s.values[hp, at, :] = values[:, lanes]
            s.keys_t[hp, :, at] = keys_t[lanes, :]
            s.values_t[hp, :, at] = values_t[lanes, :]
            for i in range(step // TILE):
                part = query[i * TILE : (i + 1) * TILE, lanes]
                for h in range(2):
                    s.queries[hp, r * (step // TILE) + i, h * TILE : (h + 1) * TILE, :] = (
                        part * pick[h]
                    )

    over(slots // step, enter)

    def attend(hp):
        for b, low, span, at in found:
            scores = matmul(s.keys[hp, low : low + span, :], s.queries[hp, b], NT)
            bias = s.bias[at : at + span, :]
            scores = scores + jnp.concatenate([bias, bias], 1)
            expo = jnp.exp(scores - jnp.max(scores, 0, keepdims=True))
            prob = expo * (1.0 / jnp.sum(expo, 0, keepdims=True))
            s.probs[hp, at : at + span, :] = prob
            out = matmul(s.values_t[hp, :, low : low + span], prob.astype(LOWF))
            out = jnp.concatenate([out[:HEAD, :TILE], out[HEAD:, TILE:]], 0)
            s.mixed[hp, b * TILE : (b + 1) * TILE, :] = out.T.astype(LOWF)
        swap(3 + hp, s.mixed.at[hp, yours], s.mixed_in.at[hp])

    over(pairs, attend)
    for index, block in enumerate((s.w_out, s.w_up, s.w_down)):
        swapped(index, block.at[core], block.at[other])
    for hp in range(pairs):
        swapped(3 + hp, s.mixed.at[hp, yours], s.mixed_in.at[hp])

    def feed(r):
        at = pl.ds(pl.multiple_of(r * step, step), step)
        full = pl.ds(pl.multiple_of(core * own + r * step, step), step)
        here = jnp.concatenate([s.mixed[hp, full, :] for hp in range(pairs)], 1)
        there = jnp.concatenate([s.mixed_in[hp, at, :] for hp in range(pairs)], 1)
        s.joined[core, at, :] = here
        s.joined[other, at, :] = there
        second = s.first[full, :] + matmul(here, s.w_out[core]) + matmul(there, s.w_out[other])
        unit, inverse = spread_rows(second)
        s.unit_one[at, :] = unit
        s.inverse_one[at, :] = jnp.broadcast_to(inverse, (step, TILE))
        lifted = (unit * gain[1]).astype(LOWF)
        s.lifted[at, :] = lifted
        third = second
        for side in range(2):
            inner = matmul(lifted, s.w_up[side])
            square = inner * inner
            bend = jnp.tanh(GELU_A * inner * (1.0 + GELU_B * square))
            gate = 0.5 * (1.0 + bend)
            act = (inner * gate).astype(LOWF)
            s.hidden[side, at, :] = act
            s.slope[side, at, :] = gate + 0.5 * inner * (1.0 - bend * bend) * (
                GELU_A * (1.0 + 3.0 * GELU_B * square)
            )
            third = third + matmul(act, s.w_down[side])
        unit, inverse = spread_rows(third)
        s.unit_two[at, :] = unit
        s.inverse_two[at, :] = jnp.broadcast_to(inverse, (step, TILE))
        s.final[at, :] = (unit * gain[2]).astype(LOWF)

    over(own // step, feed)
    s.few[...] = jnp.zeros((8, width), WIDE)

    def choose(r):
        at = pl.ds(pl.multiple_of(r * TILE, TILE), TILE)
        logits = matmul(s.final[at, :], rows_ref[slots:, :], NT) + s.logit_bias[...]
        number = tile_iota((TILE, slots), 0) + (core * own + r * TILE)
        same = tile_iota((TILE, slots), 1) == number
        top = jnp.max(logits, -1, keepdims=True)
        expo = jnp.exp(logits - top)
        total = jnp.sum(expo, -1, keepdims=True)
        alive = number[:, :1] < live
        right = jnp.sum(jnp.where(same, logits, 0.0), -1, keepdims=True)
        loss = jnp.sum(jnp.where(alive, top + jnp.log(total) - right, 0.0))
        s.few[3:4, :] += jnp.full((1, width), loss, WIDE)
        alive = jnp.where(alive, 1.0, 0.0)
        grad = (expo * (alive / total) - jnp.where(same, alive, 0.0)).astype(LOWF)
        s.d_logits[at, :] = grad
        d_final = matmul(grad, rows_ref[slots:, :])
        unit = s.unit_two[at, :]
        s.few[2:3, :] += jnp.sum(d_final * unit, 0, keepdims=True)
        d_third = spread_back(unit, s.inverse_two[at, :1], gain[2], d_final)
        s.d_third[at, :] = d_third
        s.d_branch[at, :] = d_third.astype(LOWF)

    over(own // TILE, choose)
    s.d_cand[...] = matmul(s.d_logits[...], s.final[...], TN)
    swap(5, s.d_cand, s.d_cand_in)

    def feed_back(r):
        at = pl.ds(pl.multiple_of(r * step, step), step)
        full = pl.ds(pl.multiple_of(core * own + r * step, step), step)
        d_lifted = jnp.zeros((step, width), WIDE)
        for side in range(2):
            d_hidden = matmul(s.d_branch[at, :], s.w_down[side], NT)
            d_inner = (d_hidden * s.slope[side, at, :]).astype(LOWF)
            s.d_inner[side, at, :] = d_inner
            d_lifted = d_lifted + matmul(d_inner, s.w_up[side], NT)
        unit = s.unit_one[at, :]
        s.few[1:2, :] += jnp.sum(d_lifted * unit, 0, keepdims=True)
        d_second = s.d_third[at, :] + spread_back(unit, s.inverse_one[at, :1], gain[1], d_lifted)
        s.d_second[at, :] = d_second
        d_mixed = d_second.astype(LOWF)
        s.d_mixed[at, :] = d_mixed
        here = matmul(d_mixed, s.w_out[core], NT).astype(LOWF)
        there = matmul(d_mixed, s.w_out[other], NT).astype(LOWF)
        for hp in range(pairs):
            lanes = slice(hp * TILE, (hp + 1) * TILE)
            s.d_heads[hp, full, :] = here[:, lanes]
            s.d_heads_out[hp, at, :] = there[:, lanes]

    over(own // step, feed_back)
    for hp in range(pairs):
        swap(6 + hp, s.d_heads_out.at[hp], s.d_heads.at[hp, mine])
    for side in range(2):
        s.g_down[side] = matmul(s.hidden[side], s.d_branch[...], TN)
    swap(8, s.g_down.at[other], s.g_down_in)
    for side in range(2):
        s.g_up[side] = matmul(s.lifted[...], s.d_inner[side], TN)
    swap(9, s.g_up.at[other], s.g_up_in)
    for side in range(2):
        s.g_out[side] = matmul(s.joined[side], s.d_mixed[...], TN)
    swap(10, s.g_out.at[other], s.g_out_in)
    s.d_keys[...] = jnp.zeros(s.d_keys.shape, WIDE)
    s.d_values[...] = jnp.zeros(s.d_values.shape, WIDE)
    for hp in range(pairs):
        swapped(6 + hp, s.d_heads_out.at[hp], s.d_heads.at[hp, yours])

    def attend_back(hp):
        for b, low, span, at in found:
            d_block = s.d_heads[hp, b * TILE : (b + 1) * TILE, :]
            d_pair = jnp.concatenate([d_block * pick[0], d_block * pick[1]], 0)
            d_prob = matmul(s.values[hp, low : low + span, :], d_pair, NT)
            prob = s.probs[hp, at : at + span, :]
            mean = jnp.sum(prob * d_prob, 0, keepdims=True)
            d_scores = (prob * (d_prob - mean)).astype(LOWF)
            s.d_keys[hp, low : low + span, :] += matmul(d_scores, s.queries[hp, b])
            s.d_values[hp, low : low + span, :] += matmul(prob.astype(LOWF), d_pair)
            out = matmul(s.keys_t[hp, :, low : low + span], d_scores)
            out = jnp.concatenate([out[:HEAD, :TILE], out[HEAD:, TILE:]], 0) * SCALE
            lanes = pl.ds(pl.multiple_of(hp * TILE, TILE), TILE)
            s.d_triple[0, b * TILE : (b + 1) * TILE, lanes] = out.T.astype(LOWF)

    over(pairs, attend_back)
    for hp in range(pairs):
        lanes = slice(hp * TILE, (hp + 1) * TILE)
        s.d_triple[1, :, lanes] = s.d_keys[hp].astype(LOWF)
        s.d_triple[2, :, lanes] = s.d_values[hp].astype(LOWF)
    for side in (yours, mine):
        d_normed = matmul(s.d_triple[0, side, :], s.w_in[0], NT)
        for c in range(1, 3):
            d_normed = d_normed + matmul(s.d_triple[c, side, :], s.w_in[c], NT)
        s.d_normed[side, :] = d_normed
        if side is yours:
            swap(11, s.d_normed.at[yours], s.d_normed_in)
    for c in range(3):
        gin_ref[c] = matmul(s.normed_t[...], s.d_triple[c])
    swapped(11, s.d_normed.at[yours], s.d_normed_in)
    d_normed = s.d_normed[mine, :] + s.d_normed_in[...]
    unit, inverse = spread_rows(s.first[mine, :])
    s.few[0:1, :] = jnp.sum(d_normed * unit, 0, keepdims=True)
    d_first = s.d_second[...] + spread_back(unit, inverse, gain[0], d_normed)
    s.d_first[mine, :] = d_first.astype(LOWF)
    swap(12, s.d_first.at[mine], s.d_first.at[mine])
    s.few[4:5, :] = jnp.full((1, width), 0.5 * live.astype(WIDE), WIDE)
    swap(13, s.few, s.few_in)
    swapped(5, s.d_cand, s.d_cand_in)
    rows_out[slots:, :] = (s.d_cand[...] + s.d_cand_in[...]).astype(LOWF)
    swapped(8, s.g_down.at[other], s.g_down_in)
    gdown_ref[...] = s.g_down[core] + s.g_down_in[...]
    swapped(9, s.g_up.at[other], s.g_up_in)
    gup_ref[...] = s.g_up[core] + s.g_up_in[...]
    swapped(10, s.g_out.at[other], s.g_out_in)
    gout_ref[...] = s.g_out[core] + s.g_out_in[...]
    swapped(12, s.d_first.at[mine], s.d_first.at[yours])
    rows_out[:slots, :] = s.d_first[...]
    place_half = gpos_ref.shape[0]
    hot = one_hot(tile_iota((place_half, slots), 0) + core * place_half == place_row)
    gpos_ref[...] = matmul(hot, s.d_first[...])
    swapped(13, s.few, s.few_in)
    few_ref[...] = s.few[...] + s.few_in[...]
    for index, block in enumerate((s.w_out, s.w_up, s.w_down)):
        wait_sent(block.at[core], sent.at[index], me, core)
    for hp in range(pairs):
        wait_sent(s.mixed.at[hp, yours], sent.at[3 + hp], me, core)
        wait_sent(s.d_heads_out.at[hp], sent.at[6 + hp], me, core)
    wait_sent(s.d_cand, sent.at[5], me, core)
    wait_sent(s.g_down.at[other], sent.at[8], me, core)
    wait_sent(s.g_up.at[other], sent.at[9], me, core)
    wait_sent(s.g_out.at[other], sent.at[10], me, core)
    wait_sent(s.d_normed.at[yours], sent.at[11], me, core)
    wait_sent(s.d_first.at[mine], sent.at[12], me, core)
    wait_sent(s.few, sent.at[13], me, core)


def run_layer(rows, segment, live, logq, attn_in, attn_out, ffn_up, ffn_down, position_table, norm_gains):
    slots, width = segment.shape[1], rows.shape[1]
    scratch = layer_scratch(
        slots, width, attn_out.shape[0], ffn_up.shape[1], position_table.shape[0]
    )
    shape = jax.ShapeDtypeStruct
    return pl.pallas_call(
        functools.partial(layer_kernel, tuple(scratch)),
        out_shape=(
            shape(rows.shape, LOWF),
            shape(attn_in.shape, WIDE),
            shape(attn_out.shape, WIDE),
            shape(ffn_up.shape, WIDE),
            shape(ffn_down.shape, WIDE),
            shape((position_table.shape[0] // 2, width), WIDE),
            shape((8, width), WIDE),
        ),
        in_specs=[VMEM] * 2 + [pl.BlockSpec(memory_space=pltpu.SMEM)] + [VMEM] * 7,
        out_specs=(VMEM,) * 7,
        scratch_shapes=[pltpu.VMEM(*entry) for entry in scratch.values()]
        + [DMA((LINKS,)), DMA((LINKS,))],
        compiler_params=pltpu.CompilerParams(
            collective_id=2, has_side_effects=True, vmem_limit_bytes=58 * 1024 * 1024
        ),
    )(rows, segment, live, logq, attn_in, attn_out, ffn_up, ffn_down, position_table, norm_gains)


def adamw(weight, grad, first, second, decay, rate):
    first = BETA_ONE * first + (1.0 - BETA_ONE) * grad
    second = BETA_TWO * second + (1.0 - BETA_TWO) * grad * grad
    moved = first / (1.0 - BETA_ONE**STEP) / (jnp.sqrt(second / (1.0 - BETA_TWO**STEP)) + ADAM_EPS)
    return (weight - rate * (moved + decay * weight), first, second)


def body(
    item_table,
    attn_in,
    attn_out,
    ffn_up,
    ffn_down,
    position_table,
    norm_gains,
    item_first,
    item_second,
    attn_in_first,
    attn_in_second,
    attn_out_first,
    attn_out_second,
    ffn_up_first,
    ffn_up_second,
    ffn_down_first,
    ffn_down_second,
    position_first,
    position_second,
    gains_first,
    gains_second,
    owner_group,
    row_offset,
    segment_ids,
    live_slots,
    log_freq,
):
    groups = lax.axis_size("dp")
    owners = owner_group.reshape(1, -1)
    offsets = row_offset.reshape(1, -1)
    rows, flat, reqs = fetch_rows(item_table, owners, offsets, groups)
    d_rows, *grads, few = run_layer(
        rows,
        segment_ids,
        live_slots,
        log_freq,
        attn_in,
        attn_out,
        ffn_up,
        ffn_down,
        position_table,
        norm_gains,
    )
    held, width = item_table.shape
    grad_table, shared, grad_position, few, stats = return_rows(
        d_rows, flat, reqs, grads, few, held, groups
    )
    shared = shared.astype(WIDE)
    grad_position = grad_position.astype(WIDE)
    last = 3 * width
    grad_in = shared[:last].reshape(attn_in.shape)
    grad_out = shared[last : last + attn_out.shape[0]]
    last = last + attn_out.shape[0]
    grad_up = jnp.concatenate([shared[last : last + width], shared[last + width : last + 2 * width]], 1)
    last = last + 2 * width
    grad_down = shared[last : last + ffn_down.shape[0]]
    grad_gains = few[:3]
    loss_sum, live_count = few[3, 0], few[4, 0]
    grad_norm = jnp.sqrt(stats[0, 0] + jnp.sum(grad_gains * grad_gains))
    factor = CLIP / jnp.maximum(grad_norm, CLIP)
    table_new = adamw(item_table, grad_table * factor, item_first, item_second, DECAY, RATE)
    in_new = adamw(attn_in, grad_in * factor, attn_in_first, attn_in_second, DECAY, RATE)
    out_new = adamw(attn_out, grad_out * factor, attn_out_first, attn_out_second, DECAY, RATE)
    up_new = adamw(ffn_up, grad_up * factor, ffn_up_first, ffn_up_second, DECAY, RATE)
    down_new = adamw(ffn_down, grad_down * factor, ffn_down_first, ffn_down_second, DECAY, RATE)
    position_new = adamw(
        position_table,
        grad_position * factor,
        position_first,
        position_second,
        DECAY,
        RATE_POSITION,
    )
    gains_new = adamw(norm_gains, grad_gains * factor, gains_first, gains_second, 0.0, RATE_GAINS)
    return (
        table_new[0],
        table_new[1],
        table_new[2],
        in_new[0],
        in_new[1],
        in_new[2],
        out_new[0],
        out_new[1],
        out_new[2],
        up_new[0],
        up_new[1],
        up_new[2],
        down_new[0],
        down_new[1],
        down_new[2],
        position_new[0],
        position_new[1],
        position_new[2],
        gains_new[0],
        gains_new[1],
        gains_new[2],
        loss_sum,
        live_count,
        grad_norm,
    )


def solution(mesh):
    return jax.shard_map(
        body,
        mesh=mesh,
        in_specs=(
            P(("dp", "ffn"), None),
            P(None, None, "ffn"),
            P("ffn", None),
            P(None, "ffn"),
            P("ffn", None),
            P(),
            P(),
            P(("dp", "ffn"), None),
            P(("dp", "ffn"), None),
            P(None, None, "ffn"),
            P(None, None, "ffn"),
            P("ffn", None),
            P("ffn", None),
            P(None, "ffn"),
            P(None, "ffn"),
            P("ffn", None),
            P("ffn", None),
            P(),
            P(),
            P(),
            P(),
            P("dp", None, None),
            P("dp", None),
            P("dp", None),
            P("dp"),
            P("dp", None),
        ),
        out_specs=(
            P(("dp", "ffn"), None),
            P(("dp", "ffn"), None),
            P(("dp", "ffn"), None),
            P(None, None, "ffn"),
            P(None, None, "ffn"),
            P(None, None, "ffn"),
            P("ffn", None),
            P("ffn", None),
            P("ffn", None),
            P(None, "ffn"),
            P(None, "ffn"),
            P(None, "ffn"),
            P("ffn", None),
            P("ffn", None),
            P("ffn", None),
            P(),
            P(),
            P(),
            P(),
            P(),
            P(),
            P(),
            P(),
            P(),
        ),
        check_vma=False,
    )
```

```python
import functools
import types

import jax
import jax.numpy as jnp
from jax import lax
from jax.experimental import pallas as pl
from jax.experimental.pallas import tpu as pltpu
from jax.sharding import PartitionSpec as P

HEAD = 64
STEP = 10
EPSILON = 1e-05
SCALE = 0.125
CLIP = 1.0
RATE = 0.05
RATE_POSITION = 0.3
RATE_GAINS = 0.5
DECAY = 0.01
BETA_ONE = 0.9
BETA_TWO = 0.999
ADAM_EPS = 1e-08
GELU_A = 0.7978845608028654
GELU_B = 0.044715
LOWF = jnp.bfloat16
WIDE = jnp.float32
MESH = pl.DeviceIdType.MESH
DMA = pltpu.SemaphoreType.DMA
VMEM = pl.BlockSpec(memory_space=pltpu.VMEM)
SMEM = pl.BlockSpec(memory_space=pltpu.SMEM)
FAR = pl.BlockSpec(memory_space=pltpu.HBM)
TILE = 128
GROUP = 256
NN = (((1,), (0,)), ((), ()))
NT = (((1,), (1,)), ((), ()))
TN = (((0,), (0,)), ((), ()))
LOWEST = -1e30
REACH = 4
LEVELS = 32
LINKS = 24


def tile_iota(shape, axis):
    return lax.broadcasted_iota(jnp.int32, shape, axis)


def matmul(left, right, dims=NN):
    return lax.dot_general(left, right, dims, preferred_element_type=WIDE)


def as_column(row, eye, ones):
    return matmul((eye * row).astype(LOWF), ones)


def one_hot(condition):
    return jnp.where(condition, 1.0, 0.0).astype(LOWF)


def span(start, size, unit=16):
    return pl.ds(pl.multiple_of(start, unit), size)


def over(count, step):
    def run(index, carry):
        step(index)
        return carry

    lax.fori_loop(0, count, run, 0)


def flipped(value, mask, bits=4):
    total = 0
    for bit in range(bits):
        one, two = (value // 2**bit) % 2, (mask // 2**bit) % 2
        total = total + (one + two - 2 * one * two) * 2**bit
    return total


def copy_to(source, target, send_sem, recv_sem, where):
    return pltpu.make_async_remote_copy(
        src_ref=source,
        dst_ref=target,
        send_sem=send_sem,
        recv_sem=recv_sem,
        device_id=where,
        device_id_type=MESH,
    )


def send(source, target, send_sem, recv_sem, where):
    copy_to(source, target, send_sem, recv_sem, where).start()


def spread_rows(value):
    centred = value - jnp.mean(value, -1, keepdims=True)
    inverse = lax.rsqrt(jnp.mean(centred * centred, -1, keepdims=True) + EPSILON)
    return centred * inverse, inverse


def spread_back(unit, inverse, gain, grad):
    d_unit = grad * gain
    return inverse * (
        d_unit
        - jnp.mean(d_unit, -1, keepdims=True)
        - unit * jnp.mean(d_unit * unit, -1, keepdims=True)
    )


def windows(slots):
    found, at = [], 0
    for block in range(slots // TILE):
        low = max(0, block - REACH) * TILE
        width = (block + 1) * TILE - low
        found.append((block, low, width, at))
        at += width
    return found, at


def levels_of(groups):
    inner = 4 if groups % 4 == 0 else 1
    return inner, groups // inner


def shard_rows(rows, groups):
    return -(-rows // (groups * 16)) * 16


def part_scratch(name, rows, width, groups):
    inner, outer = levels_of(groups)
    shard = shard_rows(rows, groups)
    return {
        name + "_source": pltpu.VMEM((groups * shard, width), LOWF),
        name + "_plane": pltpu.VMEM((inner, outer * shard, width), LOWF),
        name + "_half": pltpu.VMEM((outer * shard, width), LOWF),
        name + "_column": pltpu.VMEM((outer, shard, width), LOWF),
        name + "_shard": pltpu.VMEM((shard, width), WIDE),
        name + "_plane_sent": DMA((inner,)),
        name + "_plane_came": DMA((inner,)),
        name + "_column_sent": DMA((outer,)),
        name + "_column_came": DMA((outer,)),
        name + "_out_sent": DMA((outer,)),
        name + "_ahead_sent": DMA((groups,)),
        name + "_came": DMA((groups,)),
    }


class Part:
    def __init__(self, scratch, name, whole, groups, me, core):
        for key, ref in vars(scratch).items():
            if key.startswith(name + "_"):
                setattr(self, key[len(name) + 1 :], ref)
        self.whole, self.me, self.core = whole, me, core
        self.inner, self.outer = levels_of(groups)
        self.i, self.o = me % self.inner, me // self.inner
        self.size = self.shard.shape[0]

    def quarter(self, j):
        return span(j * self.outer * self.size, self.outer * self.size)

    def piece(self, j, o):
        return span((j * self.outer + o) * self.size, self.size)

    def plane_copy(self, j):
        return copy_to(
            self.source.at[self.quarter(j)],
            self.plane.at[self.i],
            self.plane_sent.at[j],
            self.plane_came.at[self.i],
            (self.o * self.inner + j, self.core),
        )

    def column_copy(self, o):
        return copy_to(
            self.half.at[span(o * self.size, self.size)],
            self.column.at[self.o],
            self.column_sent.at[o],
            self.column_came.at[self.o],
            (o * self.inner + self.i, self.core),
        )

    def out_copy(self, o):
        block = self.whole.at[self.piece(self.i, self.o)]
        came = self.came.at[self.i * self.outer + self.o]
        return copy_to(block, block, self.out_sent.at[o], came, (o * self.inner + self.i, self.core))

    def ahead_copy(self, o, j):
        block = self.whole.at[self.piece(self.i, o)]
        came = self.came.at[self.i * self.outer + o]
        sent = self.ahead_sent.at[j * self.outer + o]
        return copy_to(block, block, sent, came, (self.o * self.inner + j, self.core))

    def wait(self, ref, semaphore):
        copy_to(ref, ref, semaphore, semaphore, (self.me, self.core)).wait_recv()

    def start(self):
        over(self.inner - 1, lambda k: self.plane_copy((self.i + k + 1) % self.inner).start())

    def across(self):
        total = self.source[self.quarter(self.i), :].astype(WIDE)
        for k in range(self.inner - 1):
            j = (self.i + k + 1) % self.inner
            self.wait(self.plane.at[j], self.plane_came.at[j])
            total = total + self.plane[j].astype(WIDE)
        self.half[...] = total.astype(LOWF)
        over(self.outer - 1, lambda k: self.column_copy((self.o + k + 1) % self.outer).start())

    def settle(self):
        self.shard[...] = self.half[span(self.o * self.size, self.size), :].astype(WIDE)

        def take(k):
            o = (self.o + k + 1) % self.outer
            self.wait(self.column.at[o], self.column_came.at[o])
            self.shard[...] += self.column[o].astype(WIDE)

        over(self.outer - 1, take)
        self.whole[self.piece(self.i, self.o), :] = self.shard[...].astype(LOWF)
        over(self.outer - 1, lambda k: self.out_copy((self.o + k + 1) % self.outer).start())
        self.pass_on(self.o)

    def pass_on(self, o):
        over(self.inner - 1, lambda k: self.ahead_copy(o, (self.i + k + 1) % self.inner).start())

    def forward(self):
        def step(k):
            o = (self.o + k + 1) % self.outer
            block = self.whole.at[self.piece(self.i, o)]
            self.wait(block, self.came.at[self.i * self.outer + o])
            self.pass_on(o)

        over(self.outer - 1, step)

    def collect(self):
        def step(k):
            j = (self.i + k // self.outer + 1) % self.inner
            o = k % self.outer
            block = self.whole.at[self.piece(j, o)]
            self.wait(block, self.came.at[j * self.outer + o])

        over((self.inner - 1) * self.outer, step)

    def drain(self):
        over(self.inner - 1, lambda k: self.plane_copy((self.i + k + 1) % self.inner).wait_send())

        def far(k):
            o = (self.o + k + 1) % self.outer
            self.column_copy(o).wait_send()
            self.out_copy(o).wait_send()

        over(self.outer - 1, far)

        def near(k):
            j = (self.i + k // self.outer + 1) % self.inner
            self.ahead_copy(k % self.outer, j).wait_send()

        over((self.inner - 1) * self.outer, near)


def step_scratch(groups, held, entries, width, heads_width, hidden, places):
    slots = entries // 2
    own = slots // 2
    pairs = heads_width // TILE
    area = windows(slots)[1]
    blocks = slots // TILE
    padded = -(-2 * held // TILE) * TILE
    shapes = {
        "table": ((padded, width), LOWF),
        "flat": ((1, entries), jnp.int32),
        "column": ((slots, TILE), WIDE),
        "want": ((groups, 8, TILE), jnp.int32),
        "asked": ((groups, 8, TILE), jnp.int32),
        "reqs": ((2, entries // TILE, TILE), jnp.int32),
        "leaving": ((entries, width), LOWF),
        "arrived": ((2, entries, width), LOWF),
        "cands": ((slots, width), LOWF),
        "w_out": ((2, heads_width, width), LOWF),
        "w_up": ((2, width, hidden), LOWF),
        "w_down": ((2, hidden, width), LOWF),
        "w_in": ((3, width, heads_width), LOWF),
        "segments": ((slots, TILE), WIDE),
        "place": ((slots, TILE), WIDE),
        "place_row": ((1, slots), jnp.int32),
        "bias": ((area, TILE), WIDE),
        "pos_high": ((places, width), LOWF),
        "pos_low": ((places, width), LOWF),
        "first": ((own, width), WIDE),
        "normed": ((slots, width), LOWF),
        "normed_t": ((width, slots), LOWF),
        "queries": ((pairs, blocks, 2 * TILE, TILE), LOWF),
        "keys": ((pairs, slots, TILE), LOWF),
        "values": ((pairs, slots, TILE), LOWF),
        "keys_t": ((pairs, TILE, slots), LOWF),
        "values_t": ((pairs, TILE, slots), LOWF),
        "probs": ((pairs, area, 2 * TILE), WIDE),
        "mixed": ((pairs, slots, TILE), LOWF),
        "mixed_in": ((pairs, own, TILE), LOWF),
        "joined": ((2, own, heads_width), LOWF),
        "unit_zero": ((own, width), WIDE),
        "inverse_zero": ((own, TILE), WIDE),
        "unit_one": ((own, width), WIDE),
        "inverse_one": ((own, TILE), WIDE),
        "lifted": ((own, width), LOWF),
        "hidden": ((2, own, hidden), LOWF),
        "unit_two": ((own, width), WIDE),
        "inverse_two": ((own, TILE), WIDE),
        "final": ((own, width), LOWF),
        "logit_bias": ((1, slots), WIDE),
        "d_logits": ((own, slots), LOWF),
        "d_third": ((own, width), WIDE),
        "d_branch": ((own, width), LOWF),
        "d_inner": ((2, own, hidden), LOWF),
        "d_second": ((own, width), WIDE),
        "d_mixed": ((own, width), LOWF),
        "d_heads": ((pairs, slots, TILE), LOWF),
        "d_heads_out": ((pairs, own, TILE), LOWF),
        "d_cand": ((slots * width // TILE, TILE), WIDE),
        "g_out": ((2, heads_width, width), WIDE),
        "g_up": ((2, width, hidden), WIDE),
        "g_down": ((2, hidden, width), WIDE),
        "g_out_in": ((heads_width, width), WIDE),
        "g_up_in": ((width, hidden), WIDE),
        "g_down_in": ((hidden, width), WIDE),
        "d_keys": ((pairs, slots, TILE), WIDE),
        "d_values": ((pairs, slots, TILE), WIDE),
        "d_triple": ((3, slots, heads_width), LOWF),
        "d_normed_in": ((own, width), WIDE),
        "d_rows": ((entries, width), LOWF),
        "few": ((8, width), WIDE),
        "few_in": ((8, width), WIDE),
        "few_all": ((groups, 8, width), WIDE),
        "landed": ((2, entries, width), LOWF),
        "squares": ((2 * groups, 8, TILE), WIDE),
        "early_whole": ((groups * shard_rows(2 * hidden + heads_width, groups), width), LOWF),
        "late_whole": ((groups * shard_rows(3 * heads_width + places // 2, groups), width), LOWF),
        "other_half": ((places // 2, width), LOWF),
    }
    scratch = {name: pltpu.VMEM(*entry) for name, entry in shapes.items()}
    for name in ("want", "row", "few", "land"):
        scratch[name + "_sent"] = DMA((groups,))
        scratch[name + "_came"] = DMA((groups,))
    for name in ("pass", "hand"):
        scratch[name + "_sent"] = DMA((entries // GROUP,))
        scratch[name + "_came"] = DMA((entries // GROUP,))
    scratch["square_sent"] = DMA((2 * groups,))
    scratch["square_came"] = DMA((2 * groups,))
    scratch["sent"] = DMA((LINKS,))
    scratch["came"] = DMA((LINKS,))
    scratch["loads"] = DMA((12,))
    scratch.update(part_scratch("early", 2 * hidden + heads_width, width, groups))
    scratch.update(part_scratch("late", 3 * heads_width + places // 2, width, groups))
    return scratch


def step_kernel(groups, names, *refs):
    (table_far, in_far, out_far, up_far, down_far, pos_far) = refs[:6]
    (own_ref, off_ref, seg_ref, live_ref, logq_ref, gain_ref) = refs[6:12]
    (table_ref, early_ref, late_ref, position_ref, few_ref, stats_ref) = refs[12:18]
    s = types.SimpleNamespace(**dict(zip(names, refs[18:])))
    me, core = lax.axis_index("dp"), lax.axis_index("ffn")
    other = 1 - core
    held, width = table_far.shape
    entries = own_ref.shape[1]
    slots = entries // 2
    own = slots // 2
    half = entries // groups
    share = TILE // half
    tiles = entries // TILE
    spans = entries // GROUP
    pairs, hidden, places = s.keys.shape[0], s.w_up.shape[2], pos_far.shape[0]
    heads_width = pairs * TILE
    mine, yours = span(core * own, own), span(other * own, own)
    early = Part(s, "early", s.early_whole, groups, me, core)
    late = Part(s, "late", s.late_whole, groups, me, core)

    barrier = pltpu.get_barrier_semaphore()
    slot_of = me * 2 + core

    def greet(k):
        where = (slot_of + k + 1) % (2 * groups)
        pl.semaphore_signal(
            barrier, inc=1, device_id=(where // 2, where % 2), device_id_type=MESH
        )

    over(2 * groups - 1, greet)
    spare = s.probs.at[0]
    s.d_cand_in = s.bias.at[pl.ds(0, slots * width // TILE)]
    s.total = s.d_normed = s.probs.at[1, pl.ds(0, slots)]
    s.grad_table = spare.at[pl.ds(0, held)]
    pieces = [table_far, out_far]
    pieces += [up_far.at[:, pl.ds(c * width, width)] for c in range(hidden // width)]
    pieces += [down_far, *(in_far.at[c] for c in range(3)), pos_far]
    loads, staged, at = [], [], 0
    for index, piece in enumerate(pieces):
        near = spare.at[pl.ds(at, piece.shape[0])]
        at += piece.shape[0]
        staged.append(near)
        loads.append(pltpu.make_async_copy(piece, near, s.loads.at[index]))
    for load in loads:
        load.start()

    def swap(index, source, target):
        send(source, target, s.sent.at[index], s.came.at[index], (me, other))

    def arrived(ref, semaphore):
        copy_to(ref, ref, semaphore, semaphore, (me, core)).wait_recv()

    def departed(ref, semaphore):
        copy_to(ref, ref, semaphore, semaphore, (me, core)).wait_send()

    def swapped(index, target):
        arrived(target, s.came.at[index])

    upper = one_hot(tile_iota((GROUP, GROUP), 0) <= tile_iota((GROUP, GROUP), 1))
    group_of = tile_iota((groups, GROUP), 0)
    before = jnp.zeros((groups, 1), WIDE)
    filled = jnp.zeros((3 * groups, TILE), WIDE)
    spot = (me % share) * half - core * half
    for chunk in range(spans):
        at = slice(chunk * GROUP, (chunk + 1) * GROUP)
        owner, offset = own_ref[:, at], off_ref[:, at]
        marks = jnp.where(group_of == owner, 1.0, 0.0)
        running = matmul(marks.astype(LOWF), upper) + before
        before = running[:, GROUP - 1 :]
        ranks = (jnp.sum(marks * running, 0, keepdims=True) - 1.0).astype(jnp.int32)
        slot = owner * half + ranks
        s.flat[:, at] = jnp.where(ranks < half, slot, slot + (entries - half))
        inside = (ranks >= core * half) & (ranks < core * half + half)
        picks = one_hot(tile_iota((TILE, GROUP), 0) == jnp.where(inside, ranks + spot, -1))
        parts = jnp.concatenate(
            [
                marks * lax.shift_right_logical(offset, 6).astype(WIDE),
                marks * (offset & 63).astype(WIDE),
                marks,
            ],
            0,
        ).astype(LOWF)
        filled = filled + matmul(parts, picks, NT)
    asking = (
        64.0 * filled[:groups] + filled[groups : 2 * groups] + filled[2 * groups :]
    ).astype(jnp.int32)
    for owner in range(groups):
        s.want[owner] = jnp.broadcast_to(asking[owner : owner + 1], (8, TILE))
    s.asked[me] = s.want[me]
    pl.semaphore_wait(barrier, 2 * groups - 1)

    def ask(k):
        owner = (me + groups // 2 + k) % groups

        @pl.when(owner != me)
        def _():
            send(
                s.want.at[owner], s.asked.at[me], s.want_sent.at[owner], s.want_came.at[me], (owner, core)
            )

    over(groups, ask)
    rows_mine, rows_yours = span(core * held, held), span(other * held, held)
    loads[0].wait()
    s.table[rows_mine, :] = staged[0][...].astype(LOWF)
    s.table[2 * held :, :] = jnp.zeros((s.table.shape[0] - 2 * held, width), LOWF)
    swap(0, s.table.at[rows_mine], s.table.at[rows_mine])
    eye = (tile_iota((TILE, TILE), 0) == tile_iota((TILE, TILE), 1)).astype(WIDE)
    ones = jnp.ones((TILE, TILE), LOWF)

    def column_of(line):
        return 64.0 * as_column(lax.shift_right_logical(line, 6).astype(WIDE), eye, ones) + as_column(
            (line & 63).astype(WIDE), eye, ones
        )

    for chunk in range(slots // TILE):
        side, at = divmod(chunk * TILE, own)
        line = s.flat[:, span(side * slots + core * own + at, TILE, TILE)]
        s.column[chunk * TILE : (chunk + 1) * TILE, :] = column_of(line)
    s.total[...] = jnp.zeros(s.total.shape, WIDE)
    swapped(0, s.table.at[rows_yours])
    lanes_wide = tile_iota((TILE, TILE), 1).astype(WIDE)

    def serve(k):
        tile = flipped(me // share, tiles - 1 - k)
        line = jnp.zeros((1, TILE), jnp.int32)
        for j in range(share):
            source = tile * share + j

            @pl.when(source != me)
            def _():
                arrived(s.asked.at[source], s.want_came.at[source])

        for j in range(share):
            line = line + s.asked[tile * share + j][0:1, :]
        s.reqs[core, pl.ds(tile, 1), :] = line
        number = column_of(line)
        hot = jnp.concatenate(
            [
                one_hot(number == lanes_wide + float(b * TILE + 1))
                for b in range(s.table.shape[0] // TILE)
            ],
            1,
        )
        picked = matmul(hot, s.table[...]).astype(LOWF)
        s.leaving[span(tile * TILE, TILE), :] = picked
        into = s.arrived.at[core, span(me * half, half)]
        for j in range(share):
            source = tile * share + j
            block = s.leaving.at[span(source * half, half)]

            @pl.when(source != me)
            def _():
                send(block, into, s.row_sent.at[source], s.row_came.at[me], (source, core))

            @pl.when(source == me)
            def _():
                s.arrived[core, span(me * half, half), :] = picked[j * half : (j + 1) * half]

    over(tiles, serve)
    swap(1, s.reqs.at[core], s.reqs.at[core])

    for load in loads[1:]:
        load.wait()
    s.w_out[core] = staged[1][...].astype(LOWF)
    swap(2, s.w_out.at[core], s.w_out.at[core])
    ups = hidden // width
    for c in range(ups):
        s.w_up[core, :, c * width : (c + 1) * width] = staged[2 + c][...].astype(LOWF)
    swap(3, s.w_up.at[core], s.w_up.at[core])
    s.w_down[core] = staged[2 + ups][...].astype(LOWF)
    swap(4, s.w_down.at[core], s.w_down.at[core])
    for c in range(3):
        s.w_in[c] = staged[3 + ups + c][...].astype(LOWF)
    high = staged[-1][...].astype(LOWF)
    s.pos_high[...] = high
    s.pos_low[...] = (staged[-1][...] - high.astype(WIDE)).astype(LOWF)
    seg = seg_ref[...]
    level = tile_iota((LEVELS, slots), 0)
    starts = jnp.sum(jnp.where(seg < level, 1.0, 0.0), 1, keepdims=True)
    start = jnp.sum(jnp.where(seg == level, starts, 0.0), 0, keepdims=True)
    place_row = tile_iota((1, slots), 1) - start.astype(jnp.int32)
    s.place_row[...] = place_row
    seg_wide = seg.astype(WIDE)
    for b in range(slots // TILE):
        at = slice(b * TILE, (b + 1) * TILE)
        s.segments[at, :] = as_column(seg_wide[:, at], eye, ones)
        s.place[at, :] = column_of(place_row[:, at])
    found, _ = windows(slots)
    causal = tile_iota((TILE, TILE), 0) <= tile_iota((TILE, TILE), 1)
    for b, low, wide, at in found:
        line = seg_wide[:, b * TILE : (b + 1) * TILE]
        for t in range(wide // TILE):
            same = s.segments[low + t * TILE : low + (t + 1) * TILE, :] == line
            if low + t * TILE == b * TILE:
                same = same & causal
            s.bias[at + t * TILE : at + (t + 1) * TILE, :] = jnp.where(same, 0.0, LOWEST)
    live = live_ref[0]
    alive_row = tile_iota((1, slots), 1) < live
    s.logit_bias[...] = jnp.where(alive_row, -logq_ref[...], LOWEST)
    first_lanes = (tile_iota((1, TILE), 1) < HEAD).astype(WIDE)
    pick = [first_lanes.astype(LOWF), (1.0 - first_lanes).astype(LOWF)]
    gain = [gain_ref[g : g + 1, :] for g in range(3)]
    step = 2 * TILE

    def group_at(k):
        near = spans // 2
        turn = jnp.where(k < near // 2, k, jnp.where(k < near // 2 + near, k + near // 2, k - near))
        return flipped(me * half // GROUP, spans - 1 - turn, 3)

    def lay(side, group):
        came = s.arrived[side, span(group * GROUP, GROUP), :]
        base = (side * entries + group * GROUP).astype(WIDE)
        lane = tile_iota((GROUP, TILE), 1).astype(WIDE)

        def block(b):
            at = span(b * GROUP, GROUP)
            where = s.column[at, :] - base
            hot = jnp.concatenate([one_hot(where == lane), one_hot(where == lane + float(TILE))], 1)
            s.total[at, :] += matmul(hot, came)

        over(slots // GROUP, block)

    def take(k, buffer, came, sent_on, passed, use):
        group = group_at(k)
        for j in range(GROUP // half):
            owner = group * (GROUP // half) + j

            @pl.when(owner != me)
            def _():
                arrived(buffer.at[core, span(owner * half, half)], came.at[owner])

        block = buffer.at[core, span(group * GROUP, GROUP)]
        send(block, block, sent_on.at[group], passed.at[group], (me, other))
        use(core, group)

        @pl.when(k > 0)
        def _():
            last = group_at(k - 1)
            arrived(buffer.at[other, span(last * GROUP, GROUP)], passed.at[last])
            use(other, last)

    def take_all(buffer, came, sent_on, passed, use, between=None):
        def run(k):
            take(k, buffer, came, sent_on, passed, use)
            if between is not None:
                between(k)

        over(spans, run)
        last = group_at(jnp.int32(spans - 1))
        arrived(buffer.at[other, span(last * GROUP, GROUP)], passed.at[last])
        use(other, last)

    take_all(s.arrived, s.row_came, s.pass_sent, s.pass_came, lay)
    s.cands[mine, :] = s.total[own:, :].astype(LOWF)
    swap(5, s.cands.at[mine], s.cands.at[mine])

    def enter(r):
        at = span(r * step, step)
        full = span(core * own + r * step, step, TILE)
        where = s.place[full, :]
        lane = tile_iota((step, TILE), 1).astype(WIDE)
        hot = jnp.concatenate(
            [one_hot(where == lane + float(t * TILE)) for t in range(places // TILE)], 1
        )
        first = s.total[at, :] + matmul(hot, s.pos_high[...]) + matmul(hot, s.pos_low[...])
        s.first[at, :] = first
        unit, inverse = spread_rows(first)
        s.unit_zero[at, :] = unit
        s.inverse_zero[at, :] = jnp.broadcast_to(inverse, (step, TILE))
        s.normed[full, :] = (unit * gain[0]).astype(LOWF)

    over(own // step, enter)
    swap(6, s.normed.at[mine], s.normed.at[mine])

    def project(k):
        @pl.when(k == own // step)
        def _():
            swapped(6, s.normed.at[yours])

        block = (core * (own // step) + k) % (slots // step)
        full = span(block * step, step, TILE)
        normed = s.normed[full, :]
        s.normed_t[:, full] = normed.astype(WIDE).T.astype(LOWF)
        query = (matmul(normed, s.w_in[0]) * SCALE).astype(LOWF)
        keys = matmul(normed, s.w_in[1]).astype(LOWF)
        values = matmul(normed, s.w_in[2]).astype(LOWF)
        keys_t = keys.astype(WIDE).T.astype(LOWF)
        values_t = values.astype(WIDE).T.astype(LOWF)
        for hp in range(pairs):
            lanes = slice(hp * TILE, (hp + 1) * TILE)
            s.keys[hp, full, :] = keys[:, lanes]
            s.values[hp, full, :] = values[:, lanes]
            s.keys_t[hp, :, full] = keys_t[lanes, :]
            s.values_t[hp, :, full] = values_t[lanes, :]
            for i in range(step // TILE):
                part = query[i * TILE : (i + 1) * TILE, lanes]
                for h in range(2):
                    s.queries[hp, block * (step // TILE) + i, h * TILE : (h + 1) * TILE, :] = (
                        part * pick[h]
                    )

    over(slots // step, project)

    def attend(hp):
        for b, low, wide, at in found:
            scores = matmul(s.keys[hp, low : low + wide, :], s.queries[hp, b], NT)
            bias = s.bias[at : at + wide, :]
            scores = scores + jnp.concatenate([bias, bias], 1)
            expo = jnp.exp(scores - jnp.max(scores, 0, keepdims=True))
            prob = expo * (1.0 / jnp.sum(expo, 0, keepdims=True))
            s.probs[hp, at : at + wide, :] = prob
            out = matmul(s.values_t[hp, :, low : low + wide], prob.astype(LOWF))
            out = jnp.concatenate([out[:HEAD, :TILE], out[HEAD:, TILE:]], 0)
            s.mixed[hp, b * TILE : (b + 1) * TILE, :] = out.T.astype(LOWF)
        swap(7 + hp, s.mixed.at[hp, yours], s.mixed_in.at[hp])

    over(pairs, attend)
    for index, block in enumerate((s.w_out, s.w_up, s.w_down)):
        swapped(2 + index, block.at[other])
    for hp in range(pairs):
        swapped(7 + hp, s.mixed_in.at[hp])

    def slopes(side, q, r):
        buffer = (s.d_keys, s.d_values)[side]
        fold = slots // own
        return buffer.at[q // fold, span(q % fold * own + r * step, step)]

    def feed(r):
        at = span(r * step, step)
        full = span(core * own + r * step, step, TILE)
        here = jnp.concatenate([s.mixed[hp, full, :] for hp in range(pairs)], 1)
        there = jnp.concatenate([s.mixed_in[hp, at, :] for hp in range(pairs)], 1)
        s.joined[core, at, :] = here
        s.joined[other, at, :] = there
        second = s.first[at, :] + matmul(here, s.w_out[core]) + matmul(there, s.w_out[other])
        unit, inverse = spread_rows(second)
        s.unit_one[at, :] = unit
        s.inverse_one[at, :] = jnp.broadcast_to(inverse, (step, TILE))
        lifted = (unit * gain[1]).astype(LOWF)
        s.lifted[at, :] = lifted
        third = second
        for side in range(2):
            inner = matmul(lifted, s.w_up[side])
            square = inner * inner
            bend = jnp.tanh(GELU_A * inner * (1.0 + GELU_B * square))
            gate = 0.5 * (1.0 + bend)
            act = (inner * gate).astype(LOWF)
            s.hidden[side, at, :] = act
            slope = gate + 0.5 * inner * (1.0 - bend * bend) * (
                GELU_A * (1.0 + 3.0 * GELU_B * square)
            )
            for q in range(hidden // TILE):
                slopes(side, q, r)[...] = slope[:, q * TILE : (q + 1) * TILE]
            third = third + matmul(act, s.w_down[side])
        unit, inverse = spread_rows(third)
        s.unit_two[at, :] = unit
        s.inverse_two[at, :] = jnp.broadcast_to(inverse, (step, TILE))
        s.final[at, :] = (unit * gain[2]).astype(LOWF)

    over(own // step, feed)
    s.few[...] = jnp.zeros((8, width), WIDE)
    swapped(5, s.cands.at[yours])

    def choose(r):
        at = span(r * TILE, TILE)
        logits = matmul(s.final[at, :], s.cands[...], NT) + s.logit_bias[...]
        number = tile_iota((TILE, slots), 0) + (core * own + r * TILE)
        same = tile_iota((TILE, slots), 1) == number
        top = jnp.max(logits, -1, keepdims=True)
        expo = jnp.exp(logits - top)
        total = jnp.sum(expo, -1, keepdims=True)
        alive = number[:, :1] < live
        right = jnp.sum(jnp.where(same, logits, 0.0), -1, keepdims=True)
        loss = jnp.sum(jnp.where(alive, top + jnp.log(total) - right, 0.0))
        s.few[3:4, :] += jnp.full((1, width), loss, WIDE)
        alive = jnp.where(alive, 1.0, 0.0)
        grad = (expo * (alive / total) - jnp.where(same, alive, 0.0)).astype(LOWF)
        s.d_logits[at, :] = grad
        d_final = matmul(grad, s.cands[...])
        unit = s.unit_two[at, :]
        s.few[2:3, :] += jnp.sum(d_final * unit, 0, keepdims=True)
        d_third = spread_back(unit, s.inverse_two[at, :1], gain[2], d_final)
        s.d_third[at, :] = d_third
        s.d_branch[at, :] = d_third.astype(LOWF)

    over(own // TILE, choose)

    def feed_back(r):
        at = span(r * step, step)
        full = span(core * own + r * step, step, TILE)
        d_lifted = jnp.zeros((step, width), WIDE)
        for side in range(2):
            d_hidden = matmul(s.d_branch[at, :], s.w_down[side], NT)
            slope = jnp.concatenate([slopes(side, q, r)[...] for q in range(hidden // TILE)], 1)
            d_inner = (d_hidden * slope).astype(LOWF)
            s.d_inner[side, at, :] = d_inner
            d_lifted = d_lifted + matmul(d_inner, s.w_up[side], NT)
        unit = s.unit_one[at, :]
        s.few[1:2, :] += jnp.sum(d_lifted * unit, 0, keepdims=True)
        d_second = s.d_third[at, :] + spread_back(unit, s.inverse_one[at, :1], gain[1], d_lifted)
        s.d_second[at, :] = d_second
        d_mixed = d_second.astype(LOWF)
        s.d_mixed[at, :] = d_mixed
        here = matmul(d_mixed, s.w_out[core], NT).astype(LOWF)
        there = matmul(d_mixed, s.w_out[other], NT).astype(LOWF)
        for hp in range(pairs):
            lanes = slice(hp * TILE, (hp + 1) * TILE)
            s.d_heads[hp, full, :] = here[:, lanes]
            s.d_heads_out[hp, at, :] = there[:, lanes]

    over(own // step, feed_back)
    for hp in range(pairs):
        swap(9 + hp, s.d_heads_out.at[hp], s.d_heads.at[hp, mine])
    for side in range(2):
        s.g_down[side] = matmul(s.hidden[side], s.d_branch[...], TN)
    swap(11, s.g_down.at[other], s.g_down_in)
    for side in range(2):
        s.g_up[side] = matmul(s.lifted[...], s.d_inner[side], TN)
    swap(12, s.g_up.at[other], s.g_up_in)
    for side in range(2):
        s.g_out[side] = matmul(s.joined[side], s.d_mixed[...], TN)
    swap(13, s.g_out.at[other], s.g_out_in)
    d_cand = matmul(s.d_logits[...], s.final[...], TN)
    for c in range(width // TILE):
        s.d_cand[c * slots : (c + 1) * slots, :] = d_cand[:, c * TILE : (c + 1) * TILE]
    swap(14, s.d_cand, s.d_cand_in)
    s.d_keys[...] = jnp.zeros(s.d_keys.shape, WIDE)
    s.d_values[...] = jnp.zeros(s.d_values.shape, WIDE)

    def give_early():
        swapped(11, s.g_down_in)
        swapped(12, s.g_up_in)
        swapped(13, s.g_out_in)
        g_up = s.g_up[core] + s.g_up_in[...]
        at = 0
        for block in (
            s.g_out[core] + s.g_out_in[...],
            *(g_up[:, c * width : (c + 1) * width] for c in range(hidden // width)),
            s.g_down[core] + s.g_down_in[...],
        ):
            early.source[at : at + block.shape[0], :] = block.astype(LOWF)
            at += block.shape[0]
        if at < early.source.shape[0]:
            early.source[at:, :] = jnp.zeros((early.source.shape[0] - at, width), LOWF)
        early.start()

    give_early()
    for hp in range(pairs):
        swapped(9 + hp, s.d_heads.at[hp, yours])

    def attend_back(hp):
        for b, low, wide, at in found:
            d_block = s.d_heads[hp, b * TILE : (b + 1) * TILE, :]
            d_pair = jnp.concatenate([d_block * pick[0], d_block * pick[1]], 0)
            d_prob = matmul(s.values[hp, low : low + wide, :], d_pair, NT)
            prob = s.probs[hp, at : at + wide, :]
            mean = jnp.sum(prob * d_prob, 0, keepdims=True)
            d_scores = (prob * (d_prob - mean)).astype(LOWF)
            s.d_keys[hp, low : low + wide, :] += matmul(d_scores, s.queries[hp, b])
            s.d_values[hp, low : low + wide, :] += matmul(prob.astype(LOWF), d_pair)
            out = matmul(s.keys_t[hp, :, low : low + wide], d_scores)
            out = jnp.concatenate([out[:HEAD, :TILE], out[HEAD:, TILE:]], 0) * SCALE
            lanes = span(hp * TILE, TILE, TILE)
            s.d_triple[0, b * TILE : (b + 1) * TILE, lanes] = out.T.astype(LOWF)

        @pl.when(hp == pairs - 1)
        def _():
            early.across()

    over(pairs, attend_back)
    for hp in range(pairs):
        lanes = slice(hp * TILE, (hp + 1) * TILE)
        s.d_triple[1, :, lanes] = s.d_keys[hp].astype(LOWF)
        s.d_triple[2, :, lanes] = s.d_values[hp].astype(LOWF)
    for side in (yours, mine):
        d_normed = matmul(s.d_triple[0, side, :], s.w_in[0], NT)
        for c in range(1, 3):
            d_normed = d_normed + matmul(s.d_triple[c, side, :], s.w_in[c], NT)
        s.d_normed[side, :] = d_normed
        if side is yours:
            swap(15, s.d_normed.at[yours], s.d_normed_in)
    swapped(15, s.d_normed_in)
    d_normed = s.d_normed[mine, :] + s.d_normed_in[...]
    unit = s.unit_zero[...]
    s.few[0:1, :] = jnp.sum(d_normed * unit, 0, keepdims=True)
    d_first = s.d_second[...] + spread_back(unit, s.inverse_zero[:, :1], gain[0], d_normed)
    s.d_rows[mine, :] = d_first.astype(LOWF)
    swap(16, s.d_rows.at[mine], s.d_rows.at[mine])
    s.few[4:5, :] = jnp.full((1, width), 0.5 * live.astype(WIDE), WIDE)
    swap(17, s.few, s.few_in)
    swapped(14, s.d_cand_in)
    for c in range(width // TILE):
        at = pl.ds(c * slots, slots)
        s.d_rows[slots:, c * TILE : (c + 1) * TILE] = (s.d_cand[at, :] + s.d_cand_in[at, :]).astype(LOWF)
    for c in range(3):
        late.source[c * width : (c + 1) * width, :] = matmul(s.normed_t[...], s.d_triple[c]).astype(LOWF)
    pos_at = 3 * width
    pos_half = places // 2
    swapped(16, s.d_rows.at[yours])
    hot = one_hot(tile_iota((pos_half, slots), 0) + core * pos_half == s.place_row[...])
    late.source[pos_at : pos_at + pos_half, :] = matmul(hot, s.d_rows[:slots, :]).astype(LOWF)
    if pos_at + pos_half < late.source.shape[0]:
        late.source[pos_at + pos_half :, :] = jnp.zeros(
            (late.source.shape[0] - pos_at - pos_half, width), LOWF
        )
    late.start()
    swapped(17, s.few_in)
    s.few_all[me] = s.few[...] + s.few_in[...]

    def give_few(k):
        where = (me + k + 1) % groups
        send(s.few_all.at[me], s.few_all.at[me], s.few_sent.at[where], s.few_came.at[me], (where, core))

    over(groups - 1, give_few)
    early.settle()

    over(
        groups - 1,
        lambda k: departed(
            s.leaving.at[span((me + k + 1) % groups * half, half)], s.row_sent.at[(me + k + 1) % groups]
        ),
    )

    def give_rows(k):
        tile = flipped(me // share, tiles - 1 - k)
        number = s.flat[...] - (core * entries + tile * TILE)
        hot = one_hot(tile_iota((TILE, entries), 0) == number)
        picked = matmul(hot, s.d_rows[...]).astype(LOWF)
        s.leaving[span(tile * TILE, TILE), :] = picked
        into = s.landed.at[core, span(me * half, half)]
        for j in range(share):
            owner = tile * share + j
            block = s.leaving.at[span(owner * half, half)]

            @pl.when(owner != me)
            def _():
                send(block, into, s.land_sent.at[owner], s.land_came.at[me], (owner, core))

            @pl.when(owner == me)
            def _():
                s.landed[core, span(me * half, half), :] = picked[j * half : (j + 1) * half]

    over(tiles, give_rows)
    late.across()
    early.forward()
    late.settle()
    swapped(1, s.reqs.at[other])
    s.grad_table[...] = jnp.zeros(s.grad_table.shape, WIDE)
    part = held // 7

    def gather(side, group):
        came = s.landed[side, span(group * GROUP, GROUP), :]
        first_row = core * held + 1
        lines = [s.reqs[side, pl.ds(2 * group + i, 1), :] - first_row for i in range(2)]

        def block(b):
            at = span(b * part, part, 8)
            rows = tile_iota((part, TILE), 0) + b * part
            hot = jnp.concatenate([one_hot(rows == line) for line in lines], 1)
            s.grad_table[at, :] += matmul(hot, came)

        over(7, block)

    def between(k):
        @pl.when(k == spans // 2)
        def _():
            late.forward()

    take_all(s.landed, s.land_came, s.hand_sent, s.hand_came, gather, between)
    final = s.grad_table[...]
    table_ref[...] = final
    square = (
        jnp.sum(final * final)
        + jnp.sum(early.shard[...] * early.shard[...])
        + jnp.sum(late.shard[...] * late.shard[...])
    )
    s.squares[slot_of] = jnp.full((8, TILE), square, WIDE)

    def square_copy(k):
        where = (slot_of + k + 1) % (2 * groups)
        block = s.squares.at[slot_of]
        return copy_to(
            block, block, s.square_sent.at[where], s.square_came.at[slot_of], (where // 2, where % 2)
        )

    over(2 * groups - 1, lambda k: square_copy(k).start())
    late.collect()
    position_own = s.late_whole.at[pos_at : pos_at + pos_half]
    swap(18, position_own, s.other_half)
    early.collect()
    early_ref[...] = s.early_whole[: early_ref.shape[0], :]
    late_ref[...] = s.late_whole[: late_ref.shape[0], :]

    def take_few(k):
        where = (me + k + 1) % groups
        arrived(s.few_all.at[where], s.few_came.at[where])

    over(groups - 1, take_few)
    few_total = s.few_all[0]
    for source in range(1, groups):
        few_total = few_total + s.few_all[source]
    few_ref[...] = few_total
    position_ref[span(core * pos_half, pos_half), :] = s.late_whole[pos_at : pos_at + pos_half, :]
    swapped(18, s.other_half)
    position_ref[span(other * pos_half, pos_half), :] = s.other_half[...]

    def take_square(k):
        where = (slot_of + k + 1) % (2 * groups)
        arrived(s.squares.at[where], s.square_came.at[where])

    over(2 * groups - 1, take_square)
    gains = few_total[:3]
    norm = jnp.sqrt(jnp.sum(s.squares[...], 0) + jnp.sum(gains * gains))
    stats_ref[...] = norm

    early.drain()
    late.drain()

    def finish(k):
        where = (me + k + 1) % groups
        departed(s.want.at[where], s.want_sent.at[where])
        departed(s.leaving.at[span(where * half, half)], s.land_sent.at[where])
        departed(s.few_all.at[me], s.few_sent.at[where])

    over(groups - 1, finish)

    def finish_group(group):
        block = s.arrived.at[core, span(group * GROUP, GROUP)]
        departed(block, s.pass_sent.at[group])
        departed(block, s.hand_sent.at[group])

    over(spans, finish_group)
    over(2 * groups - 1, lambda k: square_copy(k).wait_send())
    ends = [s.table.at[rows_mine], s.reqs.at[core], s.w_out.at[core], s.w_up.at[core], s.w_down.at[core]]
    ends += [s.cands.at[mine], s.normed.at[mine]]
    ends += [s.mixed.at[hp, yours] for hp in range(2)] + [s.d_heads_out.at[hp] for hp in range(2)]
    ends += [s.g_down.at[other], s.g_up.at[other], s.g_out.at[other], s.d_cand, s.d_normed.at[yours]]
    ends += [s.d_rows.at[mine], s.few, position_own]
    for index, ref in enumerate(ends):
        departed(ref, s.sent.at[index])


def run_step(table, attn_in, attn_out, ffn_up, ffn_down, position, owners, offsets, seg, live, logq, gains, groups):
    held, width = table.shape
    entries = owners.shape[1]
    heads_width, hidden, places = attn_out.shape[0], ffn_up.shape[1], position.shape[0]
    scratch = step_scratch(groups, held, entries, width, heads_width, hidden, places)
    shape = jax.ShapeDtypeStruct
    return pl.pallas_call(
        functools.partial(step_kernel, groups, tuple(scratch)),
        out_shape=(
            shape((held, width), WIDE),
            shape((heads_width + 2 * hidden, width), LOWF),
            shape((3 * heads_width, width), LOWF),
            shape((places, width), LOWF),
            shape((8, width), WIDE),
            shape((8, TILE), WIDE),
        ),
        in_specs=[FAR] * 6 + [VMEM] * 3 + [SMEM] + [VMEM] * 2,
        out_specs=(VMEM,) * 6,
        scratch_shapes=list(scratch.values()),
        compiler_params=pltpu.CompilerParams(
            collective_id=0, has_side_effects=True, vmem_limit_bytes=60 * 1024 * 1024
        ),
    )(table, attn_in, attn_out, ffn_up, ffn_down, position, owners, offsets, seg, live, logq, gains)


def adamw(weight, grad, first, second, decay, rate):
    first = BETA_ONE * first + (1.0 - BETA_ONE) * grad
    second = BETA_TWO * second + (1.0 - BETA_TWO) * grad * grad
    moved = first / (1.0 - BETA_ONE**STEP) / (jnp.sqrt(second / (1.0 - BETA_TWO**STEP)) + ADAM_EPS)
    return (weight - rate * (moved + decay * weight), first, second)


def update_kernel(table_g, early_g, late_g, position_g, few_ref, stats_ref, *refs):
    inputs, outputs, buffers = refs[:21], refs[21:45], refs[45:63]
    came, left = refs[63], refs[64]
    names = ("table", "in", "out", "up", "down", "position")
    ins = [pltpu.make_async_copy(inputs[i], buffers[i], came.at[i]) for i in range(18)]
    outs = [pltpu.make_async_copy(buffers[i], outputs[i], left.at[i]) for i in range(18)]
    for copy in ins:
        copy.start()
    norm = stats_ref[0, 0]
    factor = CLIP / jnp.maximum(norm, CLIP)
    gains = adamw(
        inputs[18][...], few_ref[0:3, :] * factor, inputs[19][...], inputs[20][...], 0.0, RATE_GAINS
    )
    for ref, value in zip(outputs[18:21], gains):
        ref[...] = value
    outputs[21][0, 0] = few_ref[3, 0]
    outputs[22][0, 0] = few_ref[4, 0]
    outputs[23][0, 0] = norm
    width = table_g.shape[1]
    block = 16
    for index, name in enumerate(names):
        trio = buffers[3 * index : 3 * index + 3]
        for i in range(3):
            ins[3 * index + i].wait()
        rate = RATE_POSITION if name == "position" else RATE
        lead = trio[0].shape[0] if name == "in" else 1
        rows, columns = trio[0].shape[-2:]
        heads_width, hidden = buffers[6].shape[0], buffers[9].shape[1]

        def run(r, index=index, name=name, trio=trio, rows=rows, rate=rate):
            at = span(r * block, block)
            views = [ref.at[r * block // rows, span(r * block % rows, block)] if name == "in" else ref.at[at] for ref in trio]
            if name == "table":
                grad = table_g[at, :]
            elif name == "in":
                grad = late_g[at, :].astype(WIDE)
            elif name == "out":
                grad = early_g[at, :].astype(WIDE)
            elif name == "up":
                grad = jnp.concatenate(
                    [
                        early_g[span(heads_width + c * width + r * block, block), :].astype(WIDE)
                        for c in range(hidden // width)
                    ],
                    1,
                )
            elif name == "down":
                grad = early_g[span(heads_width + hidden + r * block, block), :].astype(WIDE)
            else:
                grad = position_g[at, :].astype(WIDE)
            made = adamw(views[0][...], grad * factor, views[1][...], views[2][...], DECAY, rate)
            for view, value in zip(views, made):
                view[...] = value

        over(lead * rows // block, run)
        for i in range(3):
            outs[3 * index + i].start()
    for copy in outs:
        copy.wait()


def run_update(grads, trios):
    flat = [array for trio in trios for array in trio]
    shape = jax.ShapeDtypeStruct
    scalar = shape((1, 1), WIDE)
    return pl.pallas_call(
        update_kernel,
        out_shape=tuple(shape(a.shape, WIDE) for a in flat) + (scalar,) * 3,
        in_specs=[VMEM] * 5 + [VMEM] + [FAR] * 18 + [VMEM] * 3,
        out_specs=(FAR,) * 18 + (VMEM,) * 3 + (SMEM,) * 3,
        scratch_shapes=[pltpu.VMEM(a.shape, WIDE) for a in flat[:18]] + [DMA((18,)), DMA((18,))],
        compiler_params=pltpu.CompilerParams(vmem_limit_bytes=60 * 1024 * 1024),
    )(*grads, *flat)


def body(
    item_table,
    attn_in,
    attn_out,
    ffn_up,
    ffn_down,
    position_table,
    norm_gains,
    item_first,
    item_second,
    attn_in_first,
    attn_in_second,
    attn_out_first,
    attn_out_second,
    ffn_up_first,
    ffn_up_second,
    ffn_down_first,
    ffn_down_second,
    position_first,
    position_second,
    gains_first,
    gains_second,
    owner_group,
    row_offset,
    segment_ids,
    live_slots,
    log_freq,
):
    grads = run_step(
        item_table,
        attn_in,
        attn_out,
        ffn_up,
        ffn_down,
        position_table,
        owner_group.reshape(1, -1),
        row_offset,
        segment_ids,
        live_slots,
        log_freq,
        norm_gains,
        lax.axis_size("dp"),
    )
    made = run_update(
        grads,
        (
            (item_table, item_first, item_second),
            (attn_in, attn_in_first, attn_in_second),
            (attn_out, attn_out_first, attn_out_second),
            (ffn_up, ffn_up_first, ffn_up_second),
            (ffn_down, ffn_down_first, ffn_down_second),
            (position_table, position_first, position_second),
            (norm_gains, gains_first, gains_second),
        ),
    )
    return (*made[:21], *(scalar.reshape(()) for scalar in made[21:]))


def solution(mesh):
    return jax.shard_map(
        body,
        mesh=mesh,
        in_specs=(
            P(("dp", "ffn"), None),
            P(None, None, "ffn"),
            P("ffn", None),
            P(None, "ffn"),
            P("ffn", None),
            P(),
            P(),
            P(("dp", "ffn"), None),
            P(("dp", "ffn"), None),
            P(None, None, "ffn"),
            P(None, None, "ffn"),
            P("ffn", None),
            P("ffn", None),
            P(None, "ffn"),
            P(None, "ffn"),
            P("ffn", None),
            P("ffn", None),
            P(),
            P(),
            P(),
            P(),
            P("dp", None, None),
            P("dp", None),
            P("dp", None),
            P("dp"),
            P("dp", None),
        ),
        out_specs=(
            P(("dp", "ffn"), None),
            P(("dp", "ffn"), None),
            P(("dp", "ffn"), None),
            P(None, None, "ffn"),
            P(None, None, "ffn"),
            P(None, None, "ffn"),
            P("ffn", None),
            P("ffn", None),
            P("ffn", None),
            P(None, "ffn"),
            P(None, "ffn"),
            P(None, "ffn"),
            P("ffn", None),
            P("ffn", None),
            P("ffn", None),
            P(),
            P(),
            P(),
            P(),
            P(),
            P(),
            P(),
            P(),
            P(),
        ),
        check_vma=False,
    )
```

```python
import functools
import types

import jax
import jax.numpy as jnp
from jax import lax
from jax.experimental import pallas as pl
from jax.experimental.pallas import tpu as pltpu
from jax.sharding import PartitionSpec as P

HEAD = 64
STEP = 10
EPSILON = 1e-05
SCALE = 0.125
CLIP = 1.0
RATE = 0.05
RATE_POSITION = 0.3
RATE_GAINS = 0.5
DECAY = 0.01
BETA_ONE = 0.9
BETA_TWO = 0.999
ADAM_EPS = 1e-08
GELU_A = 0.7978845608028654
GELU_B = 0.044715
LOWF = jnp.bfloat16
WIDE = jnp.float32
MESH = pl.DeviceIdType.MESH
DMA = pltpu.SemaphoreType.DMA
VMEM = pl.BlockSpec(memory_space=pltpu.VMEM)
SMEM = pl.BlockSpec(memory_space=pltpu.SMEM)
FAR = pl.BlockSpec(memory_space=pltpu.HBM)
TILE = 128
GROUP = 256
NN = (((1,), (0,)), ((), ()))
NT = (((1,), (1,)), ((), ()))
TN = (((0,), (0,)), ((), ()))
LOWEST = -1e30
REACH = 4
LEVELS = 32
LINKS = 24


def tile_iota(shape, axis):
    return lax.broadcasted_iota(jnp.int32, shape, axis)


def matmul(left, right, dims=NN):
    return lax.dot_general(left, right, dims, preferred_element_type=WIDE)


def as_column(row, eye, ones):
    return matmul((eye * row).astype(LOWF), ones)


def one_hot(condition):
    return jnp.where(condition, 1.0, 0.0).astype(LOWF)


def span(start, size, unit=16):
    return pl.ds(pl.multiple_of(start, unit), size)


def over(count, step):
    def run(index, carry):
        step(index)
        return carry

    lax.fori_loop(0, count, run, 0)


def flipped(value, mask, bits=4):
    total = 0
    for bit in range(bits):
        one, two = (value // 2**bit) % 2, (mask // 2**bit) % 2
        total = total + (one + two - 2 * one * two) * 2**bit
    return total


def copy_to(source, target, send_sem, recv_sem, where):
    return pltpu.make_async_remote_copy(
        src_ref=source,
        dst_ref=target,
        send_sem=send_sem,
        recv_sem=recv_sem,
        device_id=where,
        device_id_type=MESH,
    )


def send(source, target, send_sem, recv_sem, where):
    copy_to(source, target, send_sem, recv_sem, where).start()


def spread_rows(value):
    centred = value - jnp.mean(value, -1, keepdims=True)
    inverse = lax.rsqrt(jnp.mean(centred * centred, -1, keepdims=True) + EPSILON)
    return centred * inverse, inverse


def spread_back(unit, inverse, gain, grad):
    d_unit = grad * gain
    return inverse * (
        d_unit
        - jnp.mean(d_unit, -1, keepdims=True)
        - unit * jnp.mean(d_unit * unit, -1, keepdims=True)
    )


def windows(slots):
    found, at = [], 0
    for block in range(slots // TILE):
        low = max(0, block - REACH) * TILE
        width = (block + 1) * TILE - low
        found.append((block, low, width, at))
        at += width
    return found, at


def levels_of(groups):
    inner = 4 if groups % 4 == 0 else 1
    return inner, groups // inner


def shard_rows(rows, groups):
    return -(-rows // (groups * 16)) * 16


def part_scratch(name, rows, width, groups):
    inner, outer = levels_of(groups)
    shard = shard_rows(rows, groups)
    return {
        name + "_source": pltpu.VMEM((groups * shard, width), LOWF),
        name + "_plane": pltpu.VMEM((inner, outer * shard, width), LOWF),
        name + "_half": pltpu.VMEM((outer * shard, width), LOWF),
        name + "_column": pltpu.VMEM((outer, shard, width), LOWF),
        name + "_shard": pltpu.VMEM((shard, width), WIDE),
        name + "_plane_sent": DMA((inner,)),
        name + "_plane_came": DMA((inner,)),
        name + "_column_sent": DMA((outer,)),
        name + "_column_came": DMA((outer,)),
        name + "_out_sent": DMA((outer,)),
        name + "_ahead_sent": DMA((groups,)),
        name + "_came": DMA((groups,)),
    }


class Part:
    def __init__(self, scratch, name, whole, groups, me, core):
        for key, ref in vars(scratch).items():
            if key.startswith(name + "_"):
                setattr(self, key[len(name) + 1 :], ref)
        self.whole, self.me, self.core = whole, me, core
        self.inner, self.outer = levels_of(groups)
        self.i, self.o = me % self.inner, me // self.inner
        self.size = self.shard.shape[0]

    def quarter(self, j):
        return span(j * self.outer * self.size, self.outer * self.size)

    def piece(self, j, o):
        return span((j * self.outer + o) * self.size, self.size)

    def plane_copy(self, j):
        return copy_to(
            self.source.at[self.quarter(j)],
            self.plane.at[self.i],
            self.plane_sent.at[j],
            self.plane_came.at[self.i],
            (self.o * self.inner + j, self.core),
        )

    def column_copy(self, o):
        return copy_to(
            self.half.at[span(o * self.size, self.size)],
            self.column.at[self.o],
            self.column_sent.at[o],
            self.column_came.at[self.o],
            (o * self.inner + self.i, self.core),
        )

    def out_copy(self, o):
        block = self.whole.at[self.piece(self.i, self.o)]
        came = self.came.at[self.i * self.outer + self.o]
        return copy_to(block, block, self.out_sent.at[o], came, (o * self.inner + self.i, self.core))

    def ahead_copy(self, o, j):
        block = self.whole.at[self.piece(self.i, o)]
        came = self.came.at[self.i * self.outer + o]
        sent = self.ahead_sent.at[j * self.outer + o]
        return copy_to(block, block, sent, came, (self.o * self.inner + j, self.core))

    def wait(self, ref, semaphore):
        copy_to(ref, ref, semaphore, semaphore, (self.me, self.core)).wait_recv()

    def start(self):
        over(self.inner - 1, lambda k: self.plane_copy((self.i + k + 1) % self.inner).start())

    def across(self):
        total = self.source[self.quarter(self.i), :].astype(WIDE)
        for k in range(self.inner - 1):
            j = (self.i + k + 1) % self.inner
            self.wait(self.plane.at[j], self.plane_came.at[j])
            total = total + self.plane[j].astype(WIDE)
        self.half[...] = total.astype(LOWF)
        over(self.outer - 1, lambda k: self.column_copy((self.o + k + 1) % self.outer).start())

    def settle(self):
        self.shard[...] = self.half[span(self.o * self.size, self.size), :].astype(WIDE)

        def take(k):
            o = (self.o + k + 1) % self.outer
            self.wait(self.column.at[o], self.column_came.at[o])
            self.shard[...] += self.column[o].astype(WIDE)

        over(self.outer - 1, take)
        self.whole[self.piece(self.i, self.o), :] = self.shard[...].astype(LOWF)
        over(self.outer - 1, lambda k: self.out_copy((self.o + k + 1) % self.outer).start())
        self.pass_on(self.o)

    def pass_on(self, o):
        over(self.inner - 1, lambda k: self.ahead_copy(o, (self.i + k + 1) % self.inner).start())

    def forward(self):
        def step(k):
            o = (self.o + k + 1) % self.outer
            block = self.whole.at[self.piece(self.i, o)]
            self.wait(block, self.came.at[self.i * self.outer + o])
            self.pass_on(o)

        over(self.outer - 1, step)

    def collect(self):
        def step(k):
            j = (self.i + k // self.outer + 1) % self.inner
            o = k % self.outer
            block = self.whole.at[self.piece(j, o)]
            self.wait(block, self.came.at[j * self.outer + o])

        over((self.inner - 1) * self.outer, step)

    def drain(self):
        over(self.inner - 1, lambda k: self.plane_copy((self.i + k + 1) % self.inner).wait_send())

        def far(k):
            o = (self.o + k + 1) % self.outer
            self.column_copy(o).wait_send()
            self.out_copy(o).wait_send()

        over(self.outer - 1, far)

        def near(k):
            j = (self.i + k // self.outer + 1) % self.inner
            self.ahead_copy(k % self.outer, j).wait_send()

        over((self.inner - 1) * self.outer, near)


def step_scratch(groups, held, entries, width, heads_width, hidden, places):
    slots = entries // 2
    own = slots // 2
    pairs = heads_width // TILE
    area = windows(slots)[1]
    blocks = slots // TILE
    padded = -(-2 * held // TILE) * TILE
    shapes = {
        "table": ((padded, width), LOWF),
        "flat": ((1, entries), jnp.int32),
        "want": ((groups, 8, TILE), jnp.int32),
        "asked": ((groups, 8, TILE), jnp.int32),
        "reqs": ((2, entries // TILE, TILE), jnp.int32),
        "leaving": ((entries, width), LOWF),
        "arrived": ((2, entries, width), LOWF),
        "cands": ((slots, width), LOWF),
        "w_out": ((2, heads_width, width), LOWF),
        "w_up": ((2, width, hidden), LOWF),
        "w_down": ((2, hidden, width), LOWF),
        "w_in": ((3, width, heads_width), LOWF),
        "place_row": ((1, slots), jnp.int32),
        "bias": ((area, TILE), WIDE),
        "pos_high": ((places, width), LOWF),
        "pos_low": ((places, width), LOWF),
        "first": ((own, width), WIDE),
        "normed": ((slots, width), LOWF),
        "normed_t": ((width, slots), LOWF),
        "queries": ((pairs, blocks, 2 * TILE, TILE), LOWF),
        "keys": ((pairs, slots, TILE), LOWF),
        "values": ((pairs, slots, TILE), LOWF),
        "keys_t": ((pairs, TILE, slots), LOWF),
        "values_t": ((pairs, TILE, slots), LOWF),
        "probs": ((pairs, area, 2 * TILE), WIDE),
        "mixed": ((pairs, slots, TILE), LOWF),
        "mixed_in": ((pairs, own, TILE), LOWF),
        "joined": ((2, own, heads_width), LOWF),
        "unit_zero": ((own, width), WIDE),
        "inverse_zero": ((own, TILE), WIDE),
        "unit_one": ((own, width), WIDE),
        "inverse_one": ((own, TILE), WIDE),
        "lifted": ((own, width), LOWF),
        "hidden": ((2, own, hidden), LOWF),
        "unit_two": ((own, width), WIDE),
        "inverse_two": ((own, TILE), WIDE),
        "final": ((own, width), LOWF),
        "logit_bias": ((1, slots), WIDE),
        "d_logits": ((own, slots), LOWF),
        "d_third": ((own, width), WIDE),
        "d_branch": ((own, width), LOWF),
        "d_inner": ((2, own, hidden), LOWF),
        "d_second": ((own, width), WIDE),
        "d_mixed": ((own, width), LOWF),
        "d_heads": ((pairs, slots, TILE), LOWF),
        "d_heads_out": ((pairs, own, TILE), LOWF),
        "d_cand": ((slots * width // TILE, TILE), WIDE),
        "g_out": ((heads_width, width), WIDE),
        "g_up": ((width, hidden), WIDE),
        "g_down": ((hidden, width), WIDE),
        "g_out_out": ((heads_width, width), LOWF),
        "g_up_out": ((width, hidden), LOWF),
        "g_down_out": ((hidden, width), LOWF),
        "g_out_in": ((heads_width, width), LOWF),
        "g_up_in": ((width, hidden), LOWF),
        "g_down_in": ((hidden, width), LOWF),
        "d_keys": ((pairs, slots, TILE), WIDE),
        "d_values": ((pairs, slots, TILE), WIDE),
        "d_triple": ((3, slots, heads_width), LOWF),
        "d_normed_in": ((own, width), WIDE),
        "d_rows": ((entries, width), LOWF),
        "few": ((8, width), WIDE),
        "few_in": ((8, width), WIDE),
        "few_all": ((groups, 8, width), WIDE),
        "squares": ((2 * groups, 8, TILE), WIDE),
        "early_whole": ((groups * shard_rows(2 * hidden + heads_width, groups), width), LOWF),
        "late_whole": ((groups * shard_rows(3 * heads_width + places // 2, groups), width), LOWF),
        "other_half": ((places // 2, width), LOWF),
    }
    scratch = {name: pltpu.VMEM(*entry) for name, entry in shapes.items()}
    for name in ("want", "row", "few", "land"):
        scratch[name + "_sent"] = DMA((groups,))
        scratch[name + "_came"] = DMA((groups,))
    for name in ("pass", "hand"):
        scratch[name + "_sent"] = DMA((entries // GROUP,))
        scratch[name + "_came"] = DMA((entries // GROUP,))
    scratch["square_sent"] = DMA((2 * groups,))
    scratch["square_came"] = DMA((2 * groups,))
    scratch["sent"] = DMA((LINKS,))
    scratch["came"] = DMA((LINKS,))
    scratch["loads"] = DMA((24,))
    scratch.update(part_scratch("early", 2 * hidden + heads_width, width, groups))
    scratch.update(part_scratch("late", 3 * heads_width + places // 2, width, groups))
    return scratch


def step_kernel(groups, keeps, names, *refs):
    (own_ref, off_ref, seg_ref, live_ref, logq_ref, gain_ref) = refs[:6]
    count = 18 if keeps else 6
    fars, refs = refs[6 : 6 + count], refs[6 + count :]
    table_far, in_far, out_far, up_far, down_far, pos_far = fars[:: count // 6]
    (table_ref, early_ref, late_ref, position_ref, few_ref, stats_ref) = refs[:6]
    nears, refs = (refs[6:24], refs[24:]) if keeps else (None, refs[6:])
    s = types.SimpleNamespace(**dict(zip(names, refs)))
    me, core = lax.axis_index("dp"), lax.axis_index("ffn")
    other = 1 - core
    held, width = table_far.shape
    entries = own_ref.shape[1]
    slots = entries // 2
    own = slots // 2
    half = entries // groups
    share = TILE // half
    tiles = entries // TILE
    spans = entries // GROUP
    pairs, hidden, places = s.keys.shape[0], s.w_up.shape[2], pos_far.shape[0]
    heads_width = pairs * TILE
    mine, yours = span(core * own, own), span(other * own, own)
    early = Part(s, "early", s.early_whole, groups, me, core)
    late = Part(s, "late", s.late_whole, groups, me, core)

    barrier = pltpu.get_barrier_semaphore()
    slot_of = me * 2 + core

    def greet(k):
        where = (slot_of + k + 1) % (2 * groups)
        pl.semaphore_signal(
            barrier, inc=1, device_id=(where // 2, where % 2), device_id_type=MESH
        )

    over(2 * groups - 1, greet)
    spare = s.probs.at[0]
    s.d_cand_in = s.bias.at[pl.ds(0, slots * width // TILE)]
    s.column = s.probs.at[1, pl.ds(slots, slots), pl.ds(0, TILE)]
    s.segments = s.probs.at[1, pl.ds(slots, slots), pl.ds(TILE, TILE)]
    s.place = s.probs.at[1, pl.ds(2 * slots, slots), pl.ds(0, TILE)]
    s.total = s.d_normed = s.probs.at[1, pl.ds(0, slots)]
    s.grad_table = spare.at[pl.ds(0, held)]
    pieces = [table_far, out_far]
    pieces += [up_far.at[:, pl.ds(c * width, width)] for c in range(hidden // width)]
    pieces += [down_far, *(in_far.at[c] for c in range(3)), pos_far]
    loads, staged, at = [], [], 0
    if keeps:
        targets = [nears[0], nears[6]]
        targets += [nears[9].at[:, pl.ds(c * width, width)] for c in range(hidden // width)]
        targets += [nears[12], *(nears[3].at[c] for c in range(3)), nears[15]]
    for index, piece in enumerate(pieces):
        near = targets[index] if keeps else spare.at[pl.ds(at, piece.shape[0])]
        at += piece.shape[0]
        staged.append(near)
        loads.append(pltpu.make_async_copy(piece, near, s.loads.at[index]))
    for load in loads:
        load.start()

    def swap(index, source, target):
        send(source, target, s.sent.at[index], s.came.at[index], (me, other))

    def arrived(ref, semaphore):
        copy_to(ref, ref, semaphore, semaphore, (me, core)).wait_recv()

    def departed(ref, semaphore):
        copy_to(ref, ref, semaphore, semaphore, (me, core)).wait_send()

    def swapped(index, target):
        arrived(target, s.came.at[index])

    upper = one_hot(tile_iota((GROUP, GROUP), 0) <= tile_iota((GROUP, GROUP), 1))
    group_of = tile_iota((groups, GROUP), 0)
    before = jnp.zeros((groups, 1), WIDE)
    filled = jnp.zeros((3 * groups, TILE), WIDE)
    spot = (me % share) * half - core * half
    for chunk in range(spans):
        at = slice(chunk * GROUP, (chunk + 1) * GROUP)
        owner, offset = own_ref[:, at], off_ref[:, at]
        marks = jnp.where(group_of == owner, 1.0, 0.0)
        running = matmul(marks.astype(LOWF), upper) + before
        before = running[:, GROUP - 1 :]
        ranks = (jnp.sum(marks * running, 0, keepdims=True) - 1.0).astype(jnp.int32)
        slot = owner * half + ranks
        s.flat[:, at] = jnp.where(ranks < half, slot, slot + (entries - half))
        inside = (ranks >= core * half) & (ranks < core * half + half)
        picks = one_hot(tile_iota((TILE, GROUP), 0) == jnp.where(inside, ranks + spot, -1))
        parts = jnp.concatenate(
            [
                marks * lax.shift_right_logical(offset, 6).astype(WIDE),
                marks * (offset & 63).astype(WIDE),
                marks,
            ],
            0,
        ).astype(LOWF)
        filled = filled + matmul(parts, picks, NT)
    asking = (
        64.0 * filled[:groups] + filled[groups : 2 * groups] + filled[2 * groups :]
    ).astype(jnp.int32)
    for owner in range(groups):
        s.want[owner] = jnp.broadcast_to(asking[owner : owner + 1], (8, TILE))
    s.asked[me] = s.want[me]
    pl.semaphore_wait(barrier, 2 * groups - 1)

    def ask(k):
        owner = (me + groups // 2 + k) % groups

        @pl.when(owner != me)
        def _():
            send(
                s.want.at[owner], s.asked.at[me], s.want_sent.at[owner], s.want_came.at[me], (owner, core)
            )

    over(groups, ask)
    rows_mine, rows_yours = span(core * held, held), span(other * held, held)
    loads[0].wait()
    s.table[rows_mine, :] = staged[0][...].astype(LOWF)
    s.table[2 * held :, :] = jnp.zeros((s.table.shape[0] - 2 * held, width), LOWF)
    swap(0, s.table.at[rows_mine], s.table.at[rows_mine])
    eye = (tile_iota((TILE, TILE), 0) == tile_iota((TILE, TILE), 1)).astype(WIDE)
    ones = jnp.ones((TILE, TILE), LOWF)

    def column_of(line):
        return 64.0 * as_column(lax.shift_right_logical(line, 6).astype(WIDE), eye, ones) + as_column(
            (line & 63).astype(WIDE), eye, ones
        )

    for chunk in range(slots // TILE):
        side, at = divmod(chunk * TILE, own)
        line = s.flat[:, span(side * slots + core * own + at, TILE, TILE)]
        s.column[chunk * TILE : (chunk + 1) * TILE, :] = column_of(line)
    s.total[...] = jnp.zeros(s.total.shape, WIDE)
    swapped(0, s.table.at[rows_yours])
    lanes_wide = tile_iota((TILE, TILE), 1).astype(WIDE)

    def serve(k):
        tile = flipped(me // share, tiles - 1 - k)
        line = jnp.zeros((1, TILE), jnp.int32)
        for j in range(share):
            source = tile * share + j

            @pl.when(source != me)
            def _():
                arrived(s.asked.at[source], s.want_came.at[source])

        for j in range(share):
            line = line + s.asked[tile * share + j][0:1, :]
        s.reqs[core, pl.ds(tile, 1), :] = line
        number = column_of(line)
        hot = jnp.concatenate(
            [
                one_hot(number == lanes_wide + float(b * TILE + 1))
                for b in range(s.table.shape[0] // TILE)
            ],
            1,
        )
        picked = matmul(hot, s.table[...]).astype(LOWF)
        s.leaving[span(tile * TILE, TILE), :] = picked
        into = s.arrived.at[core, span(me * half, half)]
        for j in range(share):
            source = tile * share + j
            block = s.leaving.at[span(source * half, half)]

            @pl.when(source != me)
            def _():
                send(block, into, s.row_sent.at[source], s.row_came.at[me], (source, core))

            @pl.when(source == me)
            def _():
                s.arrived[core, span(me * half, half), :] = picked[j * half : (j + 1) * half]

    over(tiles, serve)
    swap(1, s.reqs.at[core], s.reqs.at[core])

    for load in loads[1:]:
        load.wait()
    keep = []
    if keeps:
        for i in range(12):
            index = i // 2 * 3 + 1 + i % 2
            keep.append(pltpu.make_async_copy(fars[index], nears[index], s.loads.at[12 + i]))
            keep[-1].start()
    s.w_out[core] = staged[1][...].astype(LOWF)
    swap(2, s.w_out.at[core], s.w_out.at[core])
    ups = hidden // width
    for c in range(ups):
        s.w_up[core, :, c * width : (c + 1) * width] = staged[2 + c][...].astype(LOWF)
    swap(3, s.w_up.at[core], s.w_up.at[core])
    s.w_down[core] = staged[2 + ups][...].astype(LOWF)
    swap(4, s.w_down.at[core], s.w_down.at[core])
    for c in range(3):
        s.w_in[c] = staged[3 + ups + c][...].astype(LOWF)
    high = staged[-1][...].astype(LOWF)
    s.pos_high[...] = high
    s.pos_low[...] = (staged[-1][...] - high.astype(WIDE)).astype(LOWF)
    seg = seg_ref[...]
    level = tile_iota((LEVELS, slots), 0)
    starts = jnp.sum(jnp.where(seg < level, 1.0, 0.0), 1, keepdims=True)
    start = jnp.sum(jnp.where(seg == level, starts, 0.0), 0, keepdims=True)
    place_row = tile_iota((1, slots), 1) - start.astype(jnp.int32)
    s.place_row[...] = place_row
    seg_wide = seg.astype(WIDE)
    for b in range(slots // TILE):
        at = slice(b * TILE, (b + 1) * TILE)
        s.segments[at, :] = as_column(seg_wide[:, at], eye, ones)
        s.place[at, :] = column_of(place_row[:, at])
    found, _ = windows(slots)
    causal = tile_iota((TILE, TILE), 0) <= tile_iota((TILE, TILE), 1)
    for b, low, wide, at in found:
        line = seg_wide[:, b * TILE : (b + 1) * TILE]
        for t in range(wide // TILE):
            same = s.segments[low + t * TILE : low + (t + 1) * TILE, :] == line
            if low + t * TILE == b * TILE:
                same = same & causal
            s.bias[at + t * TILE : at + (t + 1) * TILE, :] = jnp.where(same, 0.0, LOWEST)
    live = live_ref[0]
    alive_row = tile_iota((1, slots), 1) < live
    s.logit_bias[...] = jnp.where(alive_row, -logq_ref[...], LOWEST)
    first_lanes = (tile_iota((1, TILE), 1) < HEAD).astype(WIDE)
    pick = [first_lanes.astype(LOWF), (1.0 - first_lanes).astype(LOWF)]
    gain = [gain_ref[g : g + 1, :] for g in range(3)]
    step = 2 * TILE

    def group_at(k):
        near = spans // 2
        turn = jnp.where(k < near // 2, k, jnp.where(k < near // 2 + near, k + near // 2, k - near))
        return flipped(me * half // GROUP, spans - 1 - turn, 3)

    def lay(side, group):
        came = s.arrived[side, span(group * GROUP, GROUP), :]
        where = s.column[...] - (side * entries + group * GROUP).astype(WIDE)
        lane = tile_iota((slots, TILE), 1).astype(WIDE)
        hot = jnp.concatenate([one_hot(where == lane), one_hot(where == lane + float(TILE))], 1)
        s.total[...] += matmul(hot, came)

    def take(k, buffer, came, sent_on, passed, use):
        group = group_at(k)
        for j in range(GROUP // half):
            owner = group * (GROUP // half) + j

            @pl.when(owner != me)
            def _():
                arrived(buffer.at[core, span(owner * half, half)], came.at[owner])

        block = buffer.at[core, span(group * GROUP, GROUP)]
        send(block, block, sent_on.at[group], passed.at[group], (me, other))
        use(core, group)

        @pl.when(k > 0)
        def _():
            last = group_at(k - 1)
            arrived(buffer.at[other, span(last * GROUP, GROUP)], passed.at[last])
            use(other, last)

    def take_all(buffer, came, sent_on, passed, use, between=None):
        def run(k):
            take(k, buffer, came, sent_on, passed, use)
            if between is not None:
                between(k)

        over(spans, run)
        last = group_at(jnp.int32(spans - 1))
        arrived(buffer.at[other, span(last * GROUP, GROUP)], passed.at[last])
        use(other, last)

    take_all(s.arrived, s.row_came, s.pass_sent, s.pass_came, lay)
    s.cands[mine, :] = s.total[own:, :].astype(LOWF)
    swap(5, s.cands.at[mine], s.cands.at[mine])

    def enter(r):
        at = span(r * step, step)
        full = span(core * own + r * step, step, TILE)
        where = s.place[full, :]
        lane = tile_iota((step, TILE), 1).astype(WIDE)
        hot = jnp.concatenate(
            [one_hot(where == lane + float(t * TILE)) for t in range(places // TILE)], 1
        )
        first = s.total[at, :] + matmul(hot, s.pos_high[...]) + matmul(hot, s.pos_low[...])
        s.first[at, :] = first
        unit, inverse = spread_rows(first)
        s.unit_zero[at, :] = unit
        s.inverse_zero[at, :] = jnp.broadcast_to(inverse, (step, TILE))
        s.normed[full, :] = (unit * gain[0]).astype(LOWF)

    over(own // step, enter)
    swap(6, s.normed.at[mine], s.normed.at[mine])

    def project(k):
        @pl.when(k == own // step)
        def _():
            swapped(6, s.normed.at[yours])

        block = (core * (own // step) + k) % (slots // step)
        full = span(block * step, step, TILE)
        normed = s.normed[full, :]
        s.normed_t[:, full] = normed.astype(WIDE).T.astype(LOWF)
        query = (matmul(normed, s.w_in[0]) * SCALE).astype(LOWF)
        keys = matmul(normed, s.w_in[1]).astype(LOWF)
        values = matmul(normed, s.w_in[2]).astype(LOWF)
        keys_t = keys.astype(WIDE).T.astype(LOWF)
        values_t = values.astype(WIDE).T.astype(LOWF)
        for hp in range(pairs):
            lanes = slice(hp * TILE, (hp + 1) * TILE)
            s.keys[hp, full, :] = keys[:, lanes]
            s.values[hp, full, :] = values[:, lanes]
            s.keys_t[hp, :, full] = keys_t[lanes, :]
            s.values_t[hp, :, full] = values_t[lanes, :]
            for i in range(step // TILE):
                part = query[i * TILE : (i + 1) * TILE, lanes]
                for h in range(2):
                    s.queries[hp, block * (step // TILE) + i, h * TILE : (h + 1) * TILE, :] = (
                        part * pick[h]
                    )

    over(slots // step, project)

    def attend(hp):
        for b, low, wide, at in found:
            scores = matmul(s.keys[hp, low : low + wide, :], s.queries[hp, b], NT)
            bias = s.bias[at : at + wide, :]
            scores = scores + jnp.concatenate([bias, bias], 1)
            expo = jnp.exp(scores - jnp.max(scores, 0, keepdims=True))
            prob = expo * (1.0 / jnp.sum(expo, 0, keepdims=True))
            s.probs[hp, at : at + wide, :] = prob
            out = matmul(s.values_t[hp, :, low : low + wide], prob.astype(LOWF))
            out = jnp.concatenate([out[:HEAD, :TILE], out[HEAD:, TILE:]], 0)
            s.mixed[hp, b * TILE : (b + 1) * TILE, :] = out.T.astype(LOWF)
        swap(7 + hp, s.mixed.at[hp, yours], s.mixed_in.at[hp])

    over(pairs, attend)
    for index, block in enumerate((s.w_out, s.w_up, s.w_down)):
        swapped(2 + index, block.at[other])
    over(spans, lambda g: departed(s.arrived.at[core, span(g * GROUP, GROUP)], s.pass_sent.at[g]))
    for hp in range(pairs):
        swapped(7 + hp, s.mixed_in.at[hp])

    def slopes(side, q, r):
        buffer = (s.d_keys, s.d_values)[side]
        fold = slots // own
        return buffer.at[q // fold, span(q % fold * own + r * step, step)]

    def feed(r):
        at = span(r * step, step)
        full = span(core * own + r * step, step, TILE)
        here = jnp.concatenate([s.mixed[hp, full, :] for hp in range(pairs)], 1)
        there = jnp.concatenate([s.mixed_in[hp, at, :] for hp in range(pairs)], 1)
        s.joined[core, at, :] = here
        s.joined[other, at, :] = there
        second = s.first[at, :] + matmul(here, s.w_out[core]) + matmul(there, s.w_out[other])
        unit, inverse = spread_rows(second)
        s.unit_one[at, :] = unit
        s.inverse_one[at, :] = jnp.broadcast_to(inverse, (step, TILE))
        lifted = (unit * gain[1]).astype(LOWF)
        s.lifted[at, :] = lifted
        third = second
        for side in range(2):
            inner = matmul(lifted, s.w_up[side])
            square = inner * inner
            bend = jnp.tanh(GELU_A * inner * (1.0 + GELU_B * square))
            gate = 0.5 * (1.0 + bend)
            act = (inner * gate).astype(LOWF)
            s.hidden[side, at, :] = act
            slope = gate + 0.5 * inner * (1.0 - bend * bend) * (
                GELU_A * (1.0 + 3.0 * GELU_B * square)
            )
            for q in range(hidden // TILE):
                slopes(side, q, r)[...] = slope[:, q * TILE : (q + 1) * TILE]
            third = third + matmul(act, s.w_down[side])
        unit, inverse = spread_rows(third)
        s.unit_two[at, :] = unit
        s.inverse_two[at, :] = jnp.broadcast_to(inverse, (step, TILE))
        s.final[at, :] = (unit * gain[2]).astype(LOWF)

    over(own // step, feed)
    s.few[...] = jnp.zeros((8, width), WIDE)
    swapped(5, s.cands.at[yours])

    def choose(r):
        at = span(r * TILE, TILE)
        logits = matmul(s.final[at, :], s.cands[...], NT) + s.logit_bias[...]
        number = tile_iota((TILE, slots), 0) + (core * own + r * TILE)
        same = tile_iota((TILE, slots), 1) == number
        top = jnp.max(logits, -1, keepdims=True)
        expo = jnp.exp(logits - top)
        total = jnp.sum(expo, -1, keepdims=True)
        alive = number[:, :1] < live
        right = jnp.sum(jnp.where(same, logits, 0.0), -1, keepdims=True)
        loss = jnp.sum(jnp.where(alive, top + jnp.log(total) - right, 0.0))
        s.few[3:4, :] += jnp.full((1, width), loss, WIDE)
        alive = jnp.where(alive, 1.0, 0.0)
        grad = (expo * (alive / total) - jnp.where(same, alive, 0.0)).astype(LOWF)
        s.d_logits[at, :] = grad
        d_final = matmul(grad, s.cands[...])
        unit = s.unit_two[at, :]
        s.few[2:3, :] += jnp.sum(d_final * unit, 0, keepdims=True)
        d_third = spread_back(unit, s.inverse_two[at, :1], gain[2], d_final)
        s.d_third[at, :] = d_third
        s.d_branch[at, :] = d_third.astype(LOWF)

    over(own // TILE, choose)
    s.g_down_out[...] = matmul(s.hidden[other], s.d_branch[...], TN).astype(LOWF)
    swap(11, s.g_down_out, s.g_down_in)
    d_cand = matmul(s.d_logits[...], s.final[...], TN)
    for c in range(width // TILE):
        s.d_cand[c * slots : (c + 1) * slots, :] = d_cand[:, c * TILE : (c + 1) * TILE]
    swap(14, s.d_cand, s.d_cand_in)
    s.g_down[...] = matmul(s.hidden[core], s.d_branch[...], TN)

    def feed_back(r):
        at = span(r * step, step)
        full = span(core * own + r * step, step, TILE)
        d_lifted = jnp.zeros((step, width), WIDE)
        for side in range(2):
            d_hidden = matmul(s.d_branch[at, :], s.w_down[side], NT)
            slope = jnp.concatenate([slopes(side, q, r)[...] for q in range(hidden // TILE)], 1)
            d_inner = (d_hidden * slope).astype(LOWF)
            s.d_inner[side, at, :] = d_inner
            d_lifted = d_lifted + matmul(d_inner, s.w_up[side], NT)
        unit = s.unit_one[at, :]
        s.few[1:2, :] += jnp.sum(d_lifted * unit, 0, keepdims=True)
        d_second = s.d_third[at, :] + spread_back(unit, s.inverse_one[at, :1], gain[1], d_lifted)
        s.d_second[at, :] = d_second
        d_mixed = d_second.astype(LOWF)
        s.d_mixed[at, :] = d_mixed
        here = matmul(d_mixed, s.w_out[core], NT).astype(LOWF)
        there = matmul(d_mixed, s.w_out[other], NT).astype(LOWF)
        for hp in range(pairs):
            lanes = slice(hp * TILE, (hp + 1) * TILE)
            s.d_heads[hp, full, :] = here[:, lanes]
            s.d_heads_out[hp, at, :] = there[:, lanes]

    over(own // step, feed_back)
    for hp in range(pairs):
        swap(9 + hp, s.d_heads_out.at[hp], s.d_heads.at[hp, mine])
    s.g_up_out[...] = matmul(s.lifted[...], s.d_inner[other], TN).astype(LOWF)
    swap(12, s.g_up_out, s.g_up_in)
    s.g_out_out[...] = matmul(s.joined[other], s.d_mixed[...], TN).astype(LOWF)
    swap(13, s.g_out_out, s.g_out_in)
    s.g_up[...] = matmul(s.lifted[...], s.d_inner[core], TN)
    s.g_out[...] = matmul(s.joined[core], s.d_mixed[...], TN)
    s.d_keys[...] = jnp.zeros(s.d_keys.shape, WIDE)
    s.d_values[...] = jnp.zeros(s.d_values.shape, WIDE)

    def give_early():
        swapped(11, s.g_down_in)
        swapped(12, s.g_up_in)
        swapped(13, s.g_out_in)
        g_up = s.g_up[...] + s.g_up_in[...].astype(WIDE)
        at = 0
        for block in (
            s.g_out[...] + s.g_out_in[...].astype(WIDE),
            *(g_up[:, c * width : (c + 1) * width] for c in range(hidden // width)),
            s.g_down[...] + s.g_down_in[...].astype(WIDE),
        ):
            early.source[at : at + block.shape[0], :] = block.astype(LOWF)
            at += block.shape[0]
        if at < early.source.shape[0]:
            early.source[at:, :] = jnp.zeros((early.source.shape[0] - at, width), LOWF)
        early.start()

    for hp in range(pairs):
        swapped(9 + hp, s.d_heads.at[hp, yours])

    def attend_back(hp):
        for b, low, wide, at in found:
            d_block = s.d_heads[hp, b * TILE : (b + 1) * TILE, :]
            d_pair = jnp.concatenate([d_block * pick[0], d_block * pick[1]], 0)
            d_prob = matmul(s.values[hp, low : low + wide, :], d_pair, NT)
            prob = s.probs[hp, at : at + wide, :]
            mean = jnp.sum(prob * d_prob, 0, keepdims=True)
            d_scores = (prob * (d_prob - mean)).astype(LOWF)
            s.d_keys[hp, low : low + wide, :] += matmul(d_scores, s.queries[hp, b])
            s.d_values[hp, low : low + wide, :] += matmul(prob.astype(LOWF), d_pair)
            out = matmul(s.keys_t[hp, :, low : low + wide], d_scores)
            out = jnp.concatenate([out[:HEAD, :TILE], out[HEAD:, TILE:]], 0) * SCALE
            lanes = span(hp * TILE, TILE, TILE)
            s.d_triple[0, b * TILE : (b + 1) * TILE, lanes] = out.T.astype(LOWF)
            if b == 3:
                pl.when(hp == 0)(give_early)


    over(pairs, attend_back)
    for hp in range(pairs):
        lanes = slice(hp * TILE, (hp + 1) * TILE)
        s.d_triple[1, :, lanes] = s.d_keys[hp].astype(LOWF)
        s.d_triple[2, :, lanes] = s.d_values[hp].astype(LOWF)
    for side in (yours, mine):
        d_normed = matmul(s.d_triple[0, side, :], s.w_in[0], NT)
        for c in range(1, 3):
            d_normed = d_normed + matmul(s.d_triple[c, side, :], s.w_in[c], NT)
        s.d_normed[side, :] = d_normed
        if side is yours:
            swap(15, s.d_normed.at[yours], s.d_normed_in)
    early.across()
    swapped(15, s.d_normed_in)
    d_normed = s.d_normed[mine, :] + s.d_normed_in[...]
    unit = s.unit_zero[...]
    d_first = s.d_second[...] + spread_back(unit, s.inverse_zero[:, :1], gain[0], d_normed)
    s.d_rows[mine, :] = d_first.astype(LOWF)
    swap(16, s.d_rows.at[mine], s.d_rows.at[mine])
    s.few[0:1, :] = jnp.sum(d_normed * unit, 0, keepdims=True)
    s.few[4:5, :] = jnp.full((1, width), 0.5 * live.astype(WIDE), WIDE)
    swap(17, s.few, s.few_in)
    swapped(14, s.d_cand_in)
    for c in range(width // TILE):
        at = pl.ds(c * slots, slots)
        s.d_rows[slots:, c * TILE : (c + 1) * TILE] = (s.d_cand[at, :] + s.d_cand_in[at, :]).astype(LOWF)
    over(
        groups - 1,
        lambda k: departed(
            s.leaving.at[span((me + k + 1) % groups * half, half)], s.row_sent.at[(me + k + 1) % groups]
        ),
    )
    early.settle()
    swapped(16, s.d_rows.at[yours])

    def give_rows(k):
        tile = flipped(me // share, tiles - 1 - k)
        number = s.flat[...] - (core * entries + tile * TILE)
        hot = one_hot(tile_iota((TILE, entries), 0) == number)
        picked = matmul(hot, s.d_rows[...]).astype(LOWF)
        s.leaving[span(tile * TILE, TILE), :] = picked
        into = s.arrived.at[core, span(me * half, half)]
        for j in range(share):
            owner = tile * share + j
            block = s.leaving.at[span(owner * half, half)]

            @pl.when(owner != me)
            def _():
                send(block, into, s.land_sent.at[owner], s.land_came.at[me], (owner, core))

            @pl.when(owner == me)
            def _():
                s.arrived[core, span(me * half, half), :] = picked[j * half : (j + 1) * half]

    over(tiles, give_rows)
    for c in range(3):
        late.source[c * width : (c + 1) * width, :] = matmul(s.normed_t[...], s.d_triple[c]).astype(LOWF)
    pos_at = 3 * width
    pos_half = places // 2
    hot = one_hot(tile_iota((pos_half, slots), 0) + core * pos_half == s.place_row[...])
    late.source[pos_at : pos_at + pos_half, :] = matmul(hot, s.d_rows[:slots, :]).astype(LOWF)
    if pos_at + pos_half < late.source.shape[0]:
        late.source[pos_at + pos_half :, :] = jnp.zeros(
            (late.source.shape[0] - pos_at - pos_half, width), LOWF
        )
    late.start()
    swapped(17, s.few_in)
    s.few_all[me] = s.few[...] + s.few_in[...]

    def give_few(k):
        where = (me + k + 1) % groups
        send(s.few_all.at[me], s.few_all.at[me], s.few_sent.at[where], s.few_came.at[me], (where, core))

    over(groups - 1, give_few)
    early.forward()
    late.across()
    swapped(1, s.reqs.at[other])
    s.grad_table[...] = jnp.zeros(s.grad_table.shape, WIDE)

    def gather(side, group):
        came = s.arrived[side, span(group * GROUP, GROUP), :]
        first_row = core * held + 1
        lines = [s.reqs[side, pl.ds(2 * group + i, 1), :] - first_row for i in range(2)]

        rows = tile_iota((held, TILE), 0)
        hot = jnp.concatenate([one_hot(rows == line) for line in lines], 1)
        s.grad_table[...] += matmul(hot, came)

    def between(k):
        @pl.when(k == 1)
        def _():
            late.settle()

        @pl.when(k == 4)
        def _():
            late.forward()

    take_all(s.arrived, s.land_came, s.hand_sent, s.hand_came, gather, between)
    final = s.grad_table[...]
    table_ref[...] = final
    square = (
        jnp.sum(final * final)
        + jnp.sum(early.shard[...] * early.shard[...])
        + jnp.sum(late.shard[...] * late.shard[...])
    )
    s.squares[slot_of] = jnp.full((8, TILE), square, WIDE)

    def square_copy(k):
        where = (slot_of + k + 1) % (2 * groups)
        block = s.squares.at[slot_of]
        return copy_to(
            block, block, s.square_sent.at[where], s.square_came.at[slot_of], (where // 2, where % 2)
        )

    over(2 * groups - 1, lambda k: square_copy(k).start())
    late.collect()
    position_own = s.late_whole.at[pos_at : pos_at + pos_half]
    swap(18, position_own, s.other_half)
    early.collect()
    early_ref[...] = s.early_whole[: early_ref.shape[0], :]
    late_ref[...] = s.late_whole[: late_ref.shape[0], :]

    def take_few(k):
        where = (me + k + 1) % groups
        arrived(s.few_all.at[where], s.few_came.at[where])

    over(groups - 1, take_few)
    few_total = s.few_all[0]
    for source in range(1, groups):
        few_total = few_total + s.few_all[source]
    few_ref[...] = few_total
    position_ref[span(core * pos_half, pos_half), :] = s.late_whole[pos_at : pos_at + pos_half, :]
    swapped(18, s.other_half)
    position_ref[span(other * pos_half, pos_half), :] = s.other_half[...]

    def take_square(k):
        where = (slot_of + k + 1) % (2 * groups)
        arrived(s.squares.at[where], s.square_came.at[where])

    over(2 * groups - 1, take_square)
    gains = few_total[:3]
    norm = jnp.sqrt(jnp.sum(s.squares[...], 0) + jnp.sum(gains * gains))
    stats_ref[...] = norm

    for copy in keep:
        copy.wait()
    early.drain()
    late.drain()

    def finish(k):
        where = (me + k + 1) % groups
        departed(s.want.at[where], s.want_sent.at[where])
        departed(s.leaving.at[span(where * half, half)], s.land_sent.at[where])
        departed(s.few_all.at[me], s.few_sent.at[where])

    over(groups - 1, finish)

    def finish_group(group):
        block = s.arrived.at[core, span(group * GROUP, GROUP)]
        departed(block, s.hand_sent.at[group])

    over(spans, finish_group)
    over(2 * groups - 1, lambda k: square_copy(k).wait_send())
    ends = [s.table.at[rows_mine], s.reqs.at[core], s.w_out.at[core], s.w_up.at[core], s.w_down.at[core]]
    ends += [s.cands.at[mine], s.normed.at[mine]]
    ends += [s.mixed.at[hp, yours] for hp in range(2)] + [s.d_heads_out.at[hp] for hp in range(2)]
    ends += [s.g_down_out, s.g_up_out, s.g_out_out, s.d_cand, s.d_normed.at[yours]]
    ends += [s.d_rows.at[mine], s.few, position_own]
    for index, ref in enumerate(ends):
        departed(ref, s.sent.at[index])


def in_hbm(array):
    return pltpu.with_memory_space_constraint(array, pltpu.HBM)


def run_step(trios, owners, offsets, seg, live, logq, gains, groups, keeps):
    table, _, attn_out, ffn_up, _, position = (trio[0] for trio in trios)
    held, width = table.shape
    entries = owners.shape[1]
    heads_width, hidden, places = attn_out.shape[0], ffn_up.shape[1], position.shape[0]
    scratch = step_scratch(groups, held, entries, width, heads_width, hidden, places)
    shape = pltpu.VMEM
    arrays = [array for trio in trios for array in (trio if keeps else trio[:1])]
    kept = arrays if keeps else []
    return pl.pallas_call(
        functools.partial(step_kernel, groups, keeps, tuple(scratch)),
        out_shape=(
            shape((held, width), WIDE),
            shape((heads_width + 2 * hidden, width), LOWF),
            shape((3 * heads_width, width), LOWF),
            shape((places, width), LOWF),
            shape((8, width), WIDE),
            shape((8, TILE), WIDE),
            *(shape(array.shape, WIDE) for array in kept),
        ),
        in_specs=[VMEM] * 3 + [SMEM] + [VMEM] * 2 + [FAR] * len(arrays),
        out_specs=(VMEM,) * (6 + len(kept)),
        scratch_shapes=list(scratch.values()),
        compiler_params=pltpu.CompilerParams(
            collective_id=0, has_side_effects=True, vmem_limit_bytes=(48 if keeps else 60) * 1024 * 1024
        ),
    )(owners, offsets, seg, live, logq, gains, *(in_hbm(array) for array in arrays))


def adamw(weight, grad, first, second, decay, rate):
    first = BETA_ONE * first + (1.0 - BETA_ONE) * grad
    second = BETA_TWO * second + (1.0 - BETA_TWO) * grad * grad
    moved = first / (1.0 - BETA_ONE**STEP) / (jnp.sqrt(second / (1.0 - BETA_TWO**STEP)) + ADAM_EPS)
    return (weight - rate * (moved + decay * weight), first, second)


def update_kernel(kept, table_g, early_g, late_g, position_g, few_ref, stats_ref, *refs):
    inputs, outputs, buffers = refs[:21], refs[21:45], refs[45:63]
    came, left = refs[63], refs[64]
    names = ("table", "in", "out", "up", "down", "position")
    ins = []
    if not kept:
        ins = [pltpu.make_async_copy(inputs[i], buffers[i], came.at[i]) for i in range(18)]
    outs = [pltpu.make_async_copy(buffers[i], outputs[i], left.at[i]) for i in range(18)]
    for copy in ins:
        copy.start()
    norm = stats_ref[0, 0]
    factor = CLIP / jnp.maximum(norm, CLIP)
    gains = adamw(
        inputs[18][...], few_ref[0:3, :] * factor, inputs[19][...], inputs[20][...], 0.0, RATE_GAINS
    )
    for ref, value in zip(outputs[18:21], gains):
        ref[...] = value
    outputs[21][0, 0] = few_ref[3, 0]
    outputs[22][0, 0] = few_ref[4, 0]
    outputs[23][0, 0] = norm
    width = table_g.shape[1]
    block = 16
    for index, name in enumerate(names):
        trio = buffers[3 * index : 3 * index + 3]
        sources = inputs[3 * index : 3 * index + 3] if kept else trio
        for copy in ins[3 * index : 3 * index + 3]:
            copy.wait()
        rate = RATE_POSITION if name == "position" else RATE
        lead = trio[0].shape[0] if name == "in" else 1
        rows, columns = trio[0].shape[-2:]
        heads_width, hidden = buffers[6].shape[0], buffers[9].shape[1]

        def run(r, name=name, trio=trio, sources=sources, rows=rows, rate=rate):
            at = span(r * block, block)

            def view(ref):
                return ref.at[r * block // rows, span(r * block % rows, block)] if name == "in" else ref.at[at]

            values = [view(ref)[...] for ref in sources]
            if name == "table":
                grad = table_g[at, :]
            elif name == "in":
                grad = late_g[at, :].astype(WIDE)
            elif name == "out":
                grad = early_g[at, :].astype(WIDE)
            elif name == "up":
                grad = jnp.concatenate(
                    [
                        early_g[span(heads_width + c * width + r * block, block), :].astype(WIDE)
                        for c in range(hidden // width)
                    ],
                    1,
                )
            elif name == "down":
                grad = early_g[span(heads_width + hidden + r * block, block), :].astype(WIDE)
            else:
                grad = position_g[at, :].astype(WIDE)
            made = adamw(values[0], grad * factor, values[1], values[2], DECAY, rate)
            for ref, value in zip(trio, made):
                view(ref)[...] = value

        over(lead * rows // block, run)
        for i in range(3):
            outs[3 * index + i].start()
    for copy in outs:
        copy.wait()


def run_update(grads, trios, kept):
    flat = [*kept] if kept else [in_hbm(array) for trio in trios[:6] for array in trio]
    flat += trios[6]
    shape = jax.ShapeDtypeStruct
    scalar = shape((1, 1), WIDE)
    return pl.pallas_call(
        functools.partial(update_kernel, bool(kept)),
        out_shape=tuple(shape(a.shape, WIDE) for a in flat) + (scalar,) * 3,
        in_specs=[VMEM] * 6 + [VMEM if kept else FAR] * 18 + [VMEM] * 3,
        out_specs=(FAR,) * 18 + (VMEM,) * 3 + (SMEM,) * 3,
        scratch_shapes=[pltpu.VMEM(a.shape, WIDE) for a in flat[:18]] + [DMA((18,)), DMA((18,))],
        compiler_params=pltpu.CompilerParams(vmem_limit_bytes=(24 if kept else 48) * 1024 * 1024),
    )(*grads, *flat)


def body(
    item_table,
    attn_in,
    attn_out,
    ffn_up,
    ffn_down,
    position_table,
    norm_gains,
    item_first,
    item_second,
    attn_in_first,
    attn_in_second,
    attn_out_first,
    attn_out_second,
    ffn_up_first,
    ffn_up_second,
    ffn_down_first,
    ffn_down_second,
    position_first,
    position_second,
    gains_first,
    gains_second,
    owner_group,
    row_offset,
    segment_ids,
    live_slots,
    log_freq,
):
    trios = (
        (item_table, item_first, item_second),
        (attn_in, attn_in_first, attn_in_second),
        (attn_out, attn_out_first, attn_out_second),
        (ffn_up, ffn_up_first, ffn_up_second),
        (ffn_down, ffn_down_first, ffn_down_second),
        (position_table, position_first, position_second),
        (norm_gains, gains_first, gains_second),
    )
    groups = lax.axis_size("dp")
    grads = run_step(
        trios[:6],
        owner_group.reshape(1, -1),
        row_offset,
        segment_ids,
        live_slots,
        log_freq,
        norm_gains,
        groups,
        groups <= 16,
    )
    made = run_update(grads[:6], trios, grads[6:])
    return (*made[:21], *(scalar.reshape(()) for scalar in made[21:]))


def solution(mesh):
    return jax.shard_map(
        body,
        mesh=mesh,
        in_specs=(
            P(("dp", "ffn"), None),
            P(None, None, "ffn"),
            P("ffn", None),
            P(None, "ffn"),
            P("ffn", None),
            P(),
            P(),
            P(("dp", "ffn"), None),
            P(("dp", "ffn"), None),
            P(None, None, "ffn"),
            P(None, None, "ffn"),
            P("ffn", None),
            P("ffn", None),
            P(None, "ffn"),
            P(None, "ffn"),
            P("ffn", None),
            P("ffn", None),
            P(),
            P(),
            P(),
            P(),
            P("dp", None, None),
            P("dp", None),
            P("dp", None),
            P("dp"),
            P("dp", None),
        ),
        out_specs=(
            P(("dp", "ffn"), None),
            P(("dp", "ffn"), None),
            P(("dp", "ffn"), None),
            P(None, None, "ffn"),
            P(None, None, "ffn"),
            P(None, None, "ffn"),
            P("ffn", None),
            P("ffn", None),
            P("ffn", None),
            P(None, "ffn"),
            P(None, "ffn"),
            P(None, "ffn"),
            P("ffn", None),
            P("ffn", None),
            P("ffn", None),
            P(),
            P(),
            P(),
            P(),
            P(),
            P(),
            P(),
            P(),
            P(),
        ),
        check_vma=False,
    )
```

```python
import functools
import types

import jax
import jax.numpy as jnp
from jax import lax
from jax.experimental import pallas as pl
from jax.experimental.pallas import tpu as pltpu
from jax.sharding import PartitionSpec as P

HEAD = 64
STEP = 10
EPSILON = 1e-05
SCALE = 0.125
CLIP = 1.0
RATE = 0.05
RATE_POSITION = 0.3
RATE_GAINS = 0.5
DECAY = 0.01
BETA_ONE = 0.9
BETA_TWO = 0.999
ADAM_EPS = 1e-08
GELU_A = 0.7978845608028654
GELU_B = 0.044715
LOWF = jnp.bfloat16
WIDE = jnp.float32
MESH = pl.DeviceIdType.MESH
DMA = pltpu.SemaphoreType.DMA
VMEM = pl.BlockSpec(memory_space=pltpu.VMEM)
SMEM = pl.BlockSpec(memory_space=pltpu.SMEM)
FAR = pl.BlockSpec(memory_space=pltpu.HBM)
TILE = 128
GROUP = 256
NN = (((1,), (0,)), ((), ()))
NT = (((1,), (1,)), ((), ()))
TN = (((0,), (0,)), ((), ()))
LOWEST = -1e30
REACH = 4
LEVELS = 32
LINKS = 24


def tile_iota(shape, axis):
    return lax.broadcasted_iota(jnp.int32, shape, axis)


def matmul(left, right, dims=NN):
    return lax.dot_general(left, right, dims, preferred_element_type=WIDE)


def as_column(row, eye, ones):
    return matmul((eye * row).astype(LOWF), ones)


def one_hot(condition):
    return jnp.where(condition, 1.0, 0.0).astype(LOWF)


def span(start, size, unit=16):
    return pl.ds(pl.multiple_of(start, unit), size)


def over(count, step):
    def run(index, carry):
        step(index)
        return carry

    lax.fori_loop(0, count, run, 0)


def flipped(value, mask, bits=4):
    total = 0
    for bit in range(bits):
        one, two = (value // 2**bit) % 2, (mask // 2**bit) % 2
        total = total + (one + two - 2 * one * two) * 2**bit
    return total


def copy_to(source, target, send_sem, recv_sem, where):
    return pltpu.make_async_remote_copy(
        src_ref=source,
        dst_ref=target,
        send_sem=send_sem,
        recv_sem=recv_sem,
        device_id=where,
        device_id_type=MESH,
    )


def send(source, target, send_sem, recv_sem, where):
    copy_to(source, target, send_sem, recv_sem, where).start()


def spread_rows(value):
    centred = value - jnp.mean(value, -1, keepdims=True)
    inverse = lax.rsqrt(jnp.mean(centred * centred, -1, keepdims=True) + EPSILON)
    return centred * inverse, inverse


def spread_back(unit, inverse, gain, grad):
    d_unit = grad * gain
    return inverse * (
        d_unit
        - jnp.mean(d_unit, -1, keepdims=True)
        - unit * jnp.mean(d_unit * unit, -1, keepdims=True)
    )


def windows(slots):
    found, at = [], 0
    for block in range(slots // TILE):
        low = max(0, block - REACH) * TILE
        width = (block + 1) * TILE - low
        found.append((block, low, width, at))
        at += width
    return found, at


def levels_of(groups):
    inner = 4 if groups % 4 == 0 else 1
    return inner, groups // inner


def shard_rows(rows, groups):
    return -(-rows // (groups * 16)) * 16


def part_scratch(name, rows, width, groups):
    inner, outer = levels_of(groups)
    shard = shard_rows(rows, groups)
    return {
        name + "_source": pltpu.VMEM((groups * shard, width), LOWF),
        name + "_plane": pltpu.VMEM((inner, outer * shard, width), LOWF),
        name + "_half": pltpu.VMEM((outer * shard, width), LOWF),
        name + "_column": pltpu.VMEM((outer, shard, width), LOWF),
        name + "_shard": pltpu.VMEM((shard, width), WIDE),
        name + "_whole": pltpu.VMEM((groups * shard, width), LOWF),
        name + "_plane_sent": DMA((inner,)),
        name + "_plane_came": DMA((inner,)),
        name + "_column_sent": DMA((outer,)),
        name + "_column_came": DMA((outer,)),
        name + "_out_sent": DMA((outer,)),
        name + "_ahead_sent": DMA((inner,)),
        name + "_ahead_came": DMA((inner,)),
        name + "_came": DMA((outer,)),
    }


class Part:
    def __init__(self, scratch, name, groups, me, core):
        for key, ref in vars(scratch).items():
            if key.startswith(name + "_"):
                setattr(self, key[len(name) + 1 :], ref)
        self.me, self.core = me, core
        self.inner, self.outer = levels_of(groups)
        self.i, self.o = me % self.inner, me // self.inner
        self.size = self.shard.shape[0]
        self.rounds = self.outer.bit_length() - 1

    def quarter(self, j):
        return span(j * self.outer * self.size, self.outer * self.size)

    def piece(self, j, o):
        return span((j * self.outer + o) * self.size, self.size)

    def plane_copy(self, j):
        return copy_to(
            self.source.at[self.quarter(j)],
            self.plane.at[self.i],
            self.plane_sent.at[j],
            self.plane_came.at[self.i],
            (self.o * self.inner + j, self.core),
        )

    def mate(self, bit):
        return self.o + (1 - 2 * (self.o // 2**bit % 2)) * 2**bit

    def column_copy(self, bit, index):
        mate = self.mate(bit)
        low = mate % 2 ** (bit + 1)
        source = low + index * 2 ** (bit + 1)
        slot = self.outer - self.outer // 2**bit + index
        return copy_to(
            self.half.at[span(source * self.size, self.size)],
            self.column.at[slot],
            self.column_sent.at[slot],
            self.column_came.at[slot],
            (mate * self.inner + self.i, self.core),
        )

    def out_copy(self, bit, index):
        o = self.o % 2 ** (bit + 1) + index * 2 ** (bit + 1)
        block = self.whole.at[self.piece(self.i, o)]
        return copy_to(
            block,
            block,
            self.out_sent.at[self.outer - self.outer // 2**bit + index],
            self.came.at[o],
            (self.mate(bit) * self.inner + self.i, self.core),
        )

    def ahead_copy(self, j):
        block = self.whole.at[self.quarter(self.i)]
        sent, came = self.ahead_sent.at[j], self.ahead_came.at[self.i]
        return copy_to(block, block, sent, came, (self.o * self.inner + j, self.core))

    def wait(self, ref, semaphore):
        copy_to(ref, ref, semaphore, semaphore, (self.me, self.core)).wait_recv()

    def fill(self, blocks, at=0):
        for block in blocks:
            self.source[at : at + block.shape[0], :] = block.astype(LOWF)
            at += block.shape[0]
        if at < self.source.shape[0]:
            shape = (self.source.shape[0] - at, self.source.shape[1])
            self.source[at:, :] = jnp.zeros(shape, LOWF)
        self.start()

    def start(self):
        over(self.inner - 1, lambda k: self.plane_copy((self.i + k + 1) % self.inner).start())

    def across(self):
        total = self.source[self.quarter(self.i), :].astype(WIDE)
        for k in range(self.inner - 1):
            j = (self.i + k + 1) % self.inner
            self.wait(self.plane.at[j], self.plane_came.at[j])
            total = total + self.plane[j].astype(WIDE)
        self.half[...] = total.astype(LOWF)
        self.halve(0)

    def halve(self, bit):
        over(self.outer // 2 ** (bit + 1), lambda k: self.column_copy(bit, k).start())

    def settle(self, bits):
        for bit in bits:
            count = self.outer // 2 ** (bit + 1)

            def take(k, bit=bit):
                slot = self.outer - self.outer // 2**bit + k
                self.wait(self.column.at[slot], self.column_came.at[slot])
                o = self.o % 2 ** (bit + 1) + k * 2 ** (bit + 1)
                at = span(o * self.size, self.size)
                total = self.half[at, :].astype(WIDE) + self.column[slot].astype(WIDE)
                self.half[at, :] = total.astype(LOWF)
                if bit == self.rounds - 1:
                    self.shard[...] = total
                    self.whole[self.piece(self.i, self.o), :] = total.astype(LOWF)

            over(count, take)
            if bit < self.rounds - 1:
                self.halve(bit + 1)
            else:
                self.double(bit)

    def double(self, bit):
        over(self.outer // 2 ** (bit + 1), lambda k: self.out_copy(bit, k).start())

    def forward(self, bits):
        for bit in bits:

            def step(k, bit=bit):
                o = self.mate(bit) % 2 ** (bit + 1) + k * 2 ** (bit + 1)
                self.wait(self.whole.at[self.piece(self.i, o)], self.came.at[o])

            over(self.outer // 2 ** (bit + 1), step)
            if bit > 0:
                self.double(bit - 1)
            else:
                over(self.inner - 1, lambda k: self.ahead_copy((self.i + k + 1) % self.inner).start())

    def collect(self):
        def step(k):
            j = (self.i + k + 1) % self.inner
            self.wait(self.whole.at[self.quarter(j)], self.ahead_came.at[j])

        over(self.inner - 1, step)

    def drain(self):
        over(self.inner - 1, lambda k: self.plane_copy((self.i + k + 1) % self.inner).wait_send())

        for bit in range(self.rounds):

            def far(k, bit=bit):
                self.column_copy(bit, k).wait_send()
                self.out_copy(bit, k).wait_send()

            over(self.outer // 2 ** (bit + 1), far)

        over(self.inner - 1, lambda k: self.ahead_copy((self.i + k + 1) % self.inner).wait_send())


def part_rows(width, heads_width, hidden, places):
    return {
        "early": heads_width + 2 * hidden,
        "late": 3 * width + places // 2,
    }


def step_scratch(groups, held, entries, width, heads_width, hidden, places):
    slots = entries // 2
    own = slots // 2
    pairs = heads_width // TILE
    area = windows(slots)[1]
    blocks = slots // TILE
    padded = -(-2 * held // TILE) * TILE
    bank = entries // TILE // 2
    shapes = {
        "table": ((padded, width), LOWF),
        "flat": ((1, entries), jnp.int32),
        "want": ((groups, 8, TILE), jnp.int32),
        "asked": ((groups, 8, TILE), jnp.int32),
        "reqs": ((2, entries // TILE, TILE), jnp.int32),
        "leaving": ((2, bank, TILE, width), LOWF),
        "arrived": ((2, 2, bank, TILE, width), LOWF),
        "landed": ((2, 2, bank, TILE, width), LOWF),
        "cands": ((slots, width), LOWF),
        "w_out": ((2, heads_width, width), LOWF),
        "w_up": ((2, width, hidden), LOWF),
        "w_down": ((2, hidden, width), LOWF),
        "w_in": ((3, width, heads_width), LOWF),
        "place_row": ((1, slots), jnp.int32),
        "bias": ((area, TILE), WIDE),
        "pos_high": ((places, width), LOWF),
        "pos_low": ((places, width), LOWF),
        "first": ((own, width), WIDE),
        "normed": ((slots, width), LOWF),
        "normed_t": ((width, slots), LOWF),
        "queries": ((pairs, blocks, 2 * TILE, TILE), LOWF),
        "keys": ((pairs, slots, TILE), LOWF),
        "values": ((pairs, slots, TILE), LOWF),
        "keys_t": ((pairs, TILE, slots), LOWF),
        "values_t": ((pairs, TILE, slots), LOWF),
        "probs": ((pairs, area, 2 * TILE), WIDE),
        "scales": ((pairs, max(8, blocks), 2 * TILE), WIDE),
        "mixed": ((pairs, slots, TILE), LOWF),
        "mixed_in": ((pairs, own, TILE), LOWF),
        "joined": ((2, own, heads_width), LOWF),
        "unit_zero": ((own, width), WIDE),
        "inverse_zero": ((own, TILE), WIDE),
        "unit_one": ((own, width), WIDE),
        "inverse_one": ((own, TILE), WIDE),
        "lifted": ((own, width), LOWF),
        "hidden": ((2, own, hidden), LOWF),
        "unit_two": ((own, width), WIDE),
        "inverse_two": ((own, TILE), WIDE),
        "final": ((own, width), LOWF),
        "logit_bias": ((1, slots), WIDE),
        "d_logits": ((own, slots), LOWF),
        "d_third": ((own, width), WIDE),
        "d_branch": ((own, width), LOWF),
        "d_inner": ((2, own, hidden), LOWF),
        "d_second": ((own, width), WIDE),
        "d_mixed": ((own, width), LOWF),
        "d_heads": ((pairs, slots, TILE), LOWF),
        "d_heads_out": ((pairs, own, TILE), LOWF),
        "d_cand": ((slots * width // TILE, TILE), WIDE),
        "g_out": ((heads_width, width), WIDE),
        "g_up": ((width, hidden), WIDE),
        "g_down": ((hidden, width), WIDE),
        "g_out_out": ((heads_width, width), LOWF),
        "g_up_out": ((width, hidden), LOWF),
        "g_down_out": ((hidden, width), LOWF),
        "g_out_in": ((heads_width, width), LOWF),
        "g_up_in": ((width, hidden), LOWF),
        "g_down_in": ((hidden, width), LOWF),
        "d_keys": ((pairs, slots, TILE), WIDE),
        "d_values": ((pairs, slots, TILE), WIDE),
        "d_triple": ((3, slots, heads_width), LOWF),
        "d_normed_in": ((own, width), WIDE),
        "d_rows": ((entries, width), LOWF),
        "few": ((8, width), WIDE),
        "few_in": ((8, width), WIDE),
        "few_all": ((groups, 8, width), WIDE),
        "other_half": ((places // 2, width), LOWF),
    }
    scratch = {name: pltpu.VMEM(*entry) for name, entry in shapes.items()}
    for name in ("want", "row", "few", "land"):
        scratch[name + "_sent"] = DMA((groups,))
        scratch[name + "_came"] = DMA((groups,))
    for name in ("pass", "hand"):
        scratch[name + "_sent"] = DMA((bank,))
        scratch[name + "_came"] = DMA((bank,))
    scratch["sent"] = DMA((LINKS,))
    scratch["came"] = DMA((LINKS,))
    scratch["loads"] = DMA((24,))
    for name, rows in part_rows(width, heads_width, hidden, places).items():
        scratch.update(part_scratch(name, rows, width, groups))
    return scratch


def step_kernel(groups, keeps, names, *refs):
    (own_ref, off_ref, seg_ref, live_ref, logq_ref, gain_ref) = refs[:6]
    count = 18 if keeps else 6
    fars, refs = refs[6 : 6 + count], refs[6 + count :]
    table_far, in_far, out_far, up_far, down_far, pos_far = fars[:: count // 6]
    (table_ref, down_ref, mid_ref, inward_ref, position_ref, few_ref, stats_ref) = refs[:7]
    nears, refs = (refs[7:25], refs[25:]) if keeps else (None, refs[7:])
    s = types.SimpleNamespace(**dict(zip(names, refs)))
    me, core = lax.axis_index("dp"), lax.axis_index("ffn")
    other = 1 - core
    held, width = table_far.shape
    entries = own_ref.shape[1]
    slots = entries // 2
    own = slots // 2
    half = entries // groups
    share = TILE // half
    tiles = entries // TILE
    spans = entries // GROUP
    pairs, hidden, places = s.keys.shape[0], s.w_up.shape[2], pos_far.shape[0]
    heads_width = pairs * TILE
    mine, yours = span(core * own, own), span(other * own, own)
    early, late = sums = [Part(s, name, groups, me, core) for name in ("early", "late")]

    barrier = pltpu.get_barrier_semaphore()
    slot_of = me * 2 + core

    def greet(k):
        where = (slot_of + k + 1) % (2 * groups)
        pl.semaphore_signal(
            barrier, inc=1, device_id=(where // 2, where % 2), device_id_type=MESH
        )

    over(2 * groups - 1, greet)
    spare = s.probs.at[0]
    s.d_cand_in = s.bias.at[pl.ds(0, slots * width // TILE)]
    s.column = s.probs.at[1, pl.ds(slots, slots), pl.ds(0, TILE)]
    s.segments = s.probs.at[1, pl.ds(slots, slots), pl.ds(TILE, TILE)]
    s.place = s.probs.at[1, pl.ds(2 * slots, slots), pl.ds(0, TILE)]
    s.total = s.d_normed = s.probs.at[1, pl.ds(0, slots)]
    s.grad_table = spare.at[pl.ds(0, held)]
    pieces = [table_far, out_far]
    pieces += [up_far.at[:, pl.ds(c * width, width)] for c in range(hidden // width)]
    pieces += [down_far, *(in_far.at[c] for c in range(3)), pos_far]
    loads, staged, at = [], [], 0
    if keeps:
        targets = [nears[0], nears[6]]
        targets += [nears[9].at[:, pl.ds(c * width, width)] for c in range(hidden // width)]
        targets += [nears[12], *(nears[3].at[c] for c in range(3)), nears[15]]
    for index, piece in enumerate(pieces):
        near = targets[index] if keeps else spare.at[pl.ds(at, piece.shape[0])]
        at += piece.shape[0]
        staged.append(near)
        loads.append(pltpu.make_async_copy(piece, near, s.loads.at[index]))
    for load in loads:
        load.start()

    def swap(index, source, target):
        send(source, target, s.sent.at[index], s.came.at[index], (me, other))

    def arrived(ref, semaphore):
        copy_to(ref, ref, semaphore, semaphore, (me, core)).wait_recv()

    def departed(ref, semaphore):
        copy_to(ref, ref, semaphore, semaphore, (me, core)).wait_send()

    def swapped(index, target):
        arrived(target, s.came.at[index])

    upper = one_hot(tile_iota((GROUP, GROUP), 0) <= tile_iota((GROUP, GROUP), 1))
    group_of = tile_iota((groups, GROUP), 0)
    before = jnp.zeros((groups, 1), WIDE)
    filled = jnp.zeros((3 * groups, TILE), WIDE)
    spot = (me % share) * half - core * half
    for chunk in range(spans):
        at = slice(chunk * GROUP, (chunk + 1) * GROUP)
        owner, offset = own_ref[:, at], off_ref[:, at]
        marks = jnp.where(group_of == owner, 1.0, 0.0)
        running = matmul(marks.astype(LOWF), upper) + before
        before = running[:, GROUP - 1 :]
        ranks = (jnp.sum(marks * running, 0, keepdims=True) - 1.0).astype(jnp.int32)
        slot = owner * half + ranks
        s.flat[:, at] = jnp.where(ranks < half, slot, slot + (entries - half))
        inside = (ranks >= core * half) & (ranks < core * half + half)
        picks = one_hot(tile_iota((TILE, GROUP), 0) == jnp.where(inside, ranks + spot, -1))
        parts = jnp.concatenate(
            [
                marks * lax.shift_right_logical(offset, 6).astype(WIDE),
                marks * (offset & 63).astype(WIDE),
                marks,
            ],
            0,
        ).astype(LOWF)
        filled = filled + matmul(parts, picks, NT)
    asking = (
        64.0 * filled[:groups] + filled[groups : 2 * groups] + filled[2 * groups :]
    ).astype(jnp.int32)
    for owner in range(groups):
        s.want[owner] = jnp.broadcast_to(asking[owner : owner + 1], (8, TILE))
    s.asked[me] = s.want[me]
    pl.semaphore_wait(barrier, 2 * groups - 1)

    def ask(k):
        owner = (me + groups // 2 + k) % groups

        @pl.when(owner != me)
        def _():
            send(
                s.want.at[owner], s.asked.at[me], s.want_sent.at[owner], s.want_came.at[me], (owner, core)
            )

    over(groups, ask)
    rows_mine, rows_yours = span(core * held, held), span(other * held, held)
    loads[0].wait()
    s.table[rows_mine, :] = staged[0][...].astype(LOWF)
    s.table[2 * held :, :] = jnp.zeros((s.table.shape[0] - 2 * held, width), LOWF)
    swap(0, s.table.at[rows_mine], s.table.at[rows_mine])
    eye = (tile_iota((TILE, TILE), 0) == tile_iota((TILE, TILE), 1)).astype(WIDE)
    ones = jnp.ones((TILE, TILE), LOWF)

    def column_of(line):
        return 64.0 * as_column(lax.shift_right_logical(line, 6).astype(WIDE), eye, ones) + as_column(
            (line & 63).astype(WIDE), eye, ones
        )

    for chunk in range(slots // TILE):
        side, at = divmod(chunk * TILE, own)
        line = s.flat[:, span(side * slots + core * own + at, TILE, TILE)]
        s.column[chunk * TILE : (chunk + 1) * TILE, :] = column_of(line)
    s.total[...] = jnp.zeros(s.total.shape, WIDE)
    swapped(0, s.table.at[rows_yours])
    lanes_wide = tile_iota((TILE, TILE), 1).astype(WIDE)

    bank = tiles // 2

    def seat(number):
        tile = number // share
        return tile // bank, tile % bank, span(number % share * half, half)

    def ship(tile, picked, buffer, sent, came):
        s.leaving[tile // bank, tile % bank] = picked
        for j in range(share):
            number = tile * share + j

            @pl.when(number != me)
            def _():
                block = s.leaving.at[seat(number)]
                send(block, buffer.at[(core, *seat(me))], sent.at[number], came.at[me], (number, core))

            @pl.when(number == me)
            def _():
                buffer[(core, *seat(me))] = picked[j * half : (j + 1) * half]

    def serve(tile):
        line = jnp.zeros((1, TILE), jnp.int32)
        for j in range(share):
            source = tile * share + j

            @pl.when(source != me)
            def _():
                arrived(s.asked.at[source], s.want_came.at[source])

        for j in range(share):
            line = line + s.asked[tile * share + j][0:1, :]
        s.reqs[core, pl.ds(tile, 1), :] = line
        number = column_of(line)
        hot = jnp.concatenate(
            [
                one_hot(number == lanes_wide + float(b * TILE + 1))
                for b in range(s.table.shape[0] // TILE)
            ],
            1,
        )
        picked = matmul(hot, s.table[...]).astype(LOWF)
        ship(tile, picked, s.arrived, s.row_sent, s.row_came)

    keep = []
    if keeps:
        for i in range(12):
            index = i // 2 * 3 + 1 + i % 2
            keep.append(pltpu.make_async_copy(fars[index], nears[index], s.loads.at[12 + i]))
    found, _ = windows(slots)
    live = live_ref[0]
    first_lanes = (tile_iota((1, TILE), 1) < HEAD).astype(WIDE)
    pick = [first_lanes.astype(LOWF), (1.0 - first_lanes).astype(LOWF)]
    gain = [gain_ref[g : g + 1, :] for g in range(3)]
    step = 2 * TILE


    def prepare():
        for load in loads[1:]:
            load.wait()
        for copy in keep:
            copy.start()
        s.w_out[core] = staged[1][...].astype(LOWF)
        ups = hidden // width
        for c in range(ups):
            s.w_up[core, :, c * width : (c + 1) * width] = staged[2 + c][...].astype(LOWF)
        s.w_down[core] = staged[2 + ups][...].astype(LOWF)
        for c in range(3):
            s.w_in[c] = staged[3 + ups + c][...].astype(LOWF)
        high = staged[-1][...].astype(LOWF)
        s.pos_high[...] = high
        s.pos_low[...] = (staged[-1][...] - high.astype(WIDE)).astype(LOWF)
        seg = seg_ref[...]
        level = tile_iota((LEVELS, slots), 0)
        starts = jnp.sum(jnp.where(seg < level, 1.0, 0.0), 1, keepdims=True)
        start = jnp.sum(jnp.where(seg == level, starts, 0.0), 0, keepdims=True)
        place_row = tile_iota((1, slots), 1) - start.astype(jnp.int32)
        s.place_row[...] = place_row
        seg_wide = seg.astype(WIDE)
        for b in range(slots // TILE):
            at = slice(b * TILE, (b + 1) * TILE)
            s.segments[at, :] = as_column(seg_wide[:, at], eye, ones)
            s.place[at, :] = column_of(place_row[:, at])
        causal = tile_iota((TILE, TILE), 0) <= tile_iota((TILE, TILE), 1)
        for b, low, wide, at in found:
            line = seg_wide[:, b * TILE : (b + 1) * TILE]
            for t in range(wide // TILE):
                same = s.segments[low + t * TILE : low + (t + 1) * TILE, :] == line
                if low + t * TILE == b * TILE:
                    same = same & causal
                s.bias[at + t * TILE : at + (t + 1) * TILE, :] = jnp.where(same, 0.0, LOWEST)
        alive_row = tile_iota((1, slots), 1) < live
        s.logit_bias[...] = jnp.where(alive_row, -logq_ref[...], LOWEST)
        for index, block in enumerate((s.w_out, s.w_up, s.w_down)):
            swap(2 + index, block.at[core], block.at[core])

    def spot_of(h):
        return flipped(me // share % bank, bank - 1 - h)

    def pair_of(buffer, side, spot):
        return jnp.concatenate([buffer[side, 0, spot], buffer[side, 1, spot]], 0)

    def lay(side, spot):
        lane = tile_iota((slots, TILE), 1).astype(WIDE)
        firsts = [(side * entries + (spot + b * bank) * TILE).astype(WIDE) for b in range(2)]
        hot = jnp.concatenate([one_hot(s.column[...] - first == lane) for first in firsts], 1)
        s.total[...] += matmul(hot, pair_of(s.arrived, side, spot))

    def trade(ahead, give, buffer, came, sent_on, passed, use, between):
        def other_two(h):
            spot = spot_of(h)
            arrived(buffer.at[other, :, spot], passed.at[spot])
            use(other, spot)

        def receive(h):
            spot = spot_of(h)
            for b in range(2):
                for j in range(share):
                    number = (spot + b * bank) * share + j

                    @pl.when(number != me)
                    def _():
                        arrived(buffer.at[(core, *seat(number))], came.at[number])

            block = buffer.at[core, :, spot]
            send(block, block, sent_on.at[spot], passed.at[spot], (me, other))
            use(core, spot)
            pl.when(h > 0)(lambda: other_two(h - 1))

        def step(h):
            @pl.when(h < bank)
            def _():
                spot = spot_of(h)
                far = 1 - me // share // bank
                give(spot + far * bank)
                give(spot + (1 - far) * bank)

            between(h)
            pl.when(h >= ahead)(lambda: receive(h - ahead))

        over(bank + ahead, step)
        other_two(jnp.int32(bank - 1))

    trade(3, serve, s.arrived, s.row_came, s.pass_sent, s.pass_came, lay, lambda h: pl.when(h == 2)(prepare))
    swap(1, s.reqs.at[core], s.reqs.at[core])
    s.cands[mine, :] = s.total[own:, :].astype(LOWF)
    swap(5, s.cands.at[mine], s.cands.at[mine])

    def enter(r):
        at = span(r * step, step)
        full = span(core * own + r * step, step, TILE)
        where = s.place[full, :]
        lane = tile_iota((step, TILE), 1).astype(WIDE)
        hot = jnp.concatenate(
            [one_hot(where == lane + float(t * TILE)) for t in range(places // TILE)], 1
        )
        first = s.total[at, :] + matmul(hot, s.pos_high[...]) + matmul(hot, s.pos_low[...])
        s.first[at, :] = first
        unit, inverse = spread_rows(first)
        s.unit_zero[at, :] = unit
        s.inverse_zero[at, :] = jnp.broadcast_to(inverse, (step, TILE))
        s.normed[full, :] = (unit * gain[0]).astype(LOWF)

    over(own // step, enter)
    swap(6, s.normed.at[mine], s.normed.at[mine])

    def project(k):
        @pl.when(k == own // step)
        def _():
            swapped(6, s.normed.at[yours])

        block = (core * (own // step) + k) % (slots // step)
        full = span(block * step, step, TILE)
        normed = s.normed[full, :]
        s.normed_t[:, full] = normed.astype(WIDE).T.astype(LOWF)
        query = (matmul(normed, s.w_in[0]) * SCALE).astype(LOWF)
        keys = matmul(normed, s.w_in[1]).astype(LOWF)
        values = matmul(normed, s.w_in[2]).astype(LOWF)
        keys_t = keys.astype(WIDE).T.astype(LOWF)
        values_t = values.astype(WIDE).T.astype(LOWF)
        for hp in range(pairs):
            lanes = slice(hp * TILE, (hp + 1) * TILE)
            s.keys[hp, full, :] = keys[:, lanes]
            s.values[hp, full, :] = values[:, lanes]
            s.keys_t[hp, :, full] = keys_t[lanes, :]
            s.values_t[hp, :, full] = values_t[lanes, :]
            for i in range(step // TILE):
                part = query[i * TILE : (i + 1) * TILE, lanes]
                for h in range(2):
                    s.queries[hp, block * (step // TILE) + i, h * TILE : (h + 1) * TILE, :] = (
                        part * pick[h]
                    )

    over(slots // step, project)

    def attend(hp):
        for b, low, wide, at in found:
            scores = matmul(s.keys[hp, low : low + wide, :], s.queries[hp, b], NT)
            bias = s.bias[at : at + wide, :]
            scores = scores + jnp.concatenate([bias, bias], 1)
            expo = jnp.exp(scores - jnp.max(scores, 0, keepdims=True))
            scale = 1.0 / jnp.sum(expo, 0, keepdims=True)
            s.scales[hp, b : b + 1, :] = scale
            s.probs[hp, at : at + wide, :] = expo
            out = matmul(s.values_t[hp, :, low : low + wide], expo.astype(LOWF)) * scale
            out = jnp.concatenate([out[:HEAD, :TILE], out[HEAD:, TILE:]], 0)
            s.mixed[hp, b * TILE : (b + 1) * TILE, :] = out.T.astype(LOWF)
        swap(7 + hp, s.mixed.at[hp, yours], s.mixed_in.at[hp])

    over(pairs, attend)
    for index, block in enumerate((s.w_out, s.w_up, s.w_down)):
        swapped(2 + index, block.at[other])
    over(bank, lambda spot: departed(s.arrived.at[core, :, spot], s.pass_sent.at[spot]))
    for hp in range(pairs):
        swapped(7 + hp, s.mixed_in.at[hp])

    def slopes(side, q, r):
        buffer = (s.d_keys, s.d_values)[side]
        fold = slots // own
        return buffer.at[q // fold, span(q % fold * own + r * step, step)]

    def feed(r):
        at = span(r * step, step)
        full = span(core * own + r * step, step, TILE)
        here = jnp.concatenate([s.mixed[hp, full, :] for hp in range(pairs)], 1)
        there = jnp.concatenate([s.mixed_in[hp, at, :] for hp in range(pairs)], 1)
        s.joined[core, at, :] = here
        s.joined[other, at, :] = there
        second = s.first[at, :] + matmul(here, s.w_out[core]) + matmul(there, s.w_out[other])
        unit, inverse = spread_rows(second)
        s.unit_one[at, :] = unit
        s.inverse_one[at, :] = jnp.broadcast_to(inverse, (step, TILE))
        lifted = (unit * gain[1]).astype(LOWF)
        s.lifted[at, :] = lifted
        third = second
        for side in range(2):
            inner = matmul(lifted, s.w_up[side])
            square = inner * inner
            bend = jnp.tanh(GELU_A * inner * (1.0 + GELU_B * square))
            gate = 0.5 * (1.0 + bend)
            act = (inner * gate).astype(LOWF)
            s.hidden[side, at, :] = act
            slope = gate + 0.5 * inner * (1.0 - bend * bend) * (
                GELU_A * (1.0 + 3.0 * GELU_B * square)
            )
            for q in range(hidden // TILE):
                slopes(side, q, r)[...] = slope[:, q * TILE : (q + 1) * TILE]
            third = third + matmul(act, s.w_down[side])
        unit, inverse = spread_rows(third)
        s.unit_two[at, :] = unit
        s.inverse_two[at, :] = jnp.broadcast_to(inverse, (step, TILE))
        s.final[at, :] = (unit * gain[2]).astype(LOWF)

    over(own // step, feed)
    s.few[...] = jnp.zeros((8, width), WIDE)
    swapped(5, s.cands.at[yours])

    def choose(r):
        at = span(r * TILE, TILE)
        here = span(core * own + r * TILE, TILE, TILE)
        final = s.final[at, :]
        logits = matmul(final, s.cands[...], NT) + s.logit_bias[...]
        square = matmul(final, s.cands[here, :], NT) + s.logit_bias[:, here]
        same = tile_iota((TILE, TILE), 0) == tile_iota((TILE, TILE), 1)
        number = tile_iota((TILE, 1), 0) + (core * own + r * TILE)
        top = jnp.max(logits, -1, keepdims=True)
        expo = jnp.exp(logits - top)
        total = jnp.sum(expo, -1, keepdims=True)
        alive = number < live
        right = jnp.sum(jnp.where(same, square, 0.0), -1, keepdims=True)
        loss = jnp.sum(jnp.where(alive, top + jnp.log(total) - right, 0.0))
        s.few[3:4, :] += jnp.full((1, width), loss, WIDE)
        alive = jnp.where(alive, 1.0, 0.0)
        scale = alive / total
        s.d_logits[at, :] = (expo * scale).astype(LOWF)
        square = jnp.exp(square - top) * scale - jnp.where(same, alive, 0.0)
        s.d_logits[at, here] = square.astype(LOWF)
        grad = s.d_logits[at, :]
        d_final = matmul(grad, s.cands[...])
        unit = s.unit_two[at, :]
        s.few[2:3, :] += jnp.sum(d_final * unit, 0, keepdims=True)
        d_third = spread_back(unit, s.inverse_two[at, :1], gain[2], d_final)
        s.d_third[at, :] = d_third
        s.d_branch[at, :] = d_third.astype(LOWF)

    over(own // TILE, choose)
    s.g_down_out[...] = matmul(s.hidden[other], s.d_branch[...], TN).astype(LOWF)
    swap(11, s.g_down_out, s.g_down_in)
    d_cand = matmul(s.d_logits[...], s.final[...], TN)
    for c in range(width // TILE):
        s.d_cand[c * slots : (c + 1) * slots, :] = d_cand[:, c * TILE : (c + 1) * TILE]
    swap(14, s.d_cand, s.d_cand_in)
    s.g_down[...] = matmul(s.hidden[core], s.d_branch[...], TN)

    def feed_back(r):
        at = span(r * step, step)
        full = span(core * own + r * step, step, TILE)
        d_lifted = jnp.zeros((step, width), WIDE)
        for side in range(2):
            d_hidden = matmul(s.d_branch[at, :], s.w_down[side], NT)
            slope = jnp.concatenate([slopes(side, q, r)[...] for q in range(hidden // TILE)], 1)
            d_inner = (d_hidden * slope).astype(LOWF)
            s.d_inner[side, at, :] = d_inner
            d_lifted = d_lifted + matmul(d_inner, s.w_up[side], NT)
        unit = s.unit_one[at, :]
        s.few[1:2, :] += jnp.sum(d_lifted * unit, 0, keepdims=True)
        d_second = s.d_third[at, :] + spread_back(unit, s.inverse_one[at, :1], gain[1], d_lifted)
        s.d_second[at, :] = d_second
        d_mixed = d_second.astype(LOWF)
        s.d_mixed[at, :] = d_mixed
        here = matmul(d_mixed, s.w_out[core], NT).astype(LOWF)
        there = matmul(d_mixed, s.w_out[other], NT).astype(LOWF)
        for hp in range(pairs):
            lanes = slice(hp * TILE, (hp + 1) * TILE)
            s.d_heads[hp, full, :] = here[:, lanes]
            s.d_heads_out[hp, at, :] = there[:, lanes]

    over(own // step, feed_back)
    for hp in range(pairs):
        swap(9 + hp, s.d_heads_out.at[hp], s.d_heads.at[hp, mine])
    s.g_up_out[...] = matmul(s.lifted[...], s.d_inner[other], TN).astype(LOWF)
    swap(12, s.g_up_out, s.g_up_in)
    s.g_out_out[...] = matmul(s.joined[other], s.d_mixed[...], TN).astype(LOWF)
    swap(13, s.g_out_out, s.g_out_in)
    s.g_up[...] = matmul(s.lifted[...], s.d_inner[core], TN)
    s.g_out[...] = matmul(s.joined[core], s.d_mixed[...], TN)
    s.d_keys[...] = jnp.zeros(s.d_keys.shape, WIDE)
    s.d_values[...] = jnp.zeros(s.d_values.shape, WIDE)

    def give_mid():
        swapped(11, s.g_down_in)
        swapped(12, s.g_up_in)
        swapped(13, s.g_out_in)
        g_up = s.g_up[...] + s.g_up_in[...].astype(WIDE)
        early.fill(
            (
                s.g_out[...] + s.g_out_in[...].astype(WIDE),
                *(g_up[:, c * width : (c + 1) * width] for c in range(hidden // width)),
                s.g_down[...] + s.g_down_in[...].astype(WIDE),
            )
        )

    give_mid()
    for hp in range(pairs):
        swapped(9 + hp, s.d_heads.at[hp, yours])

    def attend_back(hp):
        for b, low, wide, at in found:
            d_block = s.d_heads[hp, b * TILE : (b + 1) * TILE, :]
            d_pair = jnp.concatenate([d_block * pick[0], d_block * pick[1]], 0)
            d_prob = matmul(s.values[hp, low : low + wide, :], d_pair, NT)
            prob = s.probs[hp, at : at + wide, :] * s.scales[hp, b : b + 1, :]
            mean = jnp.sum(prob * d_prob, 0, keepdims=True)
            d_scores = (prob * (d_prob - mean)).astype(LOWF)
            s.d_keys[hp, low : low + wide, :] += matmul(d_scores, s.queries[hp, b])
            s.d_values[hp, low : low + wide, :] += matmul(prob.astype(LOWF), d_pair)
            out = matmul(s.keys_t[hp, :, low : low + wide], d_scores)
            out = jnp.concatenate([out[:HEAD, :TILE], out[HEAD:, TILE:]], 0) * SCALE
            lanes = span(hp * TILE, TILE, TILE)
            s.d_triple[0, b * TILE : (b + 1) * TILE, lanes] = out.T.astype(LOWF)


    over(pairs, attend_back)
    for hp in range(pairs):
        lanes = slice(hp * TILE, (hp + 1) * TILE)
        s.d_triple[1, :, lanes] = s.d_keys[hp].astype(LOWF)
        s.d_triple[2, :, lanes] = s.d_values[hp].astype(LOWF)
    for side in (yours, mine):
        d_normed = matmul(s.d_triple[0, side, :], s.w_in[0], NT)
        for c in range(1, 3):
            d_normed = d_normed + matmul(s.d_triple[c, side, :], s.w_in[c], NT)
        s.d_normed[side, :] = d_normed
        if side is yours:
            swap(15, s.d_normed.at[yours], s.d_normed_in)
    for c in range(3):
        g_in = matmul(s.normed_t[...], s.d_triple[c])
        late.source[c * width : (c + 1) * width, :] = g_in.astype(LOWF)
    early.across()
    swapped(15, s.d_normed_in)
    d_normed = s.d_normed[mine, :] + s.d_normed_in[...]
    unit = s.unit_zero[...]
    d_first = s.d_second[...] + spread_back(unit, s.inverse_zero[:, :1], gain[0], d_normed)
    s.d_rows[mine, :] = d_first.astype(LOWF)
    swap(16, s.d_rows.at[mine], s.d_rows.at[mine])
    s.few[0:1, :] = jnp.sum(d_normed * unit, 0, keepdims=True)
    s.few[4:5, :] = jnp.full((1, width), 0.5 * live.astype(WIDE), WIDE)
    swapped(14, s.d_cand_in)
    for c in range(width // TILE):
        at = pl.ds(c * slots, slots)
        s.d_rows[slots:, c * TILE : (c + 1) * TILE] = (s.d_cand[at, :] + s.d_cand_in[at, :]).astype(LOWF)
    over(
        groups - 1,
        lambda k: departed(
            s.leaving.at[seat((me + k + 1) % groups)], s.row_sent.at[(me + k + 1) % groups]
        ),
    )
    swapped(16, s.d_rows.at[yours])

    def give_rows(tile):
        number = s.flat[...] - (core * entries + tile * TILE)
        hot = one_hot(tile_iota((TILE, entries), 0) == number)
        picked = matmul(hot, s.d_rows[...]).astype(LOWF)
        ship(tile, picked, s.landed, s.land_sent, s.land_came)

    pos_half = places // 2

    def give_late():
        hot = one_hot(tile_iota((pos_half, slots), 0) + core * pos_half == s.place_row[...])
        late.fill((matmul(hot, s.d_rows[:slots, :]),), 3 * width)

    swapped(1, s.reqs.at[other])
    s.grad_table[...] = jnp.zeros(s.grad_table.shape, WIDE)

    def gather(side, spot):
        came = pair_of(s.landed, side, spot)
        first_row = core * held + 1
        lines = [s.reqs[side, pl.ds(spot + b * bank, 1), :] - first_row for b in range(2)]
        rows = tile_iota((held, TILE), 0)
        hot = jnp.concatenate([one_hot(rows == line) for line in lines], 1)
        s.grad_table[...] += matmul(hot, came)

    def between(h):
        first, last = range(late.rounds - 1), range(late.rounds - 1, late.rounds)
        back, end = range(late.rounds - 1, 0, -1), range(1)
        plan = {
            0: (give_late,),
            1: (lambda: early.settle(first),),
            2: (lambda: early.settle(last),),
            3: (late.across, lambda: early.forward(back)),
            4: (lambda: early.forward(end), lambda: late.settle(first)),
            5: (lambda: late.settle(last),),
            6: (lambda: late.forward(back),),
            7: (lambda: late.forward(end),),
        }
        for at, acts in plan.items():
            for act in acts:
                pl.when(h == at)(act)

    trade(3, give_rows, s.landed, s.land_came, s.hand_sent, s.hand_came, gather, between)
    final = s.grad_table[...]
    table_ref[...] = final
    square = jnp.sum(final * final)
    for part in sums:
        square = square + jnp.sum(part.shard[...] * part.shard[...])
    s.few[5:6, :] = jnp.full((1, width), square, WIDE)
    swap(17, s.few, s.few_in)
    swapped(17, s.few_in)
    s.few_all[me] = s.few[...] + s.few_in[...]

    def few_copy(k):
        where = (me + k + 1) % groups
        block = s.few_all.at[me]
        return copy_to(block, block, s.few_sent.at[where], s.few_came.at[me], (where, core))

    over(groups - 1, lambda k: few_copy(k).start())
    late.collect()
    position_own = late.whole.at[pl.ds(3 * width, pos_half)]
    swap(18, position_own, s.other_half)
    early.collect()
    mid_ref[...] = early.whole[: mid_ref.shape[0], :]
    down_ref[...] = early.whole[mid_ref.shape[0] : mid_ref.shape[0] + hidden, :]
    inward_ref[...] = late.whole[: 3 * width, :]
    position_ref[span(core * pos_half, pos_half), :] = late.whole[3 * width : 3 * width + pos_half, :]
    swapped(18, s.other_half)
    position_ref[span(other * pos_half, pos_half), :] = s.other_half[...]

    def take_few(k):
        where = (me + k + 1) % groups
        arrived(s.few_all.at[where], s.few_came.at[where])

    over(groups - 1, take_few)
    few_total = s.few_all[0]
    for source in range(1, groups):
        few_total = few_total + s.few_all[source]
    few_ref[...] = few_total
    gains = few_total[:3]
    stats_ref[...] = jnp.sqrt(few_total[5:6, :TILE] + jnp.sum(gains * gains)) + jnp.zeros((8, TILE), WIDE)

    for copy in keep:
        copy.wait()
    for part in sums:
        part.drain()

    def finish(k):
        where = (me + k + 1) % groups
        departed(s.want.at[where], s.want_sent.at[where])
        departed(s.leaving.at[seat(where)], s.land_sent.at[where])

    over(groups - 1, finish)

    over(bank, lambda spot: departed(s.landed.at[core, :, spot], s.hand_sent.at[spot]))
    over(groups - 1, lambda k: few_copy(k).wait_send())
    ends = [s.table.at[rows_mine], s.reqs.at[core], s.w_out.at[core], s.w_up.at[core], s.w_down.at[core]]
    ends += [s.cands.at[mine], s.normed.at[mine]]
    ends += [s.mixed.at[hp, yours] for hp in range(2)] + [s.d_heads_out.at[hp] for hp in range(2)]
    ends += [s.g_down_out, s.g_up_out, s.g_out_out, s.d_cand, s.d_normed.at[yours]]
    ends += [s.d_rows.at[mine], s.few, position_own]
    for index, ref in enumerate(ends):
        departed(ref, s.sent.at[index])


def in_hbm(array):
    return pltpu.with_memory_space_constraint(array, pltpu.HBM)


def run_step(trios, owners, offsets, seg, live, logq, gains, groups, keeps):
    table, _, attn_out, ffn_up, _, position = (trio[0] for trio in trios)
    held, width = table.shape
    entries = owners.shape[1]
    heads_width, hidden, places = attn_out.shape[0], ffn_up.shape[1], position.shape[0]
    scratch = step_scratch(groups, held, entries, width, heads_width, hidden, places)
    shape = pltpu.VMEM
    arrays = [array for trio in trios for array in (trio if keeps else trio[:1])]
    kept = arrays if keeps else []
    return pl.pallas_call(
        functools.partial(step_kernel, groups, keeps, tuple(scratch)),
        out_shape=(
            shape((held, width), WIDE),
            shape((hidden, width), LOWF),
            shape((heads_width + hidden, width), LOWF),
            shape((3 * width, width), LOWF),
            shape((places, width), LOWF),
            shape((8, width), WIDE),
            shape((8, TILE), WIDE),
            *(shape(array.shape, WIDE) for array in kept),
        ),
        in_specs=[VMEM] * 3 + [SMEM] + [VMEM] * 2 + [FAR] * len(arrays),
        out_specs=(VMEM,) * (7 + len(kept)),
        scratch_shapes=list(scratch.values()),
        compiler_params=pltpu.CompilerParams(
            collective_id=0, has_side_effects=True, vmem_limit_bytes=(50 if keeps else 60) * 1024 * 1024
        ),
    )(owners, offsets, seg, live, logq, gains, *(in_hbm(array) for array in arrays))


def adamw(weight, grad, first, second, decay, rate):
    first = BETA_ONE * first + (1.0 - BETA_ONE) * grad
    second = BETA_TWO * second + (1.0 - BETA_TWO) * grad * grad
    moved = first / (1.0 - BETA_ONE**STEP) / (jnp.sqrt(second / (1.0 - BETA_TWO**STEP)) + ADAM_EPS)
    return (weight - rate * (moved + decay * weight), first, second)


def update_kernel(kept, table_g, down_g, mid_g, inward_g, position_g, few_ref, stats_ref, *refs):
    inputs, outputs, buffers = refs[:21], refs[21:45], refs[45:63]
    came, left = refs[63], refs[64]
    names = ("table", "in", "out", "up", "down", "position")
    ins = []
    if not kept:
        ins = [pltpu.make_async_copy(inputs[i], buffers[i], came.at[i]) for i in range(18)]
    outs = [pltpu.make_async_copy(buffers[i], outputs[i], left.at[i]) for i in range(18)]
    for copy in ins:
        copy.start()
    norm = stats_ref[0, 0]
    factor = CLIP / jnp.maximum(norm, CLIP)
    gains = adamw(
        inputs[18][...], few_ref[0:3, :] * factor, inputs[19][...], inputs[20][...], 0.0, RATE_GAINS
    )
    for ref, value in zip(outputs[18:21], gains):
        ref[...] = value
    outputs[21][0, 0] = few_ref[3, 0]
    outputs[22][0, 0] = few_ref[4, 0]
    outputs[23][0, 0] = norm
    width = table_g.shape[1]
    for index, name in enumerate(names):
        trio = buffers[3 * index : 3 * index + 3]
        sources = inputs[3 * index : 3 * index + 3] if kept else trio
        for copy in ins[3 * index : 3 * index + 3]:
            copy.wait()
        rate = RATE_POSITION if name == "position" else RATE
        block = {"table": 112, "up": 32}.get(name, 64)
        lead = trio[0].shape[0] if name == "in" else 1
        rows, columns = trio[0].shape[-2:]
        heads_width, hidden = buffers[6].shape[0], buffers[9].shape[1]

        def run(r, block=block, name=name, trio=trio, sources=sources, rows=rows, rate=rate):
            at = span(r * block, block)

            def view(ref):
                return ref.at[r * block // rows, span(r * block % rows, block)] if name == "in" else ref.at[at]

            values = [view(ref)[...] for ref in sources]
            if name == "table":
                grad = table_g[at, :]
            elif name == "in":
                grad = inward_g[at, :].astype(WIDE)
            elif name == "out":
                grad = mid_g[at, :].astype(WIDE)
            elif name == "up":
                grad = jnp.concatenate(
                    [
                        mid_g[span(heads_width + c * width + r * block, block), :].astype(WIDE)
                        for c in range(hidden // width)
                    ],
                    1,
                )
            elif name == "down":
                grad = down_g[at, :].astype(WIDE)
            else:
                grad = position_g[at, :].astype(WIDE)
            made = adamw(values[0], grad * factor, values[1], values[2], DECAY, rate)
            for ref, value in zip(trio, made):
                view(ref)[...] = value

        over(lead * rows // block, run)
        for i in range(3):
            outs[3 * index + i].start()
    for copy in outs:
        copy.wait()


def run_update(grads, trios, kept):
    flat = [*kept] if kept else [in_hbm(array) for trio in trios[:6] for array in trio]
    flat += trios[6]
    shape = jax.ShapeDtypeStruct
    scalar = shape((1, 1), WIDE)
    return pl.pallas_call(
        functools.partial(update_kernel, bool(kept)),
        out_shape=tuple(shape(a.shape, WIDE) for a in flat) + (scalar,) * 3,
        in_specs=[VMEM] * 7 + [VMEM if kept else FAR] * 18 + [VMEM] * 3,
        out_specs=(FAR,) * 18 + (VMEM,) * 3 + (SMEM,) * 3,
        scratch_shapes=[pltpu.VMEM(a.shape, WIDE) for a in flat[:18]] + [DMA((18,)), DMA((18,))],
        compiler_params=pltpu.CompilerParams(vmem_limit_bytes=(24 if kept else 48) * 1024 * 1024),
    )(*grads, *flat)


def body(
    item_table,
    attn_in,
    attn_out,
    ffn_up,
    ffn_down,
    position_table,
    norm_gains,
    item_first,
    item_second,
    attn_in_first,
    attn_in_second,
    attn_out_first,
    attn_out_second,
    ffn_up_first,
    ffn_up_second,
    ffn_down_first,
    ffn_down_second,
    position_first,
    position_second,
    gains_first,
    gains_second,
    owner_group,
    row_offset,
    segment_ids,
    live_slots,
    log_freq,
):
    trios = (
        (item_table, item_first, item_second),
        (attn_in, attn_in_first, attn_in_second),
        (attn_out, attn_out_first, attn_out_second),
        (ffn_up, ffn_up_first, ffn_up_second),
        (ffn_down, ffn_down_first, ffn_down_second),
        (position_table, position_first, position_second),
        (norm_gains, gains_first, gains_second),
    )
    groups = lax.axis_size("dp")
    made = run_step(
        trios[:6],
        owner_group.reshape(1, -1),
        row_offset,
        segment_ids,
        live_slots,
        log_freq,
        norm_gains,
        groups,
        groups <= 16,
    )
    made = run_update(made[:7], trios, made[7:])
    return (*made[:21], *(scalar.reshape(()) for scalar in made[21:]))


def solution(mesh):
    return jax.shard_map(
        body,
        mesh=mesh,
        in_specs=(
            P(("dp", "ffn"), None),
            P(None, None, "ffn"),
            P("ffn", None),
            P(None, "ffn"),
            P("ffn", None),
            P(),
            P(),
            P(("dp", "ffn"), None),
            P(("dp", "ffn"), None),
            P(None, None, "ffn"),
            P(None, None, "ffn"),
            P("ffn", None),
            P("ffn", None),
            P(None, "ffn"),
            P(None, "ffn"),
            P("ffn", None),
            P("ffn", None),
            P(),
            P(),
            P(),
            P(),
            P("dp", None, None),
            P("dp", None),
            P("dp", None),
            P("dp"),
            P("dp", None),
        ),
        out_specs=(
            P(("dp", "ffn"), None),
            P(("dp", "ffn"), None),
            P(("dp", "ffn"), None),
            P(None, None, "ffn"),
            P(None, None, "ffn"),
            P(None, None, "ffn"),
            P("ffn", None),
            P("ffn", None),
            P("ffn", None),
            P(None, "ffn"),
            P(None, "ffn"),
            P(None, "ffn"),
            P("ffn", None),
            P("ffn", None),
            P("ffn", None),
            P(),
            P(),
            P(),
            P(),
            P(),
            P(),
            P(),
            P(),
            P(),
        ),
        check_vma=False,
    )
```

```python
import functools
import types

import jax
import jax.numpy as jnp
from jax import lax
from jax.experimental import pallas as pl
from jax.experimental.pallas import tpu as pltpu
from jax.sharding import PartitionSpec as P

HEAD = 64
STEP = 10
EPSILON = 1e-05
SCALE = 0.125
CLIP = 1.0
RATE = 0.05
RATE_POSITION = 0.3
RATE_GAINS = 0.5
DECAY = 0.01
BETA_ONE = 0.9
BETA_TWO = 0.999
ADAM_EPS = 1e-08
GELU_A = 0.7978845608028654
GELU_B = 0.044715
LOWF = jnp.bfloat16
WIDE = jnp.float32
MESH = pl.DeviceIdType.MESH
DMA = pltpu.SemaphoreType.DMA
VMEM = pl.BlockSpec(memory_space=pltpu.VMEM)
SMEM = pl.BlockSpec(memory_space=pltpu.SMEM)
FAR = pl.BlockSpec(memory_space=pltpu.HBM)
TILE = 128
GROUP = 256
NN = (((1,), (0,)), ((), ()))
NT = (((1,), (1,)), ((), ()))
TN = (((0,), (0,)), ((), ()))
LOWEST = -1e30
REACH = 4
LEVELS = 32
LINKS = 24


def tile_iota(shape, axis):
    return lax.broadcasted_iota(jnp.int32, shape, axis)


def matmul(left, right, dims=NN):
    return lax.dot_general(left, right, dims, preferred_element_type=WIDE)


def as_column(row, eye, ones):
    return matmul((eye * row).astype(LOWF), ones)


def one_hot(condition):
    return jnp.where(condition, 1.0, 0.0).astype(LOWF)


def span(start, size, unit=16):
    return pl.ds(pl.multiple_of(start, unit), size)


def over(count, step):
    def run(index, carry):
        step(index)
        return carry

    lax.fori_loop(0, count, run, 0)


def flipped(value, mask, bits=4):
    total = 0
    for bit in range(bits):
        one, two = (value // 2**bit) % 2, (mask // 2**bit) % 2
        total = total + (one + two - 2 * one * two) * 2**bit
    return total


def copy_to(source, target, send_sem, recv_sem, where):
    return pltpu.make_async_remote_copy(
        src_ref=source,
        dst_ref=target,
        send_sem=send_sem,
        recv_sem=recv_sem,
        device_id=where,
        device_id_type=MESH,
    )


def send(source, target, send_sem, recv_sem, where):
    copy_to(source, target, send_sem, recv_sem, where).start()


def spread_rows(value):
    centred = value - jnp.mean(value, -1, keepdims=True)
    inverse = lax.rsqrt(jnp.mean(centred * centred, -1, keepdims=True) + EPSILON)
    return centred * inverse, inverse


def spread_back(unit, inverse, gain, grad):
    d_unit = grad * gain
    return inverse * (
        d_unit
        - jnp.mean(d_unit, -1, keepdims=True)
        - unit * jnp.mean(d_unit * unit, -1, keepdims=True)
    )


def windows(slots):
    found, at = [], 0
    for block in range(slots // TILE):
        low = max(0, block - REACH) * TILE
        width = (block + 1) * TILE - low
        found.append((block, low, width, at))
        at += width
    return found, at


def levels_of(groups):
    inner = 4 if groups % 4 == 0 else 1
    return inner, groups // inner


def shard_rows(rows, groups):
    return -(-rows // (groups * 16)) * 16


def part_scratch(name, rows, width, groups):
    inner, outer = levels_of(groups)
    shard = shard_rows(rows, groups)
    return {
        name + "_source": pltpu.VMEM((groups * shard, width), LOWF),
        name + "_plane": pltpu.VMEM((inner, outer * shard, width), LOWF),
        name + "_half": pltpu.VMEM((outer * shard, width), LOWF),
        name + "_column": pltpu.VMEM((outer, shard, width), LOWF),
        name + "_shard": pltpu.VMEM((shard, width), WIDE),
        name + "_whole": pltpu.VMEM((groups * shard, width), LOWF),
        name + "_plane_sent": DMA((inner,)),
        name + "_plane_came": DMA((inner,)),
        name + "_column_sent": DMA((outer,)),
        name + "_column_came": DMA((outer,)),
        name + "_out_sent": DMA((outer,)),
        name + "_ahead_sent": DMA((inner,)),
        name + "_ahead_came": DMA((inner,)),
        name + "_came": DMA((outer,)),
    }


class Part:
    def __init__(self, scratch, name, groups, me, core):
        for key, ref in vars(scratch).items():
            if key.startswith(name + "_"):
                setattr(self, key[len(name) + 1 :], ref)
        self.me, self.core = me, core
        self.inner, self.outer = levels_of(groups)
        self.i, self.o = me % self.inner, me // self.inner
        self.size = self.shard.shape[0]
        self.rounds = self.outer.bit_length() - 1

    def quarter(self, j):
        return span(j * self.outer * self.size, self.outer * self.size)

    def piece(self, j, o):
        return span((j * self.outer + o) * self.size, self.size)

    def plane_copy(self, j):
        return copy_to(
            self.source.at[self.quarter(j)],
            self.plane.at[self.i],
            self.plane_sent.at[j],
            self.plane_came.at[self.i],
            (self.o * self.inner + j, self.core),
        )

    def mate(self, bit):
        return self.o + (1 - 2 * (self.o // 2**bit % 2)) * 2**bit

    def column_copy(self, bit, index):
        mate = self.mate(bit)
        low = mate % 2 ** (bit + 1)
        source = low + index * 2 ** (bit + 1)
        slot = self.outer - self.outer // 2**bit + index
        return copy_to(
            self.half.at[span(source * self.size, self.size)],
            self.column.at[slot],
            self.column_sent.at[slot],
            self.column_came.at[slot],
            (mate * self.inner + self.i, self.core),
        )

    def out_copy(self, bit, index):
        o = self.o % 2 ** (bit + 1) + index * 2 ** (bit + 1)
        block = self.whole.at[self.piece(self.i, o)]
        return copy_to(
            block,
            block,
            self.out_sent.at[self.outer - self.outer // 2**bit + index],
            self.came.at[o],
            (self.mate(bit) * self.inner + self.i, self.core),
        )

    def ahead_copy(self, j):
        block = self.whole.at[self.quarter(self.i)]
        sent, came = self.ahead_sent.at[j], self.ahead_came.at[self.i]
        return copy_to(block, block, sent, came, (self.o * self.inner + j, self.core))

    def wait(self, ref, semaphore):
        copy_to(ref, ref, semaphore, semaphore, (self.me, self.core)).wait_recv()

    def fill(self, blocks, at=0):
        for block in blocks:
            self.source[at : at + block.shape[0], :] = block.astype(LOWF)
            at += block.shape[0]
        if at < self.source.shape[0]:
            shape = (self.source.shape[0] - at, self.source.shape[1])
            self.source[at:, :] = jnp.zeros(shape, LOWF)
        self.start()

    def start(self):
        over(self.inner - 1, lambda k: self.plane_copy((self.i + k + 1) % self.inner).start())

    def across(self):
        total = self.source[self.quarter(self.i), :].astype(WIDE)
        for k in range(self.inner - 1):
            j = (self.i + k + 1) % self.inner
            self.wait(self.plane.at[j], self.plane_came.at[j])
            total = total + self.plane[j].astype(WIDE)
        self.half[...] = total.astype(LOWF)
        self.halve(0)

    def halve(self, bit):
        over(self.outer // 2 ** (bit + 1), lambda k: self.column_copy(bit, k).start())

    def settle(self, bits):
        for bit in bits:
            count = self.outer // 2 ** (bit + 1)

            def take(k, bit=bit):
                slot = self.outer - self.outer // 2**bit + k
                self.wait(self.column.at[slot], self.column_came.at[slot])
                o = self.o % 2 ** (bit + 1) + k * 2 ** (bit + 1)
                at = span(o * self.size, self.size)
                total = self.half[at, :].astype(WIDE) + self.column[slot].astype(WIDE)
                self.half[at, :] = total.astype(LOWF)
                if bit == self.rounds - 1:
                    self.shard[...] = total
                    self.whole[self.piece(self.i, self.o), :] = total.astype(LOWF)

            over(count, take)
            if bit < self.rounds - 1:
                self.halve(bit + 1)
            else:
                self.double(bit)

    def double(self, bit):
        over(self.outer // 2 ** (bit + 1), lambda k: self.out_copy(bit, k).start())

    def forward(self, bits):
        for bit in bits:

            def step(k, bit=bit):
                o = self.mate(bit) % 2 ** (bit + 1) + k * 2 ** (bit + 1)
                self.wait(self.whole.at[self.piece(self.i, o)], self.came.at[o])

            over(self.outer // 2 ** (bit + 1), step)
            if bit > 0:
                self.double(bit - 1)
            else:
                over(self.inner - 1, lambda k: self.ahead_copy((self.i + k + 1) % self.inner).start())

    def collect(self):
        def step(k):
            j = (self.i + k + 1) % self.inner
            self.wait(self.whole.at[self.quarter(j)], self.ahead_came.at[j])

        over(self.inner - 1, step)

    def drain(self):
        over(self.inner - 1, lambda k: self.plane_copy((self.i + k + 1) % self.inner).wait_send())

        for bit in range(self.rounds):

            def far(k, bit=bit):
                self.column_copy(bit, k).wait_send()
                self.out_copy(bit, k).wait_send()

            over(self.outer // 2 ** (bit + 1), far)

        over(self.inner - 1, lambda k: self.ahead_copy((self.i + k + 1) % self.inner).wait_send())


def part_rows(width, heads_width, hidden, places):
    return {
        "early": heads_width + 2 * hidden,
        "late": 3 * width + places // 2,
    }


def step_scratch(groups, held, entries, width, heads_width, hidden, places):
    slots = entries // 2
    own = slots // 2
    pairs = heads_width // TILE
    area = windows(slots)[1]
    blocks = slots // TILE
    padded = -(-2 * held // TILE) * TILE
    bank = entries // TILE // 2
    shapes = {
        "table": ((padded, width), LOWF),
        "flat": ((1, entries), jnp.int32),
        "want": ((groups, 8, TILE), jnp.int32),
        "asked": ((groups, 8, TILE), jnp.int32),
        "reqs": ((2, entries // TILE, TILE), jnp.int32),
        "leaving": ((2, bank, TILE, width), LOWF),
        "arrived": ((2, 2, bank, TILE, width), LOWF),
        "landed": ((2, 2, bank, TILE, width), LOWF),
        "cands": ((slots, width), LOWF),
        "w_out": ((2, heads_width, width), LOWF),
        "w_up": ((2, width, hidden), LOWF),
        "w_down": ((2, hidden, width), LOWF),
        "w_in": ((3, width, heads_width), LOWF),
        "place_row": ((1, slots), jnp.int32),
        "bias": ((area, TILE), WIDE),
        "pos_high": ((places, width), LOWF),
        "pos_low": ((places, width), LOWF),
        "first": ((own, width), WIDE),
        "normed": ((slots, width), LOWF),
        "normed_t": ((width, slots), LOWF),
        "queries": ((pairs, blocks, 2 * TILE, TILE), LOWF),
        "keys": ((pairs, slots, TILE), LOWF),
        "values": ((pairs, slots, TILE), LOWF),
        "keys_t": ((pairs, TILE, slots), LOWF),
        "values_t": ((pairs, TILE, slots), LOWF),
        "probs": ((pairs, area, 2 * TILE), WIDE),
        "scales": ((pairs, max(8, blocks), 2 * TILE), WIDE),
        "mixed": ((pairs, slots, TILE), LOWF),
        "mixed_in": ((pairs, own, TILE), LOWF),
        "joined": ((2, own, heads_width), LOWF),
        "unit_zero": ((own, width), WIDE),
        "inverse_zero": ((own, TILE), WIDE),
        "unit_one": ((own, width), WIDE),
        "inverse_one": ((own, TILE), WIDE),
        "lifted": ((own, width), LOWF),
        "hidden": ((2, own, hidden), LOWF),
        "unit_two": ((own, width), WIDE),
        "inverse_two": ((own, TILE), WIDE),
        "final": ((own, width), LOWF),
        "logit_bias": ((1, slots), WIDE),
        "d_logits": ((own, slots), LOWF),
        "d_third": ((own, width), WIDE),
        "d_branch": ((own, width), LOWF),
        "d_inner": ((2, own, hidden), LOWF),
        "d_second": ((own, width), WIDE),
        "d_mixed": ((own, width), LOWF),
        "d_heads": ((pairs, slots, TILE), LOWF),
        "d_heads_out": ((pairs, own, TILE), LOWF),
        "d_cand": ((slots * width // TILE, TILE), WIDE),
        "g_out": ((heads_width, width), WIDE),
        "g_up": ((width, hidden), WIDE),
        "g_down": ((hidden, width), WIDE),
        "g_out_out": ((heads_width, width), LOWF),
        "g_up_out": ((width, hidden), LOWF),
        "g_down_out": ((hidden, width), LOWF),
        "g_out_in": ((heads_width, width), LOWF),
        "g_up_in": ((width, hidden), LOWF),
        "g_down_in": ((hidden, width), LOWF),
        "d_keys": ((pairs, slots, TILE), WIDE),
        "d_values": ((pairs, slots, TILE), WIDE),
        "d_triple": ((3, slots, heads_width), LOWF),
        "d_normed_in": ((own, width), WIDE),
        "d_rows": ((entries, width), LOWF),
        "few": ((8, width), WIDE),
        "few_in": ((8, width), WIDE),
        "few_all": ((groups, 8, width), WIDE),
        "other_half": ((places // 2, width), LOWF),
    }
    scratch = {name: pltpu.VMEM(*entry) for name, entry in shapes.items()}
    for name in ("want", "row", "few", "land"):
        scratch[name + "_sent"] = DMA((groups,))
        scratch[name + "_came"] = DMA((groups,))
    for name in ("pass", "hand"):
        scratch[name + "_sent"] = DMA((bank,))
        scratch[name + "_came"] = DMA((bank,))
    scratch["sent"] = DMA((LINKS,))
    scratch["came"] = DMA((LINKS,))
    scratch["loads"] = DMA((24,))
    for name, rows in part_rows(width, heads_width, hidden, places).items():
        scratch.update(part_scratch(name, rows, width, groups))
    return scratch


def step_kernel(groups, keeps, names, *refs):
    (own_ref, off_ref, seg_ref, live_ref, logq_ref, gain_ref) = refs[:6]
    count = 18 if keeps else 6
    fars, refs = refs[6 : 6 + count], refs[6 + count :]
    table_far, in_far, out_far, up_far, down_far, pos_far = fars[:: count // 6]
    (table_ref, down_ref, mid_ref, inward_ref, position_ref, few_ref, stats_ref) = refs[:7]
    nears, refs = (refs[7:25], refs[25:]) if keeps else (None, refs[7:])
    s = types.SimpleNamespace(**dict(zip(names, refs)))
    me, core = lax.axis_index("dp"), lax.axis_index("ffn")
    other = 1 - core
    held, width = table_far.shape
    entries = own_ref.shape[1]
    slots = entries // 2
    own = slots // 2
    half = entries // groups
    share = TILE // half
    tiles = entries // TILE
    spans = entries // GROUP
    pairs, hidden, places = s.keys.shape[0], s.w_up.shape[2], pos_far.shape[0]
    heads_width = pairs * TILE
    mine, yours = span(core * own, own), span(other * own, own)
    early, late = sums = [Part(s, name, groups, me, core) for name in ("early", "late")]

    barrier = pltpu.get_barrier_semaphore()
    slot_of = me * 2 + core

    def greet(k):
        where = (slot_of + k + 1) % (2 * groups)
        pl.semaphore_signal(
            barrier, inc=1, device_id=(where // 2, where % 2), device_id_type=MESH
        )

    over(2 * groups - 1, greet)
    spare = s.probs.at[0]
    s.d_cand_in = s.bias.at[pl.ds(0, slots * width // TILE)]
    s.column = s.probs.at[1, pl.ds(slots, slots), pl.ds(0, TILE)]
    s.segments = s.probs.at[1, pl.ds(slots, slots), pl.ds(TILE, TILE)]
    s.place = s.probs.at[1, pl.ds(2 * slots, slots), pl.ds(0, TILE)]
    s.total = s.d_normed = s.probs.at[1, pl.ds(0, slots)]
    s.grad_table = spare.at[pl.ds(0, held)]
    pieces = [table_far, out_far]
    pieces += [up_far.at[:, pl.ds(c * width, width)] for c in range(hidden // width)]
    pieces += [down_far, *(in_far.at[c] for c in range(3)), pos_far]
    loads, staged, at = [], [], 0
    if keeps:
        targets = [nears[0], nears[6]]
        targets += [nears[9].at[:, pl.ds(c * width, width)] for c in range(hidden // width)]
        targets += [nears[12], *(nears[3].at[c] for c in range(3)), nears[15]]
    for index, piece in enumerate(pieces):
        near = targets[index] if keeps else spare.at[pl.ds(at, piece.shape[0])]
        at += piece.shape[0]
        staged.append(near)
        loads.append(pltpu.make_async_copy(piece, near, s.loads.at[index]))
    for load in loads:
        load.start()

    def swap(index, source, target):
        send(source, target, s.sent.at[index], s.came.at[index], (me, other))

    def arrived(ref, semaphore):
        copy_to(ref, ref, semaphore, semaphore, (me, core)).wait_recv()

    def departed(ref, semaphore):
        copy_to(ref, ref, semaphore, semaphore, (me, core)).wait_send()

    def swapped(index, target):
        arrived(target, s.came.at[index])

    upper = one_hot(tile_iota((GROUP, GROUP), 0) <= tile_iota((GROUP, GROUP), 1))
    group_of = tile_iota((groups, GROUP), 0)
    before = jnp.zeros((groups, 1), WIDE)
    filled = jnp.zeros((3 * groups, TILE), WIDE)
    spot = (me % share) * half - core * half
    for chunk in range(spans):
        at = slice(chunk * GROUP, (chunk + 1) * GROUP)
        owner, offset = own_ref[:, at], off_ref[:, at]
        marks = jnp.where(group_of == owner, 1.0, 0.0)
        running = matmul(marks.astype(LOWF), upper) + before
        before = running[:, GROUP - 1 :]
        ranks = (jnp.sum(marks * running, 0, keepdims=True) - 1.0).astype(jnp.int32)
        slot = owner * half + ranks
        s.flat[:, at] = jnp.where(ranks < half, slot, slot + (entries - half))
        inside = (ranks >= core * half) & (ranks < core * half + half)
        picks = one_hot(tile_iota((TILE, GROUP), 0) == jnp.where(inside, ranks + spot, -1))
        parts = jnp.concatenate(
            [
                marks * lax.shift_right_logical(offset, 6).astype(WIDE),
                marks * (offset & 63).astype(WIDE),
                marks,
            ],
            0,
        ).astype(LOWF)
        filled = filled + matmul(parts, picks, NT)
    asking = (
        64.0 * filled[:groups] + filled[groups : 2 * groups] + filled[2 * groups :]
    ).astype(jnp.int32)
    for owner in range(groups):
        s.want[owner] = jnp.broadcast_to(asking[owner : owner + 1], (8, TILE))
    s.asked[me] = s.want[me]
    pl.semaphore_wait(barrier, 2 * groups - 1)

    def ask(k):
        owner = (me + groups // 2 + k) % groups

        @pl.when(owner != me)
        def _():
            send(
                s.want.at[owner], s.asked.at[me], s.want_sent.at[owner], s.want_came.at[me], (owner, core)
            )

    over(groups, ask)
    rows_mine, rows_yours = span(core * held, held), span(other * held, held)
    loads[0].wait()
    s.table[rows_mine, :] = staged[0][...].astype(LOWF)
    s.table[2 * held :, :] = jnp.zeros((s.table.shape[0] - 2 * held, width), LOWF)
    swap(0, s.table.at[rows_mine], s.table.at[rows_mine])
    eye = (tile_iota((TILE, TILE), 0) == tile_iota((TILE, TILE), 1)).astype(WIDE)
    ones = jnp.ones((TILE, TILE), LOWF)

    def column_of(line):
        return 64.0 * as_column(lax.shift_right_logical(line, 6).astype(WIDE), eye, ones) + as_column(
            (line & 63).astype(WIDE), eye, ones
        )

    for chunk in range(slots // TILE):
        side, at = divmod(chunk * TILE, own)
        line = s.flat[:, span(side * slots + core * own + at, TILE, TILE)]
        s.column[chunk * TILE : (chunk + 1) * TILE, :] = column_of(line)
    s.total[...] = jnp.zeros(s.total.shape, WIDE)
    swapped(0, s.table.at[rows_yours])
    lanes_wide = tile_iota((TILE, TILE), 1).astype(WIDE)

    bank = tiles // 2

    def seat(number):
        tile = number // share
        return tile // bank, tile % bank, span(number % share * half, half)

    def ship(tile, picked, buffer, sent, came):
        s.leaving[tile // bank, tile % bank] = picked
        for j in range(share):
            number = tile * share + j

            @pl.when(number != me)
            def _():
                block = s.leaving.at[seat(number)]
                send(block, buffer.at[(core, *seat(me))], sent.at[number], came.at[me], (number, core))

            @pl.when(number == me)
            def _():
                buffer[(core, *seat(me))] = picked[j * half : (j + 1) * half]

    def serve(tile):
        line = jnp.zeros((1, TILE), jnp.int32)
        for j in range(share):
            source = tile * share + j

            @pl.when(source != me)
            def _():
                arrived(s.asked.at[source], s.want_came.at[source])

        for j in range(share):
            line = line + s.asked[tile * share + j][0:1, :]
        s.reqs[core, pl.ds(tile, 1), :] = line
        number = column_of(line)
        hot = jnp.concatenate(
            [
                one_hot(number == lanes_wide + float(b * TILE + 1))
                for b in range(s.table.shape[0] // TILE)
            ],
            1,
        )
        picked = matmul(hot, s.table[...]).astype(LOWF)
        ship(tile, picked, s.arrived, s.row_sent, s.row_came)

    keep = []
    if keeps:
        for i in range(12):
            index = i // 2 * 3 + 1 + i % 2
            keep.append(pltpu.make_async_copy(fars[index], nears[index], s.loads.at[12 + i]))
    found, _ = windows(slots)
    live = live_ref[0]
    first_lanes = (tile_iota((1, TILE), 1) < HEAD).astype(WIDE)
    pick = [first_lanes.astype(LOWF), (1.0 - first_lanes).astype(LOWF)]
    gain = [gain_ref[g : g + 1, :] for g in range(3)]
    step = 2 * TILE


    def prepare():
        for load in loads[1:]:
            load.wait()
        for copy in keep:
            copy.start()
        s.w_out[core] = staged[1][...].astype(LOWF)
        ups = hidden // width
        for c in range(ups):
            s.w_up[core, :, c * width : (c + 1) * width] = staged[2 + c][...].astype(LOWF)
        s.w_down[core] = staged[2 + ups][...].astype(LOWF)
        for c in range(3):
            s.w_in[c] = staged[3 + ups + c][...].astype(LOWF)
        high = staged[-1][...].astype(LOWF)
        s.pos_high[...] = high
        s.pos_low[...] = (staged[-1][...] - high.astype(WIDE)).astype(LOWF)
        seg = seg_ref[...]
        level = tile_iota((LEVELS, slots), 0)
        starts = jnp.sum(jnp.where(seg < level, 1.0, 0.0), 1, keepdims=True)
        start = jnp.sum(jnp.where(seg == level, starts, 0.0), 0, keepdims=True)
        place_row = tile_iota((1, slots), 1) - start.astype(jnp.int32)
        s.place_row[...] = place_row
        seg_wide = seg.astype(WIDE)
        for b in range(slots // TILE):
            at = slice(b * TILE, (b + 1) * TILE)
            s.segments[at, :] = as_column(seg_wide[:, at], eye, ones)
            s.place[at, :] = column_of(place_row[:, at])
        causal = tile_iota((TILE, TILE), 0) <= tile_iota((TILE, TILE), 1)
        for b, low, wide, at in found:
            line = seg_wide[:, b * TILE : (b + 1) * TILE]
            for t in range(wide // TILE):
                same = s.segments[low + t * TILE : low + (t + 1) * TILE, :] == line
                if low + t * TILE == b * TILE:
                    same = same & causal
                s.bias[at + t * TILE : at + (t + 1) * TILE, :] = jnp.where(same, 0.0, LOWEST)
        alive_row = tile_iota((1, slots), 1) < live
        s.logit_bias[...] = jnp.where(alive_row, -logq_ref[...], LOWEST)
        for index, block in enumerate((s.w_out, s.w_up, s.w_down)):
            swap(2 + index, block.at[core], block.at[core])

    def spot_of(h):
        return flipped(me // share % bank, bank - 1 - h)

    def pair_of(buffer, side, spot):
        return jnp.concatenate([buffer[side, 0, spot], buffer[side, 1, spot]], 0)

    def lay(side, spot):
        lane = tile_iota((slots, TILE), 1).astype(WIDE)
        firsts = [(side * entries + (spot + b * bank) * TILE).astype(WIDE) for b in range(2)]
        hot = jnp.concatenate([one_hot(s.column[...] - first == lane) for first in firsts], 1)
        s.total[...] += matmul(hot, pair_of(s.arrived, side, spot))

    def trade(ahead, give, buffer, came, sent_on, passed, use, between):
        def other_two(h):
            spot = spot_of(h)
            arrived(buffer.at[other, :, spot], passed.at[spot])
            use(other, spot)

        def receive(h):
            spot = spot_of(h)
            for b in range(2):
                for j in range(share):
                    number = (spot + b * bank) * share + j

                    @pl.when(number != me)
                    def _():
                        arrived(buffer.at[(core, *seat(number))], came.at[number])

            block = buffer.at[core, :, spot]
            send(block, block, sent_on.at[spot], passed.at[spot], (me, other))
            use(core, spot)
            pl.when(h > 0)(lambda: other_two(h - 1))

        def step(h):
            @pl.when(h < bank)
            def _():
                spot = spot_of(h)
                far = 1 - me // share // bank
                give(spot + far * bank)
                give(spot + (1 - far) * bank)

            between(h)
            pl.when(h >= ahead)(lambda: receive(h - ahead))

        over(bank + ahead, step)
        other_two(jnp.int32(bank - 1))

    trade(3, serve, s.arrived, s.row_came, s.pass_sent, s.pass_came, lay, lambda h: pl.when(h == 2)(prepare))
    swap(1, s.reqs.at[core], s.reqs.at[core])
    s.cands[mine, :] = s.total[own:, :].astype(LOWF)
    swap(5, s.cands.at[mine], s.cands.at[mine])

    def enter(r):
        at = span(r * step, step)
        full = span(core * own + r * step, step, TILE)
        where = s.place[full, :]
        lane = tile_iota((step, TILE), 1).astype(WIDE)
        hot = jnp.concatenate(
            [one_hot(where == lane + float(t * TILE)) for t in range(places // TILE)], 1
        )
        first = s.total[at, :] + matmul(hot, s.pos_high[...]) + matmul(hot, s.pos_low[...])
        s.first[at, :] = first
        unit, inverse = spread_rows(first)
        s.unit_zero[at, :] = unit
        s.inverse_zero[at, :] = jnp.broadcast_to(inverse, (step, TILE))
        s.normed[full, :] = (unit * gain[0]).astype(LOWF)

    over(own // step, enter)
    swap(6, s.normed.at[mine], s.normed.at[mine])

    def project(k):
        @pl.when(k == own // step)
        def _():
            swapped(6, s.normed.at[yours])

        block = (core * (own // step) + k) % (slots // step)
        full = span(block * step, step, TILE)
        normed = s.normed[full, :]
        s.normed_t[:, full] = normed.astype(WIDE).T.astype(LOWF)
        query = (matmul(normed, s.w_in[0]) * SCALE).astype(LOWF)
        keys = matmul(normed, s.w_in[1]).astype(LOWF)
        values = matmul(normed, s.w_in[2]).astype(LOWF)
        keys_t = keys.astype(WIDE).T.astype(LOWF)
        values_t = values.astype(WIDE).T.astype(LOWF)
        for hp in range(pairs):
            lanes = slice(hp * TILE, (hp + 1) * TILE)
            s.keys[hp, full, :] = keys[:, lanes]
            s.values[hp, full, :] = values[:, lanes]
            s.keys_t[hp, :, full] = keys_t[lanes, :]
            s.values_t[hp, :, full] = values_t[lanes, :]
            for i in range(step // TILE):
                part = query[i * TILE : (i + 1) * TILE, lanes]
                for h in range(2):
                    s.queries[hp, block * (step // TILE) + i, h * TILE : (h + 1) * TILE, :] = (
                        part * pick[h]
                    )

    over(slots // step, project)

    def attend(hp):
        for b, low, wide, at in found:
            scores = matmul(s.keys[hp, low : low + wide, :], s.queries[hp, b], NT)
            bias = s.bias[at : at + wide, :]
            scores = scores + jnp.concatenate([bias, bias], 1)
            expo = jnp.exp(scores - jnp.max(scores, 0, keepdims=True))
            scale = 1.0 / jnp.sum(expo, 0, keepdims=True)
            s.scales[hp, b : b + 1, :] = scale
            s.probs[hp, at : at + wide, :] = expo
            out = matmul(s.values_t[hp, :, low : low + wide], expo.astype(LOWF)) * scale
            out = jnp.concatenate([out[:HEAD, :TILE], out[HEAD:, TILE:]], 0)
            s.mixed[hp, b * TILE : (b + 1) * TILE, :] = out.T.astype(LOWF)
        swap(7 + hp, s.mixed.at[hp, yours], s.mixed_in.at[hp])

    over(pairs, attend)
    for index, block in enumerate((s.w_out, s.w_up, s.w_down)):
        swapped(2 + index, block.at[other])
    over(bank, lambda spot: departed(s.arrived.at[core, :, spot], s.pass_sent.at[spot]))
    for hp in range(pairs):
        swapped(7 + hp, s.mixed_in.at[hp])

    def slopes(side, q, r):
        buffer = (s.d_keys, s.d_values)[side]
        fold = slots // own
        return buffer.at[q // fold, span(q % fold * own + r * step, step)]

    def feed(r):
        at = span(r * step, step)
        full = span(core * own + r * step, step, TILE)
        here = jnp.concatenate([s.mixed[hp, full, :] for hp in range(pairs)], 1)
        there = jnp.concatenate([s.mixed_in[hp, at, :] for hp in range(pairs)], 1)
        s.joined[core, at, :] = here
        s.joined[other, at, :] = there
        second = s.first[at, :] + matmul(here, s.w_out[core]) + matmul(there, s.w_out[other])
        unit, inverse = spread_rows(second)
        s.unit_one[at, :] = unit
        s.inverse_one[at, :] = jnp.broadcast_to(inverse, (step, TILE))
        lifted = (unit * gain[1]).astype(LOWF)
        s.lifted[at, :] = lifted
        third = second
        for side in range(2):
            inner = matmul(lifted, s.w_up[side])
            square = inner * inner
            bend = jnp.tanh(GELU_A * inner * (1.0 + GELU_B * square))
            gate = 0.5 * (1.0 + bend)
            act = (inner * gate).astype(LOWF)
            s.hidden[side, at, :] = act
            slope = gate + 0.5 * inner * (1.0 - bend * bend) * (
                GELU_A * (1.0 + 3.0 * GELU_B * square)
            )
            for q in range(hidden // TILE):
                slopes(side, q, r)[...] = slope[:, q * TILE : (q + 1) * TILE]
            third = third + matmul(act, s.w_down[side])
        unit, inverse = spread_rows(third)
        s.unit_two[at, :] = unit
        s.inverse_two[at, :] = jnp.broadcast_to(inverse, (step, TILE))
        s.final[at, :] = (unit * gain[2]).astype(LOWF)

    over(own // step, feed)
    s.few[...] = jnp.zeros((8, width), WIDE)
    swapped(5, s.cands.at[yours])

    def choose(r):
        at = span(r * TILE, TILE)
        here = span(core * own + r * TILE, TILE, TILE)
        final = s.final[at, :]
        logits = matmul(final, s.cands[...], NT) + s.logit_bias[...]
        square = matmul(final, s.cands[here, :], NT) + s.logit_bias[:, here]
        same = tile_iota((TILE, TILE), 0) == tile_iota((TILE, TILE), 1)
        number = tile_iota((TILE, 1), 0) + (core * own + r * TILE)
        top = jnp.max(logits, -1, keepdims=True)
        expo = jnp.exp(logits - top)
        total = jnp.sum(expo, -1, keepdims=True)
        alive = number < live
        right = jnp.sum(jnp.where(same, square, 0.0), -1, keepdims=True)
        loss = jnp.sum(jnp.where(alive, top + jnp.log(total) - right, 0.0))
        s.few[3:4, :] += jnp.full((1, width), loss, WIDE)
        alive = jnp.where(alive, 1.0, 0.0)
        scale = alive / total
        s.d_logits[at, :] = (expo * scale).astype(LOWF)
        square = jnp.exp(square - top) * scale - jnp.where(same, alive, 0.0)
        s.d_logits[at, here] = square.astype(LOWF)
        grad = s.d_logits[at, :]
        d_final = matmul(grad, s.cands[...])
        unit = s.unit_two[at, :]
        s.few[2:3, :] += jnp.sum(d_final * unit, 0, keepdims=True)
        d_third = spread_back(unit, s.inverse_two[at, :1], gain[2], d_final)
        s.d_third[at, :] = d_third
        s.d_branch[at, :] = d_third.astype(LOWF)

    over(own // TILE, choose)
    s.g_down_out[...] = matmul(s.hidden[other], s.d_branch[...], TN).astype(LOWF)
    swap(11, s.g_down_out, s.g_down_in)
    d_cand = matmul(s.d_logits[...], s.final[...], TN)
    for c in range(width // TILE):
        s.d_cand[c * slots : (c + 1) * slots, :] = d_cand[:, c * TILE : (c + 1) * TILE]
    swap(14, s.d_cand, s.d_cand_in)
    s.g_down[...] = matmul(s.hidden[core], s.d_branch[...], TN)

    def feed_back(r):
        at = span(r * step, step)
        full = span(core * own + r * step, step, TILE)
        d_lifted = jnp.zeros((step, width), WIDE)
        for side in range(2):
            d_hidden = matmul(s.d_branch[at, :], s.w_down[side], NT)
            slope = jnp.concatenate([slopes(side, q, r)[...] for q in range(hidden // TILE)], 1)
            d_inner = (d_hidden * slope).astype(LOWF)
            s.d_inner[side, at, :] = d_inner
            d_lifted = d_lifted + matmul(d_inner, s.w_up[side], NT)
        unit = s.unit_one[at, :]
        s.few[1:2, :] += jnp.sum(d_lifted * unit, 0, keepdims=True)
        d_second = s.d_third[at, :] + spread_back(unit, s.inverse_one[at, :1], gain[1], d_lifted)
        s.d_second[at, :] = d_second
        d_mixed = d_second.astype(LOWF)
        s.d_mixed[at, :] = d_mixed
        here = matmul(d_mixed, s.w_out[core], NT).astype(LOWF)
        there = matmul(d_mixed, s.w_out[other], NT).astype(LOWF)
        for hp in range(pairs):
            lanes = slice(hp * TILE, (hp + 1) * TILE)
            s.d_heads[hp, full, :] = here[:, lanes]
            s.d_heads_out[hp, at, :] = there[:, lanes]

    over(own // step, feed_back)
    for hp in range(pairs):
        swap(9 + hp, s.d_heads_out.at[hp], s.d_heads.at[hp, mine])
    s.g_up_out[...] = matmul(s.lifted[...], s.d_inner[other], TN).astype(LOWF)
    swap(12, s.g_up_out, s.g_up_in)
    s.g_out_out[...] = matmul(s.joined[other], s.d_mixed[...], TN).astype(LOWF)
    swap(13, s.g_out_out, s.g_out_in)
    s.g_up[...] = matmul(s.lifted[...], s.d_inner[core], TN)
    s.g_out[...] = matmul(s.joined[core], s.d_mixed[...], TN)
    s.d_keys[...] = jnp.zeros(s.d_keys.shape, WIDE)
    s.d_values[...] = jnp.zeros(s.d_values.shape, WIDE)

    def give_mid():
        swapped(11, s.g_down_in)
        swapped(12, s.g_up_in)
        swapped(13, s.g_out_in)
        g_up = s.g_up[...] + s.g_up_in[...].astype(WIDE)
        early.fill(
            (
                s.g_out[...] + s.g_out_in[...].astype(WIDE),
                *(g_up[:, c * width : (c + 1) * width] for c in range(hidden // width)),
                s.g_down[...] + s.g_down_in[...].astype(WIDE),
            )
        )

    give_mid()
    for hp in range(pairs):
        swapped(9 + hp, s.d_heads.at[hp, yours])

    def attend_back(hp):
        for b, low, wide, at in found:
            d_block = s.d_heads[hp, b * TILE : (b + 1) * TILE, :]
            d_pair = jnp.concatenate([d_block * pick[0], d_block * pick[1]], 0)
            d_prob = matmul(s.values[hp, low : low + wide, :], d_pair, NT)
            prob = s.probs[hp, at : at + wide, :] * s.scales[hp, b : b + 1, :]
            mean = jnp.sum(prob * d_prob, 0, keepdims=True)
            d_scores = (prob * (d_prob - mean)).astype(LOWF)
            s.d_keys[hp, low : low + wide, :] += matmul(d_scores, s.queries[hp, b])
            s.d_values[hp, low : low + wide, :] += matmul(prob.astype(LOWF), d_pair)
            out = matmul(s.keys_t[hp, :, low : low + wide], d_scores)
            out = jnp.concatenate([out[:HEAD, :TILE], out[HEAD:, TILE:]], 0) * SCALE
            lanes = span(hp * TILE, TILE, TILE)
            s.d_triple[0, b * TILE : (b + 1) * TILE, lanes] = out.T.astype(LOWF)


    over(pairs, attend_back)
    for hp in range(pairs):
        lanes = slice(hp * TILE, (hp + 1) * TILE)
        s.d_triple[1, :, lanes] = s.d_keys[hp].astype(LOWF)
        s.d_triple[2, :, lanes] = s.d_values[hp].astype(LOWF)
    for side in (yours, mine):
        d_normed = matmul(s.d_triple[0, side, :], s.w_in[0], NT)
        for c in range(1, 3):
            d_normed = d_normed + matmul(s.d_triple[c, side, :], s.w_in[c], NT)
        s.d_normed[side, :] = d_normed
        if side is yours:
            swap(15, s.d_normed.at[yours], s.d_normed_in)
    for c in range(3):
        g_in = matmul(s.normed_t[...], s.d_triple[c])
        late.source[c * width : (c + 1) * width, :] = g_in.astype(LOWF)
    early.across()
    swapped(15, s.d_normed_in)
    d_normed = s.d_normed[mine, :] + s.d_normed_in[...]
    unit = s.unit_zero[...]
    d_first = s.d_second[...] + spread_back(unit, s.inverse_zero[:, :1], gain[0], d_normed)
    s.d_rows[mine, :] = d_first.astype(LOWF)
    swap(16, s.d_rows.at[mine], s.d_rows.at[mine])
    s.few[0:1, :] = jnp.sum(d_normed * unit, 0, keepdims=True)
    s.few[4:5, :] = jnp.full((1, width), 0.5 * live.astype(WIDE), WIDE)
    swapped(14, s.d_cand_in)
    for c in range(width // TILE):
        at = pl.ds(c * slots, slots)
        s.d_rows[slots:, c * TILE : (c + 1) * TILE] = (s.d_cand[at, :] + s.d_cand_in[at, :]).astype(LOWF)
    over(
        groups - 1,
        lambda k: departed(
            s.leaving.at[seat((me + k + 1) % groups)], s.row_sent.at[(me + k + 1) % groups]
        ),
    )
    swapped(16, s.d_rows.at[yours])

    def give_rows(tile):
        number = s.flat[...] - (core * entries + tile * TILE)
        hot = one_hot(tile_iota((TILE, entries), 0) == number)
        picked = matmul(hot, s.d_rows[...]).astype(LOWF)
        ship(tile, picked, s.landed, s.land_sent, s.land_came)

    pos_half = places // 2

    def give_late():
        hot = one_hot(tile_iota((pos_half, slots), 0) + core * pos_half == s.place_row[...])
        late.fill((matmul(hot, s.d_rows[:slots, :]),), 3 * width)

    swapped(1, s.reqs.at[other])
    s.grad_table[...] = jnp.zeros(s.grad_table.shape, WIDE)

    def gather(side, spot):
        came = pair_of(s.landed, side, spot)
        first_row = core * held + 1
        lines = [s.reqs[side, pl.ds(spot + b * bank, 1), :] - first_row for b in range(2)]
        rows = tile_iota((held, TILE), 0)
        hot = jnp.concatenate([one_hot(rows == line) for line in lines], 1)
        s.grad_table[...] += matmul(hot, came)

    def between(h):
        first, last = range(late.rounds - 1), range(late.rounds - 1, late.rounds)
        back, end = range(late.rounds - 1, 0, -1), range(1)
        plan = {
            0: (give_late,),
            3: (lambda: early.settle(first),),
            4: (lambda: early.settle(last), late.across),
            5: (lambda: early.forward(back), lambda: late.settle(first)),
            6: (lambda: early.forward(end), lambda: late.settle(last)),
            7: (lambda: late.forward(back),),
            8: (lambda: late.forward(end),),
        }
        for at, acts in plan.items():
            for act in acts:
                pl.when(h == at)(act)

    trade(2, give_rows, s.landed, s.land_came, s.hand_sent, s.hand_came, gather, between)
    final = s.grad_table[...]
    table_ref[...] = final
    square = jnp.sum(final * final)
    for part in sums:
        square = square + jnp.sum(part.shard[...] * part.shard[...])
    s.few[5:6, :] = jnp.full((1, width), square, WIDE)
    swap(17, s.few, s.few_in)
    swapped(17, s.few_in)
    s.few_all[me] = s.few[...] + s.few_in[...]

    def few_copy(k):
        where = (me + k + 1) % groups
        block = s.few_all.at[me]
        return copy_to(block, block, s.few_sent.at[where], s.few_came.at[me], (where, core))

    over(groups - 1, lambda k: few_copy(k).start())
    late.collect()
    position_own = late.whole.at[pl.ds(3 * width, pos_half)]
    swap(18, position_own, s.other_half)
    early.collect()
    mid_ref[...] = early.whole[: mid_ref.shape[0], :]
    down_ref[...] = early.whole[mid_ref.shape[0] : mid_ref.shape[0] + hidden, :]
    inward_ref[...] = late.whole[: 3 * width, :]
    position_ref[span(core * pos_half, pos_half), :] = late.whole[3 * width : 3 * width + pos_half, :]
    swapped(18, s.other_half)
    position_ref[span(other * pos_half, pos_half), :] = s.other_half[...]

    for copy in keep:
        copy.wait()
    for part in sums:
        part.drain()

    def finish(k):
        where = (me + k + 1) % groups
        departed(s.want.at[where], s.want_sent.at[where])
        departed(s.leaving.at[seat(where)], s.land_sent.at[where])

    over(groups - 1, finish)

    over(bank, lambda spot: departed(s.landed.at[core, :, spot], s.hand_sent.at[spot]))
    ends = [s.table.at[rows_mine], s.reqs.at[core], s.w_out.at[core], s.w_up.at[core], s.w_down.at[core]]
    ends += [s.cands.at[mine], s.normed.at[mine]]
    ends += [s.mixed.at[hp, yours] for hp in range(2)] + [s.d_heads_out.at[hp] for hp in range(2)]
    ends += [s.g_down_out, s.g_up_out, s.g_out_out, s.d_cand, s.d_normed.at[yours]]
    ends += [s.d_rows.at[mine], s.few]
    for index, ref in enumerate(ends):
        departed(ref, s.sent.at[index])

    def take_few(k):
        where = (me + k + 1) % groups
        arrived(s.few_all.at[where], s.few_came.at[where])

    over(groups - 1, take_few)
    few_total = s.few_all[0]
    for source in range(1, groups):
        few_total = few_total + s.few_all[source]
    few_ref[...] = few_total
    gains = few_total[:3]
    stats_ref[...] = jnp.sqrt(few_total[5:6, :TILE] + jnp.sum(gains * gains)) + jnp.zeros((8, TILE), WIDE)
    over(groups - 1, lambda k: few_copy(k).wait_send())
    departed(position_own, s.sent.at[18])


def in_hbm(array):
    return pltpu.with_memory_space_constraint(array, pltpu.HBM)


def run_step(trios, owners, offsets, seg, live, logq, gains, groups, keeps):
    table, _, attn_out, ffn_up, _, position = (trio[0] for trio in trios)
    held, width = table.shape
    entries = owners.shape[1]
    heads_width, hidden, places = attn_out.shape[0], ffn_up.shape[1], position.shape[0]
    scratch = step_scratch(groups, held, entries, width, heads_width, hidden, places)
    shape = pltpu.VMEM
    arrays = [array for trio in trios for array in (trio if keeps else trio[:1])]
    kept = arrays if keeps else []
    return pl.pallas_call(
        functools.partial(step_kernel, groups, keeps, tuple(scratch)),
        out_shape=(
            shape((held, width), WIDE),
            shape((hidden, width), LOWF),
            shape((heads_width + hidden, width), LOWF),
            shape((3 * width, width), LOWF),
            shape((places, width), LOWF),
            shape((8, width), WIDE),
            shape((8, TILE), WIDE),
            *(shape(array.shape, WIDE) for array in kept),
        ),
        in_specs=[VMEM] * 3 + [SMEM] + [VMEM] * 2 + [FAR] * len(arrays),
        out_specs=(VMEM,) * (7 + len(kept)),
        scratch_shapes=list(scratch.values()),
        compiler_params=pltpu.CompilerParams(
            collective_id=0, has_side_effects=True, vmem_limit_bytes=(50 if keeps else 60) * 1024 * 1024
        ),
    )(owners, offsets, seg, live, logq, gains, *(in_hbm(array) for array in arrays))


def adamw(weight, grad, first, second, decay, rate):
    first = BETA_ONE * first + (1.0 - BETA_ONE) * grad
    second = BETA_TWO * second + (1.0 - BETA_TWO) * grad * grad
    below = jnp.sqrt(second) + ADAM_EPS * (1.0 - BETA_TWO**STEP) ** 0.5
    pace = rate * (1.0 - BETA_TWO**STEP) ** 0.5 / (1.0 - BETA_ONE**STEP)
    return ((1.0 - rate * decay) * weight - pace * (first / below), first, second)


def update_kernel(kept, table_g, down_g, mid_g, inward_g, position_g, few_ref, stats_ref, *refs):
    inputs, outputs, buffers, trio_gains = refs[:21], refs[21:45], refs[45:63], refs[63:66]
    came, left, gains_came = refs[66:69]
    names = ("table", "in", "out", "up", "down", "position")
    ins = []
    if not kept:
        ins = [pltpu.make_async_copy(inputs[i], buffers[i], came.at[i]) for i in range(18)]
    outs = [pltpu.make_async_copy(buffers[i], outputs[i], left.at[i]) for i in range(18)]
    gains_in = [pltpu.make_async_copy(inputs[18 + i], trio_gains[i], gains_came.at[i]) for i in range(3)]
    for copy in ins + gains_in:
        copy.start()
    norm = stats_ref[0, 0]
    factor = CLIP / jnp.maximum(norm, CLIP)
    outputs[21][0, 0] = few_ref[3, 0]
    outputs[22][0, 0] = few_ref[4, 0]
    outputs[23][0, 0] = norm
    width = table_g.shape[1]
    for index, name in enumerate(names):
        trio = buffers[3 * index : 3 * index + 3]
        sources = inputs[3 * index : 3 * index + 3] if kept else trio
        for copy in ins[3 * index : 3 * index + 3]:
            copy.wait()
        rate = RATE_POSITION if name == "position" else RATE
        block = {"table": 112, "up": 32}.get(name, 64)
        lead = trio[0].shape[0] if name == "in" else 1
        rows, columns = trio[0].shape[-2:]
        heads_width, hidden = buffers[6].shape[0], buffers[9].shape[1]

        def run(r, block=block, name=name, trio=trio, sources=sources, rows=rows, rate=rate):
            at = span(r * block, block)

            def view(ref):
                return ref.at[r * block // rows, span(r * block % rows, block)] if name == "in" else ref.at[at]

            values = [view(ref)[...] for ref in sources]
            if name == "table":
                grad = table_g[at, :]
            elif name == "in":
                grad = inward_g[at, :].astype(WIDE)
            elif name == "out":
                grad = mid_g[at, :].astype(WIDE)
            elif name == "up":
                grad = jnp.concatenate(
                    [
                        mid_g[span(heads_width + c * width + r * block, block), :].astype(WIDE)
                        for c in range(hidden // width)
                    ],
                    1,
                )
            elif name == "down":
                grad = down_g[at, :].astype(WIDE)
            else:
                grad = position_g[at, :].astype(WIDE)
            made = adamw(values[0], grad * factor, values[1], values[2], DECAY, rate)
            for ref, value in zip(trio, made):
                view(ref)[...] = value

        over(lead * rows // block, run)
        for i in range(3):
            outs[3 * index + i].start()
    for copy in gains_in:
        copy.wait()
    gains = adamw(
        trio_gains[0][...],
        few_ref[0:3, :] * factor,
        trio_gains[1][...],
        trio_gains[2][...],
        0.0,
        RATE_GAINS,
    )
    for ref, value in zip(outputs[18:21], gains):
        ref[...] = value
    for copy in outs:
        copy.wait()


def run_update(grads, trios, kept):
    flat = [*kept] if kept else [in_hbm(array) for trio in trios[:6] for array in trio]
    flat += [in_hbm(array) for array in trios[6]]
    shape = jax.ShapeDtypeStruct
    scalar = shape((1, 1), WIDE)
    return pl.pallas_call(
        functools.partial(update_kernel, bool(kept)),
        out_shape=tuple(shape(a.shape, WIDE) for a in flat) + (scalar,) * 3,
        in_specs=[VMEM] * 7 + [VMEM if kept else FAR] * 18 + [FAR] * 3,
        out_specs=(FAR,) * 18 + (VMEM,) * 3 + (SMEM,) * 3,
        scratch_shapes=[pltpu.VMEM(a.shape, WIDE) for a in flat] + [DMA((18,)), DMA((18,)), DMA((3,))],
        compiler_params=pltpu.CompilerParams(vmem_limit_bytes=(24 if kept else 48) * 1024 * 1024),
    )(*grads, *flat)


def body(
    item_table,
    attn_in,
    attn_out,
    ffn_up,
    ffn_down,
    position_table,
    norm_gains,
    item_first,
    item_second,
    attn_in_first,
    attn_in_second,
    attn_out_first,
    attn_out_second,
    ffn_up_first,
    ffn_up_second,
    ffn_down_first,
    ffn_down_second,
    position_first,
    position_second,
    gains_first,
    gains_second,
    owner_group,
    row_offset,
    segment_ids,
    live_slots,
    log_freq,
):
    trios = (
        (item_table, item_first, item_second),
        (attn_in, attn_in_first, attn_in_second),
        (attn_out, attn_out_first, attn_out_second),
        (ffn_up, ffn_up_first, ffn_up_second),
        (ffn_down, ffn_down_first, ffn_down_second),
        (position_table, position_first, position_second),
        (norm_gains, gains_first, gains_second),
    )
    groups = lax.axis_size("dp")
    made = run_step(
        trios[:6],
        owner_group.reshape(1, -1),
        row_offset,
        segment_ids,
        live_slots,
        log_freq,
        norm_gains,
        groups,
        groups <= 16,
    )
    made = run_update(made[:7], trios, made[7:])
    return (*made[:21], *(scalar.reshape(()) for scalar in made[21:]))


def solution(mesh):
    return jax.shard_map(
        body,
        mesh=mesh,
        in_specs=(
            P(("dp", "ffn"), None),
            P(None, None, "ffn"),
            P("ffn", None),
            P(None, "ffn"),
            P("ffn", None),
            P(),
            P(),
            P(("dp", "ffn"), None),
            P(("dp", "ffn"), None),
            P(None, None, "ffn"),
            P(None, None, "ffn"),
            P("ffn", None),
            P("ffn", None),
            P(None, "ffn"),
            P(None, "ffn"),
            P("ffn", None),
            P("ffn", None),
            P(),
            P(),
            P(),
            P(),
            P("dp", None, None),
            P("dp", None),
            P("dp", None),
            P("dp"),
            P("dp", None),
        ),
        out_specs=(
            P(("dp", "ffn"), None),
            P(("dp", "ffn"), None),
            P(("dp", "ffn"), None),
            P(None, None, "ffn"),
            P(None, None, "ffn"),
            P(None, None, "ffn"),
            P("ffn", None),
            P("ffn", None),
            P("ffn", None),
            P(None, "ffn"),
            P(None, "ffn"),
            P(None, "ffn"),
            P("ffn", None),
            P("ffn", None),
            P("ffn", None),
            P(),
            P(),
            P(),
            P(),
            P(),
            P(),
            P(),
            P(),
            P(),
        ),
        check_vma=False,
    )
```

```python
import functools
import types

import jax
import jax.numpy as jnp
from jax import lax
from jax.experimental import pallas as pl
from jax.experimental.pallas import tpu as pltpu
from jax.sharding import PartitionSpec as P

HEAD = 64
STEP = 10
EPSILON = 1e-05
SCALE = 0.125
CLIP = 1.0
RATE = 0.05
RATE_POSITION = 0.3
RATE_GAINS = 0.5
DECAY = 0.01
BETA_ONE = 0.9
BETA_TWO = 0.999
ADAM_EPS = 1e-08
GELU_A = 0.7978845608028654
GELU_B = 0.044715
LOWF = jnp.bfloat16
WIDE = jnp.float32
MESH = pl.DeviceIdType.MESH
DMA = pltpu.SemaphoreType.DMA
VMEM = pl.BlockSpec(memory_space=pltpu.VMEM)
SMEM = pl.BlockSpec(memory_space=pltpu.SMEM)
FAR = pl.BlockSpec(memory_space=pltpu.HBM)
TILE = 128
GROUP = 256
NN = (((1,), (0,)), ((), ()))
NT = (((1,), (1,)), ((), ()))
TN = (((0,), (0,)), ((), ()))
LOWEST = -1e30
REACH = 4
LEVELS = 32
LINKS = 24


def tile_iota(shape, axis):
    return lax.broadcasted_iota(jnp.int32, shape, axis)


def matmul(left, right, dims=NN):
    return lax.dot_general(left, right, dims, preferred_element_type=WIDE)


def as_column(row, eye, ones):
    return matmul((eye * row).astype(LOWF), ones)


def one_hot(condition):
    return jnp.where(condition, 1.0, 0.0).astype(LOWF)


def span(start, size, unit=16):
    return pl.ds(pl.multiple_of(start, unit), size)


def over(count, step):
    def run(index, carry):
        step(index)
        return carry

    lax.fori_loop(0, count, run, 0)


def flipped(value, mask, bits=4):
    total = 0
    for bit in range(bits):
        one, two = (value // 2**bit) % 2, (mask // 2**bit) % 2
        total = total + (one + two - 2 * one * two) * 2**bit
    return total


def copy_to(source, target, send_sem, recv_sem, where):
    return pltpu.make_async_remote_copy(
        src_ref=source,
        dst_ref=target,
        send_sem=send_sem,
        recv_sem=recv_sem,
        device_id=where,
        device_id_type=MESH,
    )


def send(source, target, send_sem, recv_sem, where):
    copy_to(source, target, send_sem, recv_sem, where).start()


def spread_rows(value):
    centred = value - jnp.mean(value, -1, keepdims=True)
    inverse = lax.rsqrt(jnp.mean(centred * centred, -1, keepdims=True) + EPSILON)
    return centred * inverse, inverse


def spread_back(unit, inverse, gain, grad):
    d_unit = grad * gain
    return inverse * (
        d_unit
        - jnp.mean(d_unit, -1, keepdims=True)
        - unit * jnp.mean(d_unit * unit, -1, keepdims=True)
    )


def windows(slots):
    found, at = [], 0
    for block in range(slots // TILE):
        low = max(0, block - REACH) * TILE
        width = (block + 1) * TILE - low
        found.append((block, low, width, at))
        at += width
    return found, at


def levels_of(groups):
    inner = 4 if groups % 4 == 0 else 1
    return inner, groups // inner


def shard_rows(rows, groups):
    return -(-rows // (groups * 16)) * 16


def part_scratch(name, rows, width, groups):
    inner, outer = levels_of(groups)
    shard = shard_rows(rows, groups)
    return {
        name + "_source": pltpu.VMEM((groups * shard, width), LOWF),
        name + "_plane": pltpu.VMEM((inner, outer * shard, width), LOWF),
        name + "_half": pltpu.VMEM((outer * shard, width), LOWF),
        name + "_column": pltpu.VMEM((outer, shard, width), LOWF),
        name + "_shard": pltpu.VMEM((shard, width), WIDE),
        name + "_whole": pltpu.VMEM((groups * shard, width), LOWF),
        name + "_plane_sent": DMA((inner,)),
        name + "_plane_came": DMA((inner,)),
        name + "_column_sent": DMA((outer,)),
        name + "_column_came": DMA((outer,)),
        name + "_out_sent": DMA((outer,)),
        name + "_ahead_sent": DMA((inner,)),
        name + "_ahead_came": DMA((inner,)),
        name + "_came": DMA((outer,)),
    }


class Part:
    def __init__(self, scratch, name, groups, me, core):
        for key, ref in vars(scratch).items():
            if key.startswith(name + "_"):
                setattr(self, key[len(name) + 1 :], ref)
        self.me, self.core = me, core
        self.inner, self.outer = levels_of(groups)
        self.i, self.o = me % self.inner, me // self.inner
        self.size = self.shard.shape[0]
        self.rounds = self.outer.bit_length() - 1

    def quarter(self, j):
        return span(j * self.outer * self.size, self.outer * self.size)

    def piece(self, j, o):
        return span((j * self.outer + o) * self.size, self.size)

    def plane_copy(self, j):
        return copy_to(
            self.source.at[self.quarter(j)],
            self.plane.at[self.i],
            self.plane_sent.at[j],
            self.plane_came.at[self.i],
            (self.o * self.inner + j, self.core),
        )

    def mate(self, bit):
        return self.o + (1 - 2 * (self.o // 2**bit % 2)) * 2**bit

    def column_copy(self, bit, index):
        mate = self.mate(bit)
        low = mate % 2 ** (bit + 1)
        source = low + index * 2 ** (bit + 1)
        slot = self.outer - self.outer // 2**bit + index
        return copy_to(
            self.half.at[span(source * self.size, self.size)],
            self.column.at[slot],
            self.column_sent.at[slot],
            self.column_came.at[slot],
            (mate * self.inner + self.i, self.core),
        )

    def out_copy(self, bit, index):
        o = self.o % 2 ** (bit + 1) + index * 2 ** (bit + 1)
        block = self.whole.at[self.piece(self.i, o)]
        return copy_to(
            block,
            block,
            self.out_sent.at[self.outer - self.outer // 2**bit + index],
            self.came.at[o],
            (self.mate(bit) * self.inner + self.i, self.core),
        )

    def ahead_copy(self, j):
        block = self.whole.at[self.quarter(self.i)]
        sent, came = self.ahead_sent.at[j], self.ahead_came.at[self.i]
        return copy_to(block, block, sent, came, (self.o * self.inner + j, self.core))

    def wait(self, ref, semaphore):
        copy_to(ref, ref, semaphore, semaphore, (self.me, self.core)).wait_recv()

    def fill(self, blocks, at=0):
        for block in blocks:
            self.source[at : at + block.shape[0], :] = block.astype(LOWF)
            at += block.shape[0]
        if at < self.source.shape[0]:
            shape = (self.source.shape[0] - at, self.source.shape[1])
            self.source[at:, :] = jnp.zeros(shape, LOWF)
        self.start()

    def start(self):
        over(self.inner - 1, lambda k: self.plane_copy((self.i + k + 1) % self.inner).start())

    def across(self):
        total = self.source[self.quarter(self.i), :].astype(WIDE)
        for k in range(self.inner - 1):
            j = (self.i + k + 1) % self.inner
            self.wait(self.plane.at[j], self.plane_came.at[j])
            total = total + self.plane[j].astype(WIDE)
        self.half[...] = total.astype(LOWF)
        self.halve(0)

    def halve(self, bit):
        over(self.outer // 2 ** (bit + 1), lambda k: self.column_copy(bit, k).start())

    def settle(self, bits):
        for bit in bits:
            count = self.outer // 2 ** (bit + 1)

            def take(k, bit=bit):
                slot = self.outer - self.outer // 2**bit + k
                self.wait(self.column.at[slot], self.column_came.at[slot])
                o = self.o % 2 ** (bit + 1) + k * 2 ** (bit + 1)
                at = span(o * self.size, self.size)
                total = self.half[at, :].astype(WIDE) + self.column[slot].astype(WIDE)
                self.half[at, :] = total.astype(LOWF)
                if bit == self.rounds - 1:
                    self.shard[...] = total
                    self.whole[self.piece(self.i, self.o), :] = total.astype(LOWF)

            over(count, take)
            if bit < self.rounds - 1:
                self.halve(bit + 1)
            else:
                self.double(bit)

    def double(self, bit):
        over(self.outer // 2 ** (bit + 1), lambda k: self.out_copy(bit, k).start())

    def forward(self, bits):
        for bit in bits:

            def step(k, bit=bit):
                o = self.mate(bit) % 2 ** (bit + 1) + k * 2 ** (bit + 1)
                self.wait(self.whole.at[self.piece(self.i, o)], self.came.at[o])

            over(self.outer // 2 ** (bit + 1), step)
            if bit > 0:
                self.double(bit - 1)
            else:
                over(self.inner - 1, lambda k: self.ahead_copy((self.i + k + 1) % self.inner).start())

    def collect(self):
        def step(k):
            j = (self.i + k + 1) % self.inner
            self.wait(self.whole.at[self.quarter(j)], self.ahead_came.at[j])

        over(self.inner - 1, step)

    def drain(self):
        over(self.inner - 1, lambda k: self.plane_copy((self.i + k + 1) % self.inner).wait_send())

        for bit in range(self.rounds):

            def far(k, bit=bit):
                self.column_copy(bit, k).wait_send()
                self.out_copy(bit, k).wait_send()

            over(self.outer // 2 ** (bit + 1), far)

        over(self.inner - 1, lambda k: self.ahead_copy((self.i + k + 1) % self.inner).wait_send())


def part_rows(width, heads_width, hidden, places):
    return {
        "early": heads_width + 2 * hidden,
        "late": 3 * width + places // 2,
    }


def step_scratch(groups, held, entries, width, heads_width, hidden, places):
    slots = entries // 2
    own = slots // 2
    pairs = heads_width // TILE
    area = windows(slots)[1]
    blocks = slots // TILE
    padded = -(-2 * held // TILE) * TILE
    bank = entries // TILE // 2
    shapes = {
        "table": ((padded, width), LOWF),
        "flat": ((1, entries), jnp.int32),
        "want": ((groups, 8, TILE), jnp.int32),
        "asked": ((groups, 8, TILE), jnp.int32),
        "reqs": ((2, entries // TILE, TILE), jnp.int32),
        "leaving": ((2, bank, TILE, width), LOWF),
        "arrived": ((2, 2, bank, TILE, width), LOWF),
        "landed": ((2, 2, bank, TILE, width), LOWF),
        "cands": ((slots, width), LOWF),
        "w_out": ((2, heads_width, width), LOWF),
        "w_up": ((2, width, hidden), LOWF),
        "w_down": ((2, hidden, width), LOWF),
        "w_in": ((3, width, heads_width), LOWF),
        "place_row": ((1, slots), jnp.int32),
        "bias": ((area, TILE), WIDE),
        "pos_high": ((places, width), LOWF),
        "pos_low": ((places, width), LOWF),
        "first": ((own, width), WIDE),
        "normed": ((slots, width), LOWF),
        "normed_t": ((width, slots), LOWF),
        "queries": ((pairs, blocks, 2 * TILE, TILE), LOWF),
        "keys": ((pairs, slots, TILE), LOWF),
        "values": ((pairs, slots, TILE), LOWF),
        "keys_t": ((pairs, TILE, slots), LOWF),
        "values_t": ((pairs, TILE, slots), LOWF),
        "probs": ((pairs, area, 2 * TILE), WIDE),
        "scales": ((pairs, max(8, blocks), 2 * TILE), WIDE),
        "mixed": ((pairs, slots, TILE), LOWF),
        "mixed_in": ((pairs, own, TILE), LOWF),
        "joined": ((2, own, heads_width), LOWF),
        "unit_zero": ((own, width), WIDE),
        "inverse_zero": ((own, TILE), WIDE),
        "unit_one": ((own, width), WIDE),
        "inverse_one": ((own, TILE), WIDE),
        "lifted": ((own, width), LOWF),
        "hidden": ((2, own, hidden), LOWF),
        "unit_two": ((own, width), WIDE),
        "inverse_two": ((own, TILE), WIDE),
        "final": ((own, width), LOWF),
        "logit_bias": ((1, slots), WIDE),
        "d_logits": ((own, slots), LOWF),
        "d_third": ((own, width), WIDE),
        "d_branch": ((own, width), LOWF),
        "d_inner": ((2, own, hidden), LOWF),
        "d_second": ((own, width), WIDE),
        "d_mixed": ((own, width), LOWF),
        "d_heads": ((pairs, slots, TILE), LOWF),
        "d_heads_out": ((pairs, own, TILE), LOWF),
        "d_cand": ((slots * width // TILE, TILE), WIDE),
        "g_out": ((heads_width, width), WIDE),
        "g_up": ((width, hidden), WIDE),
        "g_down": ((hidden, width), WIDE),
        "g_out_out": ((heads_width, width), LOWF),
        "g_up_out": ((width, hidden), LOWF),
        "g_down_out": ((hidden, width), LOWF),
        "g_out_in": ((heads_width, width), LOWF),
        "g_up_in": ((width, hidden), LOWF),
        "g_down_in": ((hidden, width), LOWF),
        "d_keys": ((pairs, slots, TILE), WIDE),
        "d_values": ((pairs, slots, TILE), WIDE),
        "d_triple": ((3, slots, heads_width), LOWF),
        "d_normed_in": ((own, width), WIDE),
        "d_rows": ((entries, width), LOWF),
        "few": ((8, width), WIDE),
        "few_in": ((8, width), WIDE),
        "few_all": ((groups, 8, width), WIDE),
        "other_half": ((places // 2, width), LOWF),
    }
    scratch = {name: pltpu.VMEM(*entry) for name, entry in shapes.items()}
    for name in ("want", "row", "few", "land"):
        scratch[name + "_sent"] = DMA((groups,))
        scratch[name + "_came"] = DMA((groups,))
    for name in ("pass", "hand"):
        scratch[name + "_sent"] = DMA((bank,))
        scratch[name + "_came"] = DMA((bank,))
    scratch["sent"] = DMA((LINKS,))
    scratch["came"] = DMA((LINKS,))
    scratch["loads"] = DMA((24,))
    for name, rows in part_rows(width, heads_width, hidden, places).items():
        scratch.update(part_scratch(name, rows, width, groups))
    return scratch


def step_kernel(groups, keeps, names, *refs):
    (own_ref, off_ref, seg_ref, live_ref, logq_ref, gain_ref) = refs[:6]
    count = 18 if keeps else 6
    fars, refs = refs[6 : 6 + count], refs[6 + count :]
    table_far, in_far, out_far, up_far, down_far, pos_far = fars[:: count // 6]
    (table_ref, down_ref, mid_ref, inward_ref, position_ref, few_ref, stats_ref) = refs[:7]
    nears, refs = (refs[7:25], refs[25:]) if keeps else (None, refs[7:])
    s = types.SimpleNamespace(**dict(zip(names, refs)))
    me, core = lax.axis_index("dp"), lax.axis_index("ffn")
    other = 1 - core
    held, width = table_far.shape
    entries = own_ref.shape[1]
    slots = entries // 2
    own = slots // 2
    half = entries // groups
    share = TILE // half
    tiles = entries // TILE
    spans = entries // GROUP
    pairs, hidden, places = s.keys.shape[0], s.w_up.shape[2], pos_far.shape[0]
    heads_width = pairs * TILE
    mine, yours = span(core * own, own), span(other * own, own)
    early, late = sums = [Part(s, name, groups, me, core) for name in ("early", "late")]

    barrier = pltpu.get_barrier_semaphore()
    slot_of = me * 2 + core

    def greet(k):
        where = (slot_of + k + 1) % (2 * groups)
        pl.semaphore_signal(
            barrier, inc=1, device_id=(where // 2, where % 2), device_id_type=MESH
        )

    over(2 * groups - 1, greet)
    spare = s.probs.at[0]
    s.d_cand_in = s.bias.at[pl.ds(0, slots * width // TILE)]
    s.column = s.probs.at[1, pl.ds(slots, slots), pl.ds(0, TILE)]
    s.segments = s.probs.at[1, pl.ds(slots, slots), pl.ds(TILE, TILE)]
    s.place = s.probs.at[1, pl.ds(2 * slots, slots), pl.ds(0, TILE)]
    s.total = s.d_normed = s.probs.at[1, pl.ds(0, slots)]
    s.grad_table = spare.at[pl.ds(0, held)]
    pieces = [table_far, out_far]
    pieces += [up_far.at[:, pl.ds(c * width, width)] for c in range(hidden // width)]
    pieces += [down_far, *(in_far.at[c] for c in range(3)), pos_far]
    loads, staged, at = [], [], 0
    if keeps:
        targets = [nears[0], nears[6]]
        targets += [nears[9].at[:, pl.ds(c * width, width)] for c in range(hidden // width)]
        targets += [nears[12], *(nears[3].at[c] for c in range(3)), nears[15]]
    for index, piece in enumerate(pieces):
        near = targets[index] if keeps else spare.at[pl.ds(at, piece.shape[0])]
        at += piece.shape[0]
        staged.append(near)
        loads.append(pltpu.make_async_copy(piece, near, s.loads.at[index]))
    for load in loads:
        load.start()

    def swap(index, source, target):
        send(source, target, s.sent.at[index], s.came.at[index], (me, other))

    def arrived(ref, semaphore):
        copy_to(ref, ref, semaphore, semaphore, (me, core)).wait_recv()

    def departed(ref, semaphore):
        copy_to(ref, ref, semaphore, semaphore, (me, core)).wait_send()

    def swapped(index, target):
        arrived(target, s.came.at[index])

    upper = one_hot(tile_iota((GROUP, GROUP), 0) <= tile_iota((GROUP, GROUP), 1))
    group_of = tile_iota((groups, GROUP), 0)
    before = jnp.zeros((groups, 1), WIDE)
    filled = jnp.zeros((3 * groups, TILE), WIDE)
    spot = (me % share) * half - core * half
    for chunk in range(spans):
        at = slice(chunk * GROUP, (chunk + 1) * GROUP)
        owner, offset = own_ref[:, at], off_ref[:, at]
        marks = jnp.where(group_of == owner, 1.0, 0.0)
        running = matmul(marks.astype(LOWF), upper) + before
        before = running[:, GROUP - 1 :]
        ranks = (jnp.sum(marks * running, 0, keepdims=True) - 1.0).astype(jnp.int32)
        slot = owner * half + ranks
        s.flat[:, at] = jnp.where(ranks < half, slot, slot + (entries - half))
        inside = (ranks >= core * half) & (ranks < core * half + half)
        picks = one_hot(tile_iota((TILE, GROUP), 0) == jnp.where(inside, ranks + spot, -1))
        parts = jnp.concatenate(
            [
                marks * lax.shift_right_logical(offset, 6).astype(WIDE),
                marks * (offset & 63).astype(WIDE),
                marks,
            ],
            0,
        ).astype(LOWF)
        filled = filled + matmul(parts, picks, NT)
    asking = (
        64.0 * filled[:groups] + filled[groups : 2 * groups] + filled[2 * groups :]
    ).astype(jnp.int32)
    for owner in range(groups):
        s.want[owner] = jnp.broadcast_to(asking[owner : owner + 1], (8, TILE))
    s.asked[me] = s.want[me]
    pl.semaphore_wait(barrier, 2 * groups - 1)

    def ask(k):
        owner = (me + groups // 2 + k) % groups

        @pl.when(owner != me)
        def _():
            send(
                s.want.at[owner], s.asked.at[me], s.want_sent.at[owner], s.want_came.at[me], (owner, core)
            )

    over(groups, ask)
    rows_mine, rows_yours = span(core * held, held), span(other * held, held)
    loads[0].wait()
    s.table[rows_mine, :] = staged[0][...].astype(LOWF)
    s.table[2 * held :, :] = jnp.zeros((s.table.shape[0] - 2 * held, width), LOWF)
    swap(0, s.table.at[rows_mine], s.table.at[rows_mine])
    eye = (tile_iota((TILE, TILE), 0) == tile_iota((TILE, TILE), 1)).astype(WIDE)
    ones = jnp.ones((TILE, TILE), LOWF)

    def column_of(line):
        return 64.0 * as_column(lax.shift_right_logical(line, 6).astype(WIDE), eye, ones) + as_column(
            (line & 63).astype(WIDE), eye, ones
        )

    for chunk in range(slots // TILE):
        side, at = divmod(chunk * TILE, own)
        line = s.flat[:, span(side * slots + core * own + at, TILE, TILE)]
        s.column[chunk * TILE : (chunk + 1) * TILE, :] = column_of(line)
    s.total[...] = jnp.zeros(s.total.shape, WIDE)
    swapped(0, s.table.at[rows_yours])
    lanes_wide = tile_iota((TILE, TILE), 1).astype(WIDE)

    bank = tiles // 2

    def seat(number):
        tile = number // share
        return tile // bank, tile % bank, span(number % share * half, half)

    def ship(tile, picked, buffer, sent, came):
        s.leaving[tile // bank, tile % bank] = picked
        for j in range(share):
            number = tile * share + j

            @pl.when(number != me)
            def _():
                block = s.leaving.at[seat(number)]
                send(block, buffer.at[(core, *seat(me))], sent.at[number], came.at[me], (number, core))

            @pl.when(number == me)
            def _():
                buffer[(core, *seat(me))] = picked[j * half : (j + 1) * half]

    def serve(tile):
        line = jnp.zeros((1, TILE), jnp.int32)
        for j in range(share):
            source = tile * share + j

            @pl.when(source != me)
            def _():
                arrived(s.asked.at[source], s.want_came.at[source])

        for j in range(share):
            line = line + s.asked[tile * share + j][0:1, :]
        s.reqs[core, pl.ds(tile, 1), :] = line
        number = column_of(line)
        hot = jnp.concatenate(
            [
                one_hot(number == lanes_wide + float(b * TILE + 1))
                for b in range(s.table.shape[0] // TILE)
            ],
            1,
        )
        picked = matmul(hot, s.table[...]).astype(LOWF)
        ship(tile, picked, s.arrived, s.row_sent, s.row_came)

    keep = []
    if keeps:
        for i in range(12):
            index = i // 2 * 3 + 1 + i % 2
            keep.append(pltpu.make_async_copy(fars[index], nears[index], s.loads.at[12 + i]))
    found, _ = windows(slots)
    live = live_ref[0]
    first_lanes = (tile_iota((1, TILE), 1) < HEAD).astype(WIDE)
    pick = [first_lanes.astype(LOWF), (1.0 - first_lanes).astype(LOWF)]
    gain = [gain_ref[g : g + 1, :] for g in range(3)]
    step = 2 * TILE


    def prepare():
        for load in loads[1:]:
            load.wait()
        for copy in keep:
            copy.start()
        s.w_out[core] = staged[1][...].astype(LOWF)
        ups = hidden // width
        for c in range(ups):
            s.w_up[core, :, c * width : (c + 1) * width] = staged[2 + c][...].astype(LOWF)
        s.w_down[core] = staged[2 + ups][...].astype(LOWF)
        for c in range(3):
            s.w_in[c] = staged[3 + ups + c][...].astype(LOWF)
        high = staged[-1][...].astype(LOWF)
        s.pos_high[...] = high
        s.pos_low[...] = (staged[-1][...] - high.astype(WIDE)).astype(LOWF)
        seg = seg_ref[...]
        level = tile_iota((LEVELS, slots), 0)
        starts = jnp.sum(jnp.where(seg < level, 1.0, 0.0), 1, keepdims=True)
        start = jnp.sum(jnp.where(seg == level, starts, 0.0), 0, keepdims=True)
        place_row = tile_iota((1, slots), 1) - start.astype(jnp.int32)
        s.place_row[...] = place_row
        seg_wide = seg.astype(WIDE)
        for b in range(slots // TILE):
            at = slice(b * TILE, (b + 1) * TILE)
            s.segments[at, :] = as_column(seg_wide[:, at], eye, ones)
            s.place[at, :] = column_of(place_row[:, at])
        causal = tile_iota((TILE, TILE), 0) <= tile_iota((TILE, TILE), 1)
        for b, low, wide, at in found:
            line = seg_wide[:, b * TILE : (b + 1) * TILE]
            for t in range(wide // TILE):
                same = s.segments[low + t * TILE : low + (t + 1) * TILE, :] == line
                if low + t * TILE == b * TILE:
                    same = same & causal
                s.bias[at + t * TILE : at + (t + 1) * TILE, :] = jnp.where(same, 0.0, LOWEST)
        alive_row = tile_iota((1, slots), 1) < live
        s.logit_bias[...] = jnp.where(alive_row, -logq_ref[...], LOWEST)
        for index, block in enumerate((s.w_out, s.w_up, s.w_down)):
            swap(2 + index, block.at[core], block.at[core])

    def spot_of(h):
        return flipped(me // share % bank, bank - 1 - h)

    def pair_of(buffer, side, spot):
        return jnp.concatenate([buffer[side, 0, spot], buffer[side, 1, spot]], 0)

    def lay(side, spot):
        lane = tile_iota((slots, TILE), 1).astype(WIDE)
        firsts = [(side * entries + (spot + b * bank) * TILE).astype(WIDE) for b in range(2)]
        hot = jnp.concatenate([one_hot(s.column[...] - first == lane) for first in firsts], 1)
        s.total[...] += matmul(hot, pair_of(s.arrived, side, spot))

    def trade(ahead, give, buffer, came, sent_on, passed, use, between):
        def other_two(h):
            spot = spot_of(h)
            arrived(buffer.at[other, :, spot], passed.at[spot])
            use(other, spot)

        def receive(h):
            spot = spot_of(h)
            for b in range(2):
                for j in range(share):
                    number = (spot + b * bank) * share + j

                    @pl.when(number != me)
                    def _():
                        arrived(buffer.at[(core, *seat(number))], came.at[number])

            block = buffer.at[core, :, spot]
            send(block, block, sent_on.at[spot], passed.at[spot], (me, other))
            use(core, spot)
            pl.when(h > 0)(lambda: other_two(h - 1))

        def step(h):
            @pl.when(h < bank)
            def _():
                spot = spot_of(h)
                far = 1 - me // share // bank
                give(spot + far * bank)
                give(spot + (1 - far) * bank)

            between(h)
            pl.when(h >= ahead)(lambda: receive(h - ahead))

        over(bank + ahead, step)
        other_two(jnp.int32(bank - 1))

    trade(3, serve, s.arrived, s.row_came, s.pass_sent, s.pass_came, lay, lambda h: pl.when(h == 2)(prepare))
    swap(1, s.reqs.at[core], s.reqs.at[core])
    s.cands[mine, :] = s.total[own:, :].astype(LOWF)
    swap(5, s.cands.at[mine], s.cands.at[mine])

    def enter(r):
        at = span(r * step, step)
        full = span(core * own + r * step, step, TILE)
        where = s.place[full, :]
        lane = tile_iota((step, TILE), 1).astype(WIDE)
        hot = jnp.concatenate(
            [one_hot(where == lane + float(t * TILE)) for t in range(places // TILE)], 1
        )
        first = s.total[at, :] + matmul(hot, s.pos_high[...]) + matmul(hot, s.pos_low[...])
        s.first[at, :] = first
        unit, inverse = spread_rows(first)
        s.unit_zero[at, :] = unit
        s.inverse_zero[at, :] = jnp.broadcast_to(inverse, (step, TILE))
        s.normed[full, :] = (unit * gain[0]).astype(LOWF)

    over(own // step, enter)
    swap(6, s.normed.at[mine], s.normed.at[mine])

    def project(k):
        @pl.when(k == own // step)
        def _():
            swapped(6, s.normed.at[yours])

        block = (core * (own // step) + k) % (slots // step)
        full = span(block * step, step, TILE)
        normed = s.normed[full, :]
        s.normed_t[:, full] = normed.astype(WIDE).T.astype(LOWF)
        query = (matmul(normed, s.w_in[0]) * SCALE).astype(LOWF)
        keys = matmul(normed, s.w_in[1]).astype(LOWF)
        values = matmul(normed, s.w_in[2]).astype(LOWF)
        keys_t = keys.astype(WIDE).T.astype(LOWF)
        values_t = values.astype(WIDE).T.astype(LOWF)
        for hp in range(pairs):
            lanes = slice(hp * TILE, (hp + 1) * TILE)
            s.keys[hp, full, :] = keys[:, lanes]
            s.values[hp, full, :] = values[:, lanes]
            s.keys_t[hp, :, full] = keys_t[lanes, :]
            s.values_t[hp, :, full] = values_t[lanes, :]
            for i in range(step // TILE):
                part = query[i * TILE : (i + 1) * TILE, lanes]
                for h in range(2):
                    s.queries[hp, block * (step // TILE) + i, h * TILE : (h + 1) * TILE, :] = (
                        part * pick[h]
                    )

    over(slots // step, project)

    def attend(hp):
        for b, low, wide, at in found:
            scores = matmul(s.keys[hp, low : low + wide, :], s.queries[hp, b], NT)
            bias = s.bias[at : at + wide, :]
            scores = scores + jnp.concatenate([bias, bias], 1)
            expo = jnp.exp(scores - jnp.max(scores, 0, keepdims=True))
            scale = 1.0 / jnp.sum(expo, 0, keepdims=True)
            s.scales[hp, b : b + 1, :] = scale
            s.probs[hp, at : at + wide, :] = expo
            out = matmul(s.values_t[hp, :, low : low + wide], expo.astype(LOWF)) * scale
            out = jnp.concatenate([out[:HEAD, :TILE], out[HEAD:, TILE:]], 0)
            s.mixed[hp, b * TILE : (b + 1) * TILE, :] = out.T.astype(LOWF)
        swap(7 + hp, s.mixed.at[hp, yours], s.mixed_in.at[hp])

    over(pairs, attend)
    for index, block in enumerate((s.w_out, s.w_up, s.w_down)):
        swapped(2 + index, block.at[other])
    over(bank, lambda spot: departed(s.arrived.at[core, :, spot], s.pass_sent.at[spot]))
    for hp in range(pairs):
        swapped(7 + hp, s.mixed_in.at[hp])

    def slopes(side, q, r):
        buffer = (s.d_keys, s.d_values)[side]
        fold = slots // own
        return buffer.at[q // fold, span(q % fold * own + r * step, step)]

    def feed(r):
        at = span(r * step, step)
        full = span(core * own + r * step, step, TILE)
        here = jnp.concatenate([s.mixed[hp, full, :] for hp in range(pairs)], 1)
        there = jnp.concatenate([s.mixed_in[hp, at, :] for hp in range(pairs)], 1)
        s.joined[core, at, :] = here
        s.joined[other, at, :] = there
        second = s.first[at, :] + matmul(here, s.w_out[core]) + matmul(there, s.w_out[other])
        unit, inverse = spread_rows(second)
        s.unit_one[at, :] = unit
        s.inverse_one[at, :] = jnp.broadcast_to(inverse, (step, TILE))
        lifted = (unit * gain[1]).astype(LOWF)
        s.lifted[at, :] = lifted
        third = second
        for side in range(2):
            inner = matmul(lifted, s.w_up[side])
            square = inner * inner
            bend = jnp.tanh(GELU_A * inner * (1.0 + GELU_B * square))
            gate = 0.5 * (1.0 + bend)
            act = (inner * gate).astype(LOWF)
            s.hidden[side, at, :] = act
            slope = gate + 0.5 * inner * (1.0 - bend * bend) * (
                GELU_A * (1.0 + 3.0 * GELU_B * square)
            )
            for q in range(hidden // TILE):
                slopes(side, q, r)[...] = slope[:, q * TILE : (q + 1) * TILE]
            third = third + matmul(act, s.w_down[side])
        unit, inverse = spread_rows(third)
        s.unit_two[at, :] = unit
        s.inverse_two[at, :] = jnp.broadcast_to(inverse, (step, TILE))
        s.final[at, :] = (unit * gain[2]).astype(LOWF)

    over(own // step, feed)
    s.few[...] = jnp.zeros((8, width), WIDE)
    swapped(5, s.cands.at[yours])

    def choose(r):
        at = span(r * TILE, TILE)
        here = span(core * own + r * TILE, TILE, TILE)
        final = s.final[at, :]
        logits = matmul(final, s.cands[...], NT) + s.logit_bias[...]
        square = matmul(final, s.cands[here, :], NT) + s.logit_bias[:, here]
        same = tile_iota((TILE, TILE), 0) == tile_iota((TILE, TILE), 1)
        number = tile_iota((TILE, 1), 0) + (core * own + r * TILE)
        top = jnp.max(logits, -1, keepdims=True)
        expo = jnp.exp(logits - top)
        total = jnp.sum(expo, -1, keepdims=True)
        alive = number < live
        right = jnp.sum(jnp.where(same, square, 0.0), -1, keepdims=True)
        loss = jnp.sum(jnp.where(alive, top + jnp.log(total) - right, 0.0))
        s.few[3:4, :] += jnp.full((1, width), loss, WIDE)
        alive = jnp.where(alive, 1.0, 0.0)
        scale = alive / total
        s.d_logits[at, :] = (expo * scale).astype(LOWF)
        square = jnp.exp(square - top) * scale - jnp.where(same, alive, 0.0)
        s.d_logits[at, here] = square.astype(LOWF)
        grad = s.d_logits[at, :]
        d_final = matmul(grad, s.cands[...])
        unit = s.unit_two[at, :]
        s.few[2:3, :] += jnp.sum(d_final * unit, 0, keepdims=True)
        d_third = spread_back(unit, s.inverse_two[at, :1], gain[2], d_final)
        s.d_third[at, :] = d_third
        s.d_branch[at, :] = d_third.astype(LOWF)

    for r in range(own // TILE):
        choose(jnp.int32(r))
    s.g_down_out[...] = matmul(s.hidden[other], s.d_branch[...], TN).astype(LOWF)
    swap(11, s.g_down_out, s.g_down_in)
    d_cand = matmul(s.d_logits[...], s.final[...], TN)
    for c in range(width // TILE):
        s.d_cand[c * slots : (c + 1) * slots, :] = d_cand[:, c * TILE : (c + 1) * TILE]
    swap(14, s.d_cand, s.d_cand_in)
    s.g_down[...] = matmul(s.hidden[core], s.d_branch[...], TN)

    def feed_back(r):
        at = span(r * step, step)
        full = span(core * own + r * step, step, TILE)
        d_lifted = jnp.zeros((step, width), WIDE)
        for side in range(2):
            d_hidden = matmul(s.d_branch[at, :], s.w_down[side], NT)
            slope = jnp.concatenate([slopes(side, q, r)[...] for q in range(hidden // TILE)], 1)
            d_inner = (d_hidden * slope).astype(LOWF)
            s.d_inner[side, at, :] = d_inner
            d_lifted = d_lifted + matmul(d_inner, s.w_up[side], NT)
        unit = s.unit_one[at, :]
        s.few[1:2, :] += jnp.sum(d_lifted * unit, 0, keepdims=True)
        d_second = s.d_third[at, :] + spread_back(unit, s.inverse_one[at, :1], gain[1], d_lifted)
        s.d_second[at, :] = d_second
        d_mixed = d_second.astype(LOWF)
        s.d_mixed[at, :] = d_mixed
        here = matmul(d_mixed, s.w_out[core], NT).astype(LOWF)
        there = matmul(d_mixed, s.w_out[other], NT).astype(LOWF)
        for hp in range(pairs):
            lanes = slice(hp * TILE, (hp + 1) * TILE)
            s.d_heads[hp, full, :] = here[:, lanes]
            s.d_heads_out[hp, at, :] = there[:, lanes]

    over(own // step, feed_back)
    for hp in range(pairs):
        swap(9 + hp, s.d_heads_out.at[hp], s.d_heads.at[hp, mine])
    s.g_up_out[...] = matmul(s.lifted[...], s.d_inner[other], TN).astype(LOWF)
    swap(12, s.g_up_out, s.g_up_in)
    s.g_out_out[...] = matmul(s.joined[other], s.d_mixed[...], TN).astype(LOWF)
    swap(13, s.g_out_out, s.g_out_in)
    s.g_up[...] = matmul(s.lifted[...], s.d_inner[core], TN)
    s.g_out[...] = matmul(s.joined[core], s.d_mixed[...], TN)
    s.d_keys[...] = jnp.zeros(s.d_keys.shape, WIDE)
    s.d_values[...] = jnp.zeros(s.d_values.shape, WIDE)

    def give_mid():
        swapped(11, s.g_down_in)
        swapped(12, s.g_up_in)
        swapped(13, s.g_out_in)
        g_up = s.g_up[...] + s.g_up_in[...].astype(WIDE)
        early.fill(
            (
                s.g_out[...] + s.g_out_in[...].astype(WIDE),
                *(g_up[:, c * width : (c + 1) * width] for c in range(hidden // width)),
                s.g_down[...] + s.g_down_in[...].astype(WIDE),
            )
        )

    give_mid()
    for hp in range(pairs):
        swapped(9 + hp, s.d_heads.at[hp, yours])

    def attend_back(hp):
        for b, low, wide, at in found:
            d_block = s.d_heads[hp, b * TILE : (b + 1) * TILE, :]
            d_pair = jnp.concatenate([d_block * pick[0], d_block * pick[1]], 0)
            d_prob = matmul(s.values[hp, low : low + wide, :], d_pair, NT)
            prob = s.probs[hp, at : at + wide, :] * s.scales[hp, b : b + 1, :]
            mean = jnp.sum(prob * d_prob, 0, keepdims=True)
            d_scores = (prob * (d_prob - mean)).astype(LOWF)
            s.d_keys[hp, low : low + wide, :] += matmul(d_scores, s.queries[hp, b])
            s.d_values[hp, low : low + wide, :] += matmul(prob.astype(LOWF), d_pair)
            out = matmul(s.keys_t[hp, :, low : low + wide], d_scores)
            out = jnp.concatenate([out[:HEAD, :TILE], out[HEAD:, TILE:]], 0) * SCALE
            lanes = span(hp * TILE, TILE, TILE)
            s.d_triple[0, b * TILE : (b + 1) * TILE, lanes] = out.T.astype(LOWF)


    over(pairs, attend_back)
    for hp in range(pairs):
        lanes = slice(hp * TILE, (hp + 1) * TILE)
        s.d_triple[1, :, lanes] = s.d_keys[hp].astype(LOWF)
        s.d_triple[2, :, lanes] = s.d_values[hp].astype(LOWF)
    for side in (yours, mine):
        d_normed = matmul(s.d_triple[0, side, :], s.w_in[0], NT)
        for c in range(1, 3):
            d_normed = d_normed + matmul(s.d_triple[c, side, :], s.w_in[c], NT)
        s.d_normed[side, :] = d_normed
        if side is yours:
            swap(15, s.d_normed.at[yours], s.d_normed_in)
    for c in range(3):
        g_in = matmul(s.normed_t[...], s.d_triple[c])
        late.source[c * width : (c + 1) * width, :] = g_in.astype(LOWF)
    early.across()
    swapped(15, s.d_normed_in)
    d_normed = s.d_normed[mine, :] + s.d_normed_in[...]
    unit = s.unit_zero[...]
    d_first = s.d_second[...] + spread_back(unit, s.inverse_zero[:, :1], gain[0], d_normed)
    s.d_rows[mine, :] = d_first.astype(LOWF)
    swap(16, s.d_rows.at[mine], s.d_rows.at[mine])
    s.few[0:1, :] = jnp.sum(d_normed * unit, 0, keepdims=True)
    s.few[4:5, :] = jnp.full((1, width), 0.5 * live.astype(WIDE), WIDE)
    swapped(14, s.d_cand_in)
    for c in range(width // TILE):
        at = pl.ds(c * slots, slots)
        s.d_rows[slots:, c * TILE : (c + 1) * TILE] = (s.d_cand[at, :] + s.d_cand_in[at, :]).astype(LOWF)
    over(
        groups - 1,
        lambda k: departed(
            s.leaving.at[seat((me + k + 1) % groups)], s.row_sent.at[(me + k + 1) % groups]
        ),
    )
    swapped(16, s.d_rows.at[yours])

    def give_rows(tile):
        number = s.flat[...] - (core * entries + tile * TILE)
        hot = one_hot(tile_iota((TILE, entries), 0) == number)
        picked = matmul(hot, s.d_rows[...]).astype(LOWF)
        ship(tile, picked, s.landed, s.land_sent, s.land_came)

    pos_half = places // 2

    def give_late():
        hot = one_hot(tile_iota((pos_half, slots), 0) + core * pos_half == s.place_row[...])
        late.fill((matmul(hot, s.d_rows[:slots, :]),), 3 * width)

    swapped(1, s.reqs.at[other])
    s.grad_table[...] = jnp.zeros(s.grad_table.shape, WIDE)

    def gather(side, spot):
        came = pair_of(s.landed, side, spot)
        first_row = core * held + 1
        lines = [s.reqs[side, pl.ds(spot + b * bank, 1), :] - first_row for b in range(2)]
        rows = tile_iota((held, TILE), 0)
        hot = jnp.concatenate([one_hot(rows == line) for line in lines], 1)
        s.grad_table[...] += matmul(hot, came)

    def between(h):
        first, last = range(late.rounds - 1), range(late.rounds - 1, late.rounds)
        back, end = range(late.rounds - 1, 0, -1), range(1)
        plan = {
            0: (give_late,),
            3: (lambda: early.settle(first),),
            4: (lambda: early.settle(last), late.across),
            5: (lambda: early.forward(back), lambda: late.settle(first)),
            6: (lambda: early.forward(end), lambda: late.settle(last)),
            7: (lambda: late.forward(back),),
            8: (lambda: late.forward(end),),
        }
        for at, acts in plan.items():
            for act in acts:
                pl.when(h == at)(act)

    trade(2, give_rows, s.landed, s.land_came, s.hand_sent, s.hand_came, gather, between)
    final = s.grad_table[...]
    table_ref[...] = final
    square = jnp.sum(final * final)
    for part in sums:
        square = square + jnp.sum(part.shard[...] * part.shard[...])
    s.few[5:6, :] = jnp.full((1, width), square, WIDE)
    swap(17, s.few, s.few_in)
    swapped(17, s.few_in)
    s.few_all[me] = s.few[...] + s.few_in[...]

    def few_copy(k):
        where = (me + k + 1) % groups
        block = s.few_all.at[me]
        return copy_to(block, block, s.few_sent.at[where], s.few_came.at[me], (where, core))

    over(groups - 1, lambda k: few_copy(k).start())
    late.collect()
    position_own = late.whole.at[pl.ds(3 * width, pos_half)]
    swap(18, position_own, s.other_half)
    early.collect()
    mid_ref[...] = early.whole[: mid_ref.shape[0], :]
    down_ref[...] = early.whole[mid_ref.shape[0] : mid_ref.shape[0] + hidden, :]
    inward_ref[...] = late.whole[: 3 * width, :]
    position_ref[span(core * pos_half, pos_half), :] = late.whole[3 * width : 3 * width + pos_half, :]
    swapped(18, s.other_half)
    position_ref[span(other * pos_half, pos_half), :] = s.other_half[...]

    for copy in keep:
        copy.wait()
    for part in sums:
        part.drain()

    def finish(k):
        where = (me + k + 1) % groups
        departed(s.want.at[where], s.want_sent.at[where])
        departed(s.leaving.at[seat(where)], s.land_sent.at[where])

    over(groups - 1, finish)

    over(bank, lambda spot: departed(s.landed.at[core, :, spot], s.hand_sent.at[spot]))
    ends = [s.table.at[rows_mine], s.reqs.at[core], s.w_out.at[core], s.w_up.at[core], s.w_down.at[core]]
    ends += [s.cands.at[mine], s.normed.at[mine]]
    ends += [s.mixed.at[hp, yours] for hp in range(2)] + [s.d_heads_out.at[hp] for hp in range(2)]
    ends += [s.g_down_out, s.g_up_out, s.g_out_out, s.d_cand, s.d_normed.at[yours]]
    ends += [s.d_rows.at[mine], s.few]
    for index, ref in enumerate(ends):
        departed(ref, s.sent.at[index])

    def take_few(k):
        where = (me + k + 1) % groups
        arrived(s.few_all.at[where], s.few_came.at[where])

    over(groups - 1, take_few)
    few_total = s.few_all[0]
    for source in range(1, groups):
        few_total = few_total + s.few_all[source]
    few_ref[...] = few_total
    gains = few_total[:3]
    stats_ref[...] = jnp.sqrt(few_total[5:6, :TILE] + jnp.sum(gains * gains)) + jnp.zeros((8, TILE), WIDE)
    over(groups - 1, lambda k: few_copy(k).wait_send())
    departed(position_own, s.sent.at[18])


def in_hbm(array):
    return pltpu.with_memory_space_constraint(array, pltpu.HBM)


def run_step(trios, owners, offsets, seg, live, logq, gains, groups, keeps):
    table, _, attn_out, ffn_up, _, position = (trio[0] for trio in trios)
    held, width = table.shape
    entries = owners.shape[1]
    heads_width, hidden, places = attn_out.shape[0], ffn_up.shape[1], position.shape[0]
    scratch = step_scratch(groups, held, entries, width, heads_width, hidden, places)
    shape = pltpu.VMEM
    arrays = [array for trio in trios for array in (trio if keeps else trio[:1])]
    kept = arrays if keeps else []
    return pl.pallas_call(
        functools.partial(step_kernel, groups, keeps, tuple(scratch)),
        out_shape=(
            shape((held, width), WIDE),
            shape((hidden, width), LOWF),
            shape((heads_width + hidden, width), LOWF),
            shape((3 * width, width), LOWF),
            shape((places, width), LOWF),
            shape((8, width), WIDE),
            shape((8, TILE), WIDE),
            *(shape(array.shape, WIDE) for array in kept),
        ),
        in_specs=[VMEM] * 3 + [SMEM] + [VMEM] * 2 + [FAR] * len(arrays),
        out_specs=(VMEM,) * (7 + len(kept)),
        scratch_shapes=list(scratch.values()),
        compiler_params=pltpu.CompilerParams(
            collective_id=0, has_side_effects=True, vmem_limit_bytes=(50 if keeps else 60) * 1024 * 1024
        ),
    )(owners, offsets, seg, live, logq, gains, *(in_hbm(array) for array in arrays))


def adamw(weight, grad, first, second, decay, rate):
    first = BETA_ONE * first + (1.0 - BETA_ONE) * grad
    second = BETA_TWO * second + (1.0 - BETA_TWO) * grad * grad
    below = jnp.sqrt(second) + ADAM_EPS * (1.0 - BETA_TWO**STEP) ** 0.5
    pace = rate * (1.0 - BETA_TWO**STEP) ** 0.5 / (1.0 - BETA_ONE**STEP)
    return ((1.0 - rate * decay) * weight - pace * (first / below), first, second)


def update_kernel(kept, table_g, down_g, mid_g, inward_g, position_g, few_ref, stats_ref, *refs):
    inputs, outputs, buffers, trio_gains = refs[:21], refs[21:45], refs[45:63], refs[63:66]
    came, left, gains_came = refs[66:69]
    names = ("table", "in", "out", "up", "down", "position")
    ins = []
    if not kept:
        ins = [pltpu.make_async_copy(inputs[i], buffers[i], came.at[i]) for i in range(18)]
    outs = [pltpu.make_async_copy(buffers[i], outputs[i], left.at[i]) for i in range(18)]
    gains_in = [pltpu.make_async_copy(inputs[18 + i], trio_gains[i], gains_came.at[i]) for i in range(3)]
    for copy in ins + gains_in:
        copy.start()
    norm = stats_ref[0, 0]
    factor = CLIP / jnp.maximum(norm, CLIP)
    outputs[21][0, 0] = few_ref[3, 0]
    outputs[22][0, 0] = few_ref[4, 0]
    outputs[23][0, 0] = norm
    width = table_g.shape[1]
    for index, name in enumerate(names):
        trio = buffers[3 * index : 3 * index + 3]
        sources = inputs[3 * index : 3 * index + 3] if kept else trio
        for copy in ins[3 * index : 3 * index + 3]:
            copy.wait()
        rate = RATE_POSITION if name == "position" else RATE
        block = {"table": 112, "up": 32}.get(name, 64)
        lead = trio[0].shape[0] if name == "in" else 1
        rows, columns = trio[0].shape[-2:]
        heads_width, hidden = buffers[6].shape[0], buffers[9].shape[1]

        def run(r, block=block, name=name, trio=trio, sources=sources, rows=rows, rate=rate):
            at = span(r * block, block)

            def view(ref):
                return ref.at[r * block // rows, span(r * block % rows, block)] if name == "in" else ref.at[at]

            values = [view(ref)[...] for ref in sources]
            if name == "table":
                grad = table_g[at, :]
            elif name == "in":
                grad = inward_g[at, :].astype(WIDE)
            elif name == "out":
                grad = mid_g[at, :].astype(WIDE)
            elif name == "up":
                grad = jnp.concatenate(
                    [
                        mid_g[span(heads_width + c * width + r * block, block), :].astype(WIDE)
                        for c in range(hidden // width)
                    ],
                    1,
                )
            elif name == "down":
                grad = down_g[at, :].astype(WIDE)
            else:
                grad = position_g[at, :].astype(WIDE)
            made = adamw(values[0], grad * factor, values[1], values[2], DECAY, rate)
            for ref, value in zip(trio, made):
                view(ref)[...] = value

        over(lead * rows // block, run)
        for i in range(3):
            outs[3 * index + i].start()
    for copy in gains_in:
        copy.wait()
    gains = adamw(
        trio_gains[0][...],
        few_ref[0:3, :] * factor,
        trio_gains[1][...],
        trio_gains[2][...],
        0.0,
        RATE_GAINS,
    )
    for ref, value in zip(outputs[18:21], gains):
        ref[...] = value
    for copy in outs:
        copy.wait()


def run_update(grads, trios, kept):
    flat = [*kept] if kept else [in_hbm(array) for trio in trios[:6] for array in trio]
    flat += [in_hbm(array) for array in trios[6]]
    shape = jax.ShapeDtypeStruct
    scalar = shape((1, 1), WIDE)
    return pl.pallas_call(
        functools.partial(update_kernel, bool(kept)),
        out_shape=tuple(shape(a.shape, WIDE) for a in flat) + (scalar,) * 3,
        in_specs=[VMEM] * 7 + [VMEM if kept else FAR] * 18 + [FAR] * 3,
        out_specs=(FAR,) * 18 + (VMEM,) * 3 + (SMEM,) * 3,
        scratch_shapes=[pltpu.VMEM(a.shape, WIDE) for a in flat] + [DMA((18,)), DMA((18,)), DMA((3,))],
        compiler_params=pltpu.CompilerParams(vmem_limit_bytes=(24 if kept else 48) * 1024 * 1024),
    )(*grads, *flat)


def body(
    item_table,
    attn_in,
    attn_out,
    ffn_up,
    ffn_down,
    position_table,
    norm_gains,
    item_first,
    item_second,
    attn_in_first,
    attn_in_second,
    attn_out_first,
    attn_out_second,
    ffn_up_first,
    ffn_up_second,
    ffn_down_first,
    ffn_down_second,
    position_first,
    position_second,
    gains_first,
    gains_second,
    owner_group,
    row_offset,
    segment_ids,
    live_slots,
    log_freq,
):
    trios = (
        (item_table, item_first, item_second),
        (attn_in, attn_in_first, attn_in_second),
        (attn_out, attn_out_first, attn_out_second),
        (ffn_up, ffn_up_first, ffn_up_second),
        (ffn_down, ffn_down_first, ffn_down_second),
        (position_table, position_first, position_second),
        (norm_gains, gains_first, gains_second),
    )
    groups = lax.axis_size("dp")
    made = run_step(
        trios[:6],
        owner_group.reshape(1, -1),
        row_offset,
        segment_ids,
        live_slots,
        log_freq,
        norm_gains,
        groups,
        groups <= 16,
    )
    made = run_update(made[:7], trios, made[7:])
    return (*made[:21], *(scalar.reshape(()) for scalar in made[21:]))


def solution(mesh):
    return jax.shard_map(
        body,
        mesh=mesh,
        in_specs=(
            P(("dp", "ffn"), None),
            P(None, None, "ffn"),
            P("ffn", None),
            P(None, "ffn"),
            P("ffn", None),
            P(),
            P(),
            P(("dp", "ffn"), None),
            P(("dp", "ffn"), None),
            P(None, None, "ffn"),
            P(None, None, "ffn"),
            P("ffn", None),
            P("ffn", None),
            P(None, "ffn"),
            P(None, "ffn"),
            P("ffn", None),
            P("ffn", None),
            P(),
            P(),
            P(),
            P(),
            P("dp", None, None),
            P("dp", None),
            P("dp", None),
            P("dp"),
            P("dp", None),
        ),
        out_specs=(
            P(("dp", "ffn"), None),
            P(("dp", "ffn"), None),
            P(("dp", "ffn"), None),
            P(None, None, "ffn"),
            P(None, None, "ffn"),
            P(None, None, "ffn"),
            P("ffn", None),
            P("ffn", None),
            P("ffn", None),
            P(None, "ffn"),
            P(None, "ffn"),
            P(None, "ffn"),
            P("ffn", None),
            P("ffn", None),
            P("ffn", None),
            P(),
            P(),
            P(),
            P(),
            P(),
            P(),
            P(),
            P(),
            P(),
        ),
        check_vma=False,
    )
```
